32 devices in a mesh: grp: 2 (over x), blk: 16 (over z, y, core).
Axes of the slice: x: 2, y: 2, z: 4, core: 2. Of those that a mesh axis runs over, the one named last changes fastest.
Arguments:
- queries: bfloat16 [32, 64, 128], P(('grp', 'blk')), may hold values from -120 to 120
- prefix_kv: bfloat16 [2, 2, 16384, 128], P(None, 'grp', 'blk'), may hold values from -6 to 6
- suffix_kv: bfloat16 [32, 256, 2, 4, 128], P(('grp', 'blk')), may hold values from -8 to 8
- new_kv: bfloat16 [32, 2, 4, 128], P(('grp', 'blk')), may hold values from -5 to 5
- suffix_len: int32 [32], P(('grp', 'blk')), may hold values from 1 to 256, as said below
Outputs:
- attended: bfloat16 [32, 64, 128], P(('grp', 'blk'))
The draws below stay inside these ranges and needn't reach their ends.
Inputs may be any that keep to these rules, and one draw needn't show every extreme that they name: `suffix_len`: some request has all 256 positions live in every draw.
All inputs are finite; a program needn't handle non-finite values.
Results may differ from the reference program's by a relative error of at most 0.0044.
Values may be sent and summed in bfloat16 or wider, within the bound.
No kernel may reach another device: no remote copies, remote signals or barrier semaphores. Data moves between devices by JAX's collectives and lax.ppermute only.
A program may use at most 64 MiB of HBM per device.

```python
import jax
import jax.numpy as jnp
from jax import lax

H = 64
KVH = 4
HD = 128
SL = 256
S_MAX = 256
REQ = 32
GSPAN = 4096
PREFIX = 8192
N_GRP = 2


def common_draw(key):
    fresh_key = jax.random.fold_in(key, 101)
    new_pair = jnp.clip(jax.random.normal(fresh_key, (REQ, 2, KVH, HD), jnp.float32), -5.0, 5.0)
    return new_pair


def draw_new_kv(key, part):
    new_pair = common_draw(key)
    return new_pair.astype(jnp.bfloat16)


def draw_queries(key, part):
    new_pair = common_draw(key)
    key = jax.random.fold_in(key, 3)
    expand = jnp.repeat(new_pair[:, 0], H // KVH, axis=1)
    result = 3.0 * jnp.clip(jax.random.normal(key, (REQ, H, HD), jnp.float32), -5.0, 5.0) + expand
    return result.astype(jnp.bfloat16)


def draw_suffix_kv(key, part):
    new_pair = common_draw(key)
    key = jax.random.fold_in(key, 5)
    base = jnp.clip(jax.random.normal(key, (REQ, S_MAX, 2, KVH, HD), jnp.float32), -5.0, 5.0)
    cache_keys = base[:, :, 0] + 0.5 * new_pair[:, None, 0]
    return jnp.stack([cache_keys, base[:, :, 1]], axis=2).astype(jnp.bfloat16)


def draw_suffix_len(key, part):
    key = jax.random.fold_in(key, 7)
    lengths = jax.random.randint(key, (REQ,), 1, S_MAX + 1)
    longest = jax.random.randint(jax.random.fold_in(key, 1), (), 0, REQ)
    return jnp.where(jnp.arange(REQ) == longest, S_MAX, lengths).astype(jnp.int32)


def steps_of(key, dims, cuts, least, top_value):
    factor_of, own = 1.0, jax.random.fold_in(key, 6)
    for axis_at, parts in cuts:
        draws = jnp.exp(jax.random.uniform(jax.random.fold_in(own, axis_at), (parts,), jnp.float32, least / len(cuts), top_value / len(cuts)))
        factor_of = factor_of * jnp.repeat(draws, dims[axis_at] // parts).reshape([-1 if axis == axis_at else 1 for axis in range(len(dims))])
    return factor_of


def gaussian(key, extent, width, most, split=(), kind=jnp.bfloat16):
    entries = width * jax.random.normal(key, extent, jnp.float32)
    if split:
        entries = entries * steps_of(key, extent, split, -0.22, 0.18)
    return jnp.clip(entries, -most, most).astype(kind)


def setup_inputs(seed: int = 0) -> dict:
    seeds = jax.random.split(jax.random.key(seed), 6)
    return {
        "queries": draw_queries(jax.random.fold_in(seeds[5], 71), 0),
        "prefix_kv": gaussian(seeds[1], (2, N_GRP, KVH * GSPAN, HD), 1.0, 6.0, ((1, 2), (2, 16))),
        "suffix_kv": draw_suffix_kv(jax.random.fold_in(seeds[5], 71), 0),
        "new_kv": draw_new_kv(jax.random.fold_in(seeds[5], 71), 0),
        "suffix_len": draw_suffix_len(jax.random.fold_in(seeds[5], 71), 0),
    }


def combine(first, second):
    best_score = jnp.maximum(first[2], second[2])
    early = jnp.exp(first[2] - best_score)
    later = jnp.exp(second[2] - best_score)
    numerator = first[0] * early[..., None] + second[0] * later[..., None]
    denominator = first[1] * early + second[1] * later
    return (numerator, denominator, best_score)


def block_partial(grouped, key_block_tiles, block_values):
    scores = jnp.einsum('rgpd,gkd->rgpk', grouped, key_block_tiles.astype(jnp.float32)) * (HD ** -0.5)
    best_score = jnp.max(scores, -1)
    softmax_weight = lax.optimization_barrier(jnp.exp(scores - best_score[..., None]).astype(jnp.bfloat16)).astype(jnp.float32)
    denominator = jnp.sum(softmax_weight, -1)
    numerator = jnp.einsum('rgpk,gkd->rgpd', softmax_weight, block_values.astype(jnp.float32))
    return (numerator, denominator, best_score)


def suffix_partial(grouped, suffix_kv, new_kv, suffix_len):
    reciprocal_scale = HD ** -0.5
    cache_keys = suffix_kv[:, :, 0].astype(jnp.float32)
    stored_value_rows = suffix_kv[:, :, 1].astype(jnp.float32)
    scores = jnp.einsum('rgpd,rsgd->rgps', grouped, cache_keys) * reciprocal_scale
    inside = jnp.arange(S_MAX, dtype=jnp.int32)[None, :] < suffix_len[:, None]
    scores = jnp.where(inside[:, None, None, :], scores, -jnp.inf)
    own_score = jnp.einsum('rgpd,rgd->rgp', grouped, new_kv[:, 0].astype(jnp.float32)) * reciprocal_scale
    best_score = jnp.maximum(jnp.max(scores, -1), own_score)
    softmax_weight = lax.optimization_barrier(jnp.exp(scores - best_score[..., None]).astype(jnp.bfloat16)).astype(jnp.float32)
    own_weight = lax.optimization_barrier(jnp.exp(own_score - best_score).astype(jnp.bfloat16)).astype(jnp.float32)
    denominator = jnp.sum(softmax_weight, -1) + own_weight
    numerator = jnp.einsum('rgps,rsgd->rgpd', softmax_weight, stored_value_rows)
    numerator = numerator + own_weight[..., None] * new_kv[:, 1].astype(jnp.float32)[:, :, None, :]
    return (numerator, denominator, best_score)


def reference(queries, prefix_kv, suffix_kv, new_kv, suffix_len):
    grouped = queries.astype(jnp.float32).reshape(REQ, KVH, H // KVH, HD)
    ordered = prefix_kv.reshape(2, N_GRP, KVH, GSPAN, HD)
    ordered = jnp.transpose(ordered, (0, 2, 1, 3, 4)).reshape(2, KVH, PREFIX, HD)
    running = suffix_partial(grouped, suffix_kv, new_kv, suffix_len)

    def absorb(running, block_index):
        offset = block_index * SL
        key_block_tiles = lax.dynamic_slice_in_dim(ordered[0], offset, SL, 1)
        block_values = lax.dynamic_slice_in_dim(ordered[1], offset, SL, 1)
        return combine(running, block_partial(grouped, key_block_tiles, block_values)), None

    running, unused = lax.scan(absorb, running, jnp.arange(PREFIX // SL, dtype=jnp.int32))
    numerator, denominator, best_score = running
    return (numerator / denominator[..., None]).reshape(REQ, H, HD).astype(jnp.bfloat16)
```

```python
import functools
import math

import jax
import jax.numpy as jnp
from jax import lax
from jax.experimental import pallas as pl
from jax.experimental.pallas import tpu as pltpu
from jax.sharding import PartitionSpec as P

H = 64
KVH = 4
HD = 128
SHARE = H // KVH
SCALE2 = HD ** (-0.5) * math.log2(math.e)
VMEM = pl.BlockSpec(memory_space=pltpu.VMEM)
ROWS = 128
NT = (((1,), (1,)), ((), ()))


def dot_nt(a, b):
    return lax.dot_general(a, b, NT, preferred_element_type=jnp.float32)


def dot(a, b):
    return jnp.dot(a, b, preferred_element_type=jnp.float32)


def log2(x):
    return jnp.log(x) * math.log2(math.e)


def split3(x):
    hi = x.astype(jnp.bfloat16).astype(jnp.float32)
    rest = x - hi
    mid = rest.astype(jnp.bfloat16).astype(jnp.float32)
    low = (rest - mid).astype(jnp.bfloat16).astype(jnp.float32)
    return hi, mid, low


def prefix_kernel(q_ref, kv_ref, out_ref):
    per_step = ROWS // SHARE
    requests = q_ref.shape[0]
    lane = lax.broadcasted_iota(jnp.int32, (ROWS, HD), 1)

    def step(at):
        keys = kv_ref[0]
        values = kv_ref[1]
        extended = jnp.concatenate([values, jnp.ones_like(values)], axis=1)
        rows = q_ref[pl.ds(at, per_step)].reshape(ROWS, HD)
        scores = dot_nt(rows, keys)
        best = jnp.max(scores, axis=1, keepdims=True)
        weight = jnp.exp2((scores - best) * SCALE2).astype(jnp.bfloat16)
        both = dot(weight, extended)
        total = both[:, HD:]
        result = both[:, :HD] / total
        hi, mid, low = split3(best * SCALE2 + log2(total))
        stats = jnp.where(lane == 0, hi, jnp.where(lane == 1, mid, jnp.where(lane == 2, low, 0.0)))
        out_ref[pl.ds(at, per_step), :SHARE] = result.astype(jnp.bfloat16).reshape(per_step, SHARE, HD)
        out_ref[pl.ds(at, per_step), SHARE:] = stats.astype(jnp.bfloat16).reshape(per_step, SHARE, HD)

    unrolled = 4 if requests % (4 * per_step) == 0 else 1

    def steps(index, unused):
        for inner in range(unrolled):
            step((index * unrolled + inner) * per_step)
        return unused

    trips = requests // (per_step * unrolled)
    if trips == 1:
        steps(0, 0)
    else:
        lax.fori_loop(0, trips, steps, 0)


def suffix_kernel(len_ref, q_ref, cache_ref, new_ref, out_ref, lse_ref):
    q = q_ref[0]
    rows = cache_ref.shape[1]
    live = len_ref[0]

    def masked(scores, limit):
        at = lax.broadcasted_iota(jnp.int32, scores.shape, 1)
        head = lax.broadcasted_iota(jnp.int32, scores.shape, 0) // SHARE
        own = (at % (2 * KVH) == head) & (at < limit * (2 * KVH))
        return jnp.where(own, scores, -jnp.inf)

    cache = cache_ref[0]
    new = new_ref[0]
    scores = masked(dot_nt(q, cache), live)
    new_scores = masked(dot_nt(q, new), 1)
    best = jnp.maximum(jnp.max(scores, axis=1, keepdims=True), jnp.max(new_scores, axis=1, keepdims=True))
    weight = jnp.exp2((scores - best) * SCALE2).astype(jnp.bfloat16).astype(jnp.float32)
    new_weight = jnp.exp2((new_scores - best) * SCALE2).astype(jnp.bfloat16).astype(jnp.float32)
    total = jnp.sum(weight, axis=1, keepdims=True) + jnp.sum(new_weight, axis=1, keepdims=True)
    moved = pltpu.roll(weight, KVH, 1).astype(jnp.bfloat16)
    new_moved = jnp.concatenate([new_weight[:, KVH:], new_weight[:, :KVH]], axis=1).astype(jnp.bfloat16)
    numerator = dot(moved, cache) + dot(new_moved, new)
    out_ref[...] = numerator / total
    lse_ref[...] = jnp.broadcast_to(best * SCALE2 + log2(total), lse_ref.shape)


def merge_kernel(groups, per_head, part_ref, suffix_ref, lse_ref, out_ref):
    sources = part_ref.shape[0]
    stats = part_ref[:, SHARE:].reshape(sources * SHARE, HD)
    part_lse = dot(stats, jnp.ones((HD, HD), jnp.bfloat16)).reshape(sources, SHARE, HD)
    for head in range(KVH):
        span = slice(head * SHARE, (head + 1) * SHARE)
        own = [(g * KVH + head) * per_head + i for g in range(groups) for i in range(per_head)]
        own_lse = lse_ref[span]
        best = own_lse
        for source in own:
            best = jnp.maximum(best, part_lse[source])
        total = jnp.exp2(own_lse - best)
        numerator = total * suffix_ref[span]
        for source in own:
            factor = jnp.exp2(part_lse[source] - best)
            total = total + factor
            numerator = numerator + factor * part_ref[source, :SHARE].astype(jnp.float32)
        out_ref[0, span] = (numerator / total).astype(jnp.bfloat16)


def local(queries, prefix_kv, suffix_kv, new_kv, suffix_len):
    groups = lax.axis_size("grp")
    members = lax.axis_size("blk")
    per_head = members // KVH
    devices = groups * members
    span = prefix_kv.shape[2]
    own = queries.reshape(1, KVH, 1, SHARE, HD)
    outgoing = jnp.broadcast_to(own, (groups, KVH, per_head, SHARE, HD)).reshape(devices, SHARE, HD)
    arrived = lax.all_to_all(outgoing, ("grp", "blk"), split_axis=0, concat_axis=0, tiled=True)

    suffix, suffix_lse = pl.pallas_call(
        suffix_kernel,
        out_shape=[jax.ShapeDtypeStruct((H, HD), jnp.float32)] * 2,
        in_specs=[pl.BlockSpec(memory_space=pltpu.SMEM), VMEM, VMEM, VMEM],
        out_specs=[VMEM, VMEM],
        name="suffix",
        cost_estimate=pl.CostEstimate(flops=70_000_000, bytes_accessed=600_000, transcendentals=140_000),
    )(suffix_len, queries, suffix_kv.reshape(1, -1, HD), new_kv.reshape(1, -1, HD))

    partial = pl.pallas_call(
        prefix_kernel,
        out_shape=jax.ShapeDtypeStruct((devices, 2 * SHARE, HD), jnp.bfloat16),
        in_specs=[VMEM, VMEM],
        out_specs=VMEM,
        name="prefix",
        compiler_params=pltpu.CompilerParams(vmem_limit_bytes=48 * 1024 * 1024),
        cost_estimate=pl.CostEstimate(
            flops=6 * devices * SHARE * span * HD, bytes_accessed=800_000, transcendentals=devices * SHARE * span
        ),
    )(arrived, prefix_kv.reshape(2, span, HD))

    returned = lax.all_to_all(partial, ("grp", "blk"), split_axis=0, concat_axis=0, tiled=True)
    return pl.pallas_call(
        functools.partial(merge_kernel, groups, per_head),
        out_shape=jax.ShapeDtypeStruct((1, H, HD), jnp.bfloat16),
        in_specs=[VMEM, VMEM, VMEM],
        out_specs=VMEM,
        name="merge",
        compiler_params=pltpu.CompilerParams(vmem_limit_bytes=48 * 1024 * 1024),
    )(returned, suffix, suffix_lse)


def solution(mesh):
    in_specs = (
        P(("grp", "blk"), None, None),
        P(None, "grp", "blk", None),
        P(("grp", "blk"), None, None, None, None),
        P(("grp", "blk"), None, None, None),
        P(("grp", "blk")),
    )
    out_specs = P(("grp", "blk"), None, None)
    return jax.shard_map(local, mesh=mesh, in_specs=in_specs, out_specs=out_specs, check_vma=False)
```

```python
import functools
import math

import jax
import jax.numpy as jnp
from jax import lax
from jax.experimental import pallas as pl
from jax.experimental.pallas import tpu as pltpu
from jax.sharding import PartitionSpec as P

H = 64
KVH = 4
HD = 128
SHARE = H // KVH
SCALE2 = HD ** (-0.5) * math.log2(math.e)
VMEM = pl.BlockSpec(memory_space=pltpu.VMEM)
ROWS = 128
CORES = 2
LIMIT = 24 * 1024 * 1024
NT = (((1,), (1,)), ((), ()))


def dot_nt(a, b):
    return lax.dot_general(a, b, NT, preferred_element_type=jnp.float32)


def dot(a, b):
    return jnp.dot(a, b, preferred_element_type=jnp.float32)


def log2(x):
    return jnp.log(x) * math.log2(math.e)


def split3(x):
    hi = x.astype(jnp.bfloat16).astype(jnp.float32)
    rest = x - hi
    mid = rest.astype(jnp.bfloat16).astype(jnp.float32)
    low = (rest - mid).astype(jnp.bfloat16).astype(jnp.float32)
    return hi, mid, low


def prefix_kernel(q_ref, kv_ref, other_ref, out_ref):
    per_step = ROWS // SHARE
    requests = q_ref.shape[0]
    lane = lax.broadcasted_iota(jnp.int32, (ROWS, HD), 1)

    def extended(ref):
        return jnp.concatenate([ref[1], jnp.ones_like(ref[1])], axis=1)

    def step(at):
        rows = q_ref[pl.ds(at, per_step)].reshape(ROWS, HD)
        scores = dot_nt(rows, kv_ref[0])
        other_scores = dot_nt(rows, other_ref[0])
        best = jnp.max(jnp.maximum(scores, other_scores), axis=1, keepdims=True)
        weight = jnp.exp2((scores - best) * SCALE2).astype(jnp.bfloat16)
        other_weight = jnp.exp2((other_scores - best) * SCALE2).astype(jnp.bfloat16)
        both = dot(weight, extended(kv_ref)) + dot(other_weight, extended(other_ref))
        total = both[:, HD:]
        result = both[:, :HD] / total
        hi, mid, low = split3(best * SCALE2 + log2(total))
        stats = jnp.where(lane == 0, hi, jnp.where(lane == 1, mid, jnp.where(lane == 2, low, 0.0)))
        out_ref[pl.ds(at, per_step), :SHARE] = result.astype(jnp.bfloat16).reshape(per_step, SHARE, HD)
        out_ref[pl.ds(at, per_step), SHARE:] = stats.astype(jnp.bfloat16).reshape(per_step, SHARE, HD)

    unrolled = 2 if requests % (2 * per_step) == 0 else 1

    def steps(index, unused):
        for inner in range(unrolled):
            step((index * unrolled + inner) * per_step)
        return unused

    trips = requests // (per_step * unrolled)
    if trips == 1:
        steps(0, 0)
    else:
        lax.fori_loop(0, trips, steps, 0)


def suffix_kernel(len_ref, q_ref, cache_ref, new_ref, out_ref, lse_ref):
    q = q_ref[0]
    rows = cache_ref.shape[1]
    live = len_ref[0]

    def masked(scores, limit):
        at = lax.broadcasted_iota(jnp.int32, scores.shape, 1)
        head = lax.broadcasted_iota(jnp.int32, scores.shape, 0) // SHARE
        own = (at % (2 * KVH) == head) & (at < limit * (2 * KVH))
        return jnp.where(own, scores, -jnp.inf)

    cache = cache_ref[0]
    new = new_ref[0]
    scores = masked(dot_nt(q, cache), live)
    new_scores = masked(dot_nt(q, new), 1)
    best = jnp.maximum(jnp.max(scores, axis=1, keepdims=True), jnp.max(new_scores, axis=1, keepdims=True))
    weight = jnp.exp2((scores - best) * SCALE2).astype(jnp.bfloat16).astype(jnp.float32)
    new_weight = jnp.exp2((new_scores - best) * SCALE2).astype(jnp.bfloat16).astype(jnp.float32)
    total = jnp.sum(weight, axis=1, keepdims=True) + jnp.sum(new_weight, axis=1, keepdims=True)
    moved = pltpu.roll(weight, KVH, 1).astype(jnp.bfloat16)
    new_moved = jnp.concatenate([new_weight[:, KVH:], new_weight[:, :KVH]], axis=1).astype(jnp.bfloat16)
    numerator = dot(moved, cache) + dot(new_moved, new)
    out_ref[...] = numerator / total
    lse_ref[...] = jnp.broadcast_to(best * SCALE2 + log2(total), lse_ref.shape)


def merge_kernel(groups, per_head, part_ref, suffix_ref, lse_ref, out_ref):
    sources = part_ref.shape[0]
    stats = part_ref[:, SHARE:].reshape(sources * SHARE, HD)
    part_lse = dot(stats, jnp.ones((HD, HD), jnp.bfloat16)).reshape(sources, SHARE, HD)
    for head in range(KVH):
        span = slice(head * SHARE, (head + 1) * SHARE)
        own = [(g * KVH + head) * per_head + i for g in range(groups) for i in range(per_head)]
        own_lse = lse_ref[span]
        best = own_lse
        for source in own:
            best = jnp.maximum(best, part_lse[source])
        total = jnp.exp2(own_lse - best)
        numerator = total * suffix_ref[span]
        for source in own:
            factor = jnp.exp2(part_lse[source] - best)
            total = total + factor
            numerator = numerator + factor * part_ref[source, :SHARE].astype(jnp.float32)
        out_ref[0, span] = (numerator / total).astype(jnp.bfloat16)


def local(queries, prefix_kv, suffix_kv, new_kv, suffix_len):
    groups = lax.axis_size("grp")
    members = lax.axis_size("blk")
    pairs = members // CORES
    per_head = pairs // KVH
    partners = groups * pairs
    span = prefix_kv.shape[2]
    everyone = ("grp", "blk")
    lanes = [[chip * CORES + core for chip in range(partners)] for core in range(CORES)]

    other = lax.ppermute(prefix_kv, "blk", [(i, i ^ 1) for i in range(members)])
    own = queries.reshape(1, KVH, 1, SHARE, HD)
    outgoing = jnp.broadcast_to(own, (groups, KVH, per_head, SHARE, HD)).reshape(partners, SHARE, HD)
    exchange = functools.partial(
        lax.all_to_all, axis_name=everyone, split_axis=0, concat_axis=0, axis_index_groups=lanes, tiled=True
    )
    arrived = exchange(outgoing)

    suffix, suffix_lse = pl.pallas_call(
        suffix_kernel,
        out_shape=[jax.ShapeDtypeStruct((H, HD), jnp.float32)] * 2,
        in_specs=[pl.BlockSpec(memory_space=pltpu.SMEM), VMEM, VMEM, VMEM],
        out_specs=[VMEM, VMEM],
        name="suffix",
        compiler_params=pltpu.CompilerParams(vmem_limit_bytes=LIMIT),
        cost_estimate=pl.CostEstimate(flops=70_000_000, bytes_accessed=600_000, transcendentals=140_000),
    )(suffix_len, queries, suffix_kv.reshape(1, -1, HD), new_kv.reshape(1, -1, HD))

    partial = pl.pallas_call(
        prefix_kernel,
        out_shape=jax.ShapeDtypeStruct((partners, 2 * SHARE, HD), jnp.bfloat16),
        in_specs=[VMEM, VMEM, VMEM],
        out_specs=VMEM,
        name="prefix",
        compiler_params=pltpu.CompilerParams(vmem_limit_bytes=LIMIT),
        cost_estimate=pl.CostEstimate(
            flops=12 * partners * SHARE * span * HD,
            bytes_accessed=1_600_000,
            transcendentals=2 * partners * SHARE * span,
        ),
    )(arrived, prefix_kv.reshape(2, span, HD), other.reshape(2, span, HD))

    returned = exchange(partial)
    return pl.pallas_call(
        functools.partial(merge_kernel, groups, per_head),
        out_shape=jax.ShapeDtypeStruct((1, H, HD), jnp.bfloat16),
        in_specs=[VMEM, VMEM, VMEM],
        out_specs=VMEM,
        name="merge",
        compiler_params=pltpu.CompilerParams(vmem_limit_bytes=LIMIT),
    )(returned, suffix, suffix_lse)


def solution(mesh):
    in_specs = (
        P(("grp", "blk"), None, None),
        P(None, "grp", "blk", None),
        P(("grp", "blk"), None, None, None, None),
        P(("grp", "blk"), None, None, None),
        P(("grp", "blk")),
    )
    out_specs = P(("grp", "blk"), None, None)
    return jax.shard_map(local, mesh=mesh, in_specs=in_specs, out_specs=out_specs, check_vma=False)
```

```python
import functools
import math

import jax
import jax.numpy as jnp
from jax import lax
from jax.experimental import pallas as pl
from jax.experimental.pallas import tpu as pltpu
from jax.sharding import PartitionSpec as P

H = 64
KVH = 4
HD = 128
SHARE = H // KVH
SCALE2 = HD ** (-0.5) * math.log2(math.e)
VMEM = pl.BlockSpec(memory_space=pltpu.VMEM)
ROWS = 128
CORES = 2
HALF = SHARE // CORES
LIMIT = 24 * 1024 * 1024
NT = (((1,), (1,)), ((), ()))


def dot_nt(a, b):
    return lax.dot_general(a, b, NT, preferred_element_type=jnp.float32)


def dot(a, b):
    return jnp.dot(a, b, preferred_element_type=jnp.float32)


def log2(x):
    return jnp.log(x) * math.log2(math.e)


def split3(x):
    hi = x.astype(jnp.bfloat16).astype(jnp.float32)
    rest = x - hi
    mid = rest.astype(jnp.bfloat16).astype(jnp.float32)
    low = (rest - mid).astype(jnp.bfloat16).astype(jnp.float32)
    return hi, mid, low


def prefix_kernel(q_ref, kv_ref, other_ref, out_ref):
    per_step = ROWS // HALF
    lane = lax.broadcasted_iota(jnp.int32, (ROWS, HD), 1)

    def extended(ref):
        return jnp.concatenate([ref[1], jnp.ones_like(ref[1])], axis=1)

    def step(at):
        rows = q_ref[pl.ds(at * HALF, ROWS)]
        scores = dot_nt(rows, kv_ref[0])
        other_scores = dot_nt(rows, other_ref[0])
        best = jnp.max(jnp.maximum(scores, other_scores), axis=1, keepdims=True)
        weight = jnp.exp2((scores - best) * SCALE2).astype(jnp.bfloat16)
        other_weight = jnp.exp2((other_scores - best) * SCALE2).astype(jnp.bfloat16)
        both = dot(weight, extended(kv_ref)) + dot(other_weight, extended(other_ref))
        total = both[:, HD:]
        result = both[:, :HD] / total
        hi, mid, low = split3(best * SCALE2 + log2(total))
        stats = jnp.where(lane == 0, hi, jnp.where(lane == 1, mid, jnp.where(lane == 2, low, 0.0)))
        shape = (per_step, HALF, HD)
        message = jnp.concatenate([result.reshape(shape), stats.reshape(shape)], axis=1)
        out_ref[pl.ds(at * 2 * HALF, 2 * ROWS)] = message.reshape(2 * ROWS, HD).astype(jnp.bfloat16)

    trips = q_ref.shape[0] // ROWS
    if trips <= 4:
        for trip in range(trips):
            step(trip * per_step)
    else:

        def body(trip, unused):
            step(pl.multiple_of(trip * per_step, per_step))
            return unused

        lax.fori_loop(0, trips, body, 0)


def owned(shape, limit):
    at = lax.broadcasted_iota(jnp.int32, shape, 1)
    head = lax.broadcasted_iota(jnp.int32, shape, 0) // SHARE
    return (at % (2 * KVH) == head) & (at < limit * (2 * KVH))


def suffix_kernel(len_ref, q_ref, cache_ref, new_ref, out_ref, best_ref, total_ref):
    q = q_ref[0]
    cache = cache_ref[0]
    raw = dot_nt(q, cache)
    scores = jnp.where(owned(raw.shape, len_ref[0]), raw, -jnp.inf)
    new_raw = dot_nt(q, new_ref[0])
    new_scores = jnp.where(owned(new_raw.shape, 1), new_raw, -jnp.inf)
    best = jnp.maximum(jnp.max(scores, axis=1, keepdims=True), jnp.max(new_scores, axis=1, keepdims=True))
    weight = jnp.exp2((scores - best) * SCALE2).astype(jnp.bfloat16).astype(jnp.float32)
    moved = pltpu.roll(weight, KVH, 1).astype(jnp.bfloat16)
    out_ref[...] = dot(moved, cache)
    best_ref[...] = jnp.broadcast_to(best, best_ref.shape)
    total_ref[...] = jnp.broadcast_to(jnp.sum(weight, axis=1, keepdims=True), total_ref.shape)


def fresh_kernel(q_ref, new_ref, num_ref, best_ref, total_ref, out_ref, lse_ref):
    new = new_ref[0]
    raw = dot_nt(q_ref[0], new)
    best = best_ref[...]
    scores = jnp.where(owned(raw.shape, 1), raw, -jnp.inf)
    weight = jnp.exp2((scores - best[:, : raw.shape[1]]) * SCALE2).astype(jnp.bfloat16).astype(jnp.float32)
    moved = jnp.concatenate([weight[:, KVH:], weight[:, :KVH]], axis=1).astype(jnp.bfloat16)
    total = total_ref[...] + jnp.sum(weight, axis=1, keepdims=True)
    out_ref[...] = (num_ref[...] + dot(moved, new)) / total
    lse_ref[...] = best * SCALE2 + log2(total)


def fan_kernel(served, q_ref, out_ref):
    q = q_ref[0].astype(jnp.float32)
    out_ref[...] = jnp.concatenate([q[its * HALF : (its + 1) * HALF] for its in served], axis=0).astype(jnp.bfloat16)


def merge_kernel(served, part_ref, suffix_ref, lse_ref, out_ref):
    sums = dot(part_ref[...], jnp.ones((HD, HD), jnp.bfloat16)).reshape(len(served), 2 * HALF, HD)
    rows = part_ref[...].astype(jnp.float32).reshape(len(served), 2 * HALF, HD)
    blocks = []
    for block in range(H // HALF):
        span = slice(block * HALF, (block + 1) * HALF)
        own = [slot for slot, its in enumerate(served) if its == block]
        own_lse = lse_ref[span]
        best = own_lse
        for slot in own:
            best = jnp.maximum(best, sums[slot, HALF:])
        total = jnp.exp2(own_lse - best)
        numerator = total * suffix_ref[span]
        for slot in own:
            factor = jnp.exp2(sums[slot, HALF:] - best)
            total = total + factor
            numerator = numerator + factor * rows[slot, :HALF]
        blocks.append(numerator / total)
    out_ref[0] = jnp.concatenate(blocks, axis=0).astype(jnp.bfloat16)


def call(kernel, name, outs, operands, specs=None, **cost):
    return pl.pallas_call(
        kernel,
        out_shape=outs,
        in_specs=specs or [VMEM] * len(operands),
        out_specs=jax.tree.map(lambda _: VMEM, outs),
        name=name,
        compiler_params=pltpu.CompilerParams(vmem_limit_bytes=LIMIT),
        cost_estimate=pl.CostEstimate(**cost) if cost else None,
    )(*operands)


def local(queries, prefix_kv, suffix_kv, new_kv, suffix_len):
    groups = lax.axis_size("grp")
    members = lax.axis_size("blk")
    per_head = members // KVH
    devices = groups * members
    span = prefix_kv.shape[2]
    order = list(reversed(range(devices)))
    served = [device % members // per_head * CORES + device % CORES for device in order]

    def one(rows, dtype=jnp.float32):
        return jax.ShapeDtypeStruct((rows, HD), dtype)

    def exchange(array):
        return lax.all_to_all(array, ("grp", "blk"), 0, 0, axis_index_groups=[order], tiled=True)

    other = lax.ppermute(prefix_kv, "blk", [(i, i ^ 1) for i in range(members)])
    outgoing = call(functools.partial(fan_kernel, served), "fan", one(devices * HALF, jnp.bfloat16), (queries,))
    arrived = exchange(outgoing.reshape(devices, HALF, HD)).reshape(devices * HALF, HD)

    new = new_kv.reshape(1, -1, HD)
    suffix = call(
        suffix_kernel,
        "suffix",
        [one(H)] * 3,
        (suffix_len, queries, suffix_kv.reshape(1, -1, HD), new),
        [pl.BlockSpec(memory_space=pltpu.SMEM), VMEM, VMEM, VMEM],
        flops=70_000_000,
        bytes_accessed=600_000,
        transcendentals=140_000,
    )
    arrived, suffix = lax.optimization_barrier((arrived, suffix))
    partial = call(
        prefix_kernel,
        "prefix",
        one(devices * 2 * HALF, jnp.bfloat16),
        (arrived, prefix_kv.reshape(2, span, HD), other.reshape(2, span, HD)),
        flops=12 * devices * HALF * span * HD,
        bytes_accessed=1_600_000,
        transcendentals=2 * devices * HALF * span,
    )
    partial, suffix = lax.optimization_barrier((partial, suffix))
    returned = exchange(partial.reshape(devices, 2 * HALF, HD)).reshape(-1, HD)
    fresh = call(fresh_kernel, "fresh", [one(H)] * 2, (queries, new, *suffix), flops=1_000_000, bytes_accessed=200_000, transcendentals=10_000)
    return call(
        functools.partial(merge_kernel, served),
        "merge",
        jax.ShapeDtypeStruct((1, H, HD), jnp.bfloat16),
        (returned, *fresh),
    )


def solution(mesh):
    in_specs = (
        P(("grp", "blk"), None, None),
        P(None, "grp", "blk", None),
        P(("grp", "blk"), None, None, None, None),
        P(("grp", "blk"), None, None, None),
        P(("grp", "blk")),
    )
    out_specs = P(("grp", "blk"), None, None)
    return jax.shard_map(local, mesh=mesh, in_specs=in_specs, out_specs=out_specs, check_vma=False)
```

```python
import functools
import math

import jax
import jax.numpy as jnp
from jax import lax
from jax.experimental import pallas as pl
from jax.experimental.pallas import tpu as pltpu
from jax.sharding import PartitionSpec as P

H = 64
KVH = 4
HD = 128
SHARE = H // KVH
SCALE2 = HD ** (-0.5) * math.log2(math.e)
VMEM = pl.BlockSpec(memory_space=pltpu.VMEM)
ROWS = 128
CORES = 2
HALF = SHARE // CORES
LIMIT = 24 * 1024 * 1024
NT = (((1,), (1,)), ((), ()))


def dot_nt(a, b):
    return lax.dot_general(a, b, NT, preferred_element_type=jnp.float32)


def dot(a, b):
    return jnp.dot(a, b, preferred_element_type=jnp.float32)


def log2(x):
    return jnp.log(x) * math.log2(math.e)


def split3(x):
    hi = x.astype(jnp.bfloat16).astype(jnp.float32)
    rest = x - hi
    mid = rest.astype(jnp.bfloat16).astype(jnp.float32)
    low = (rest - mid).astype(jnp.bfloat16).astype(jnp.float32)
    return hi, mid, low


def prefix_kernel(q_ref, kv_ref, other_ref, out_ref):
    per_step = ROWS // HALF
    lane = lax.broadcasted_iota(jnp.int32, (ROWS, HD), 1)

    def extended(ref):
        return jnp.concatenate([ref[1], jnp.ones_like(ref[1])], axis=1)

    def step(at):
        rows = q_ref[pl.ds(at * HALF, ROWS)]
        scores = dot_nt(rows, kv_ref[0])
        other_scores = dot_nt(rows, other_ref[0])
        best = jnp.max(jnp.maximum(scores, other_scores), axis=1, keepdims=True)
        weight = jnp.exp2((scores - best) * SCALE2).astype(jnp.bfloat16)
        other_weight = jnp.exp2((other_scores - best) * SCALE2).astype(jnp.bfloat16)
        both = dot(weight, extended(kv_ref)) + dot(other_weight, extended(other_ref))
        total = both[:, HD:]
        result = both[:, :HD] / total
        hi, mid, low = split3(best * SCALE2 + log2(total))
        stats = jnp.where(lane == 0, hi, jnp.where(lane == 1, mid, jnp.where(lane == 2, low, 0.0)))
        shape = (per_step, HALF, HD)
        message = jnp.concatenate([result.reshape(shape), stats.reshape(shape)], axis=1)
        out_ref[pl.ds(at * 2 * HALF, 2 * ROWS)] = message.reshape(2 * ROWS, HD).astype(jnp.bfloat16)

    trips = q_ref.shape[0] // ROWS
    if trips <= 4:
        for trip in range(trips):
            step(trip * per_step)
    else:

        def body(trip, unused):
            step(pl.multiple_of(trip * per_step, per_step))
            return unused

        lax.fori_loop(0, trips, body, 0)


def owned(shape, limit):
    at = lax.broadcasted_iota(jnp.int32, shape, 1)
    head = lax.broadcasted_iota(jnp.int32, shape, 0) // SHARE
    return (at % (2 * KVH) == head) & (at < limit * (2 * KVH))


def suffix_kernel(len_ref, q_ref, cache_ref, new_ref, out_ref, lse_ref):
    q = q_ref[0]
    cache = cache_ref[0]
    new = new_ref[0]
    raw = dot_nt(q, cache)
    scores = jnp.where(owned(raw.shape, len_ref[0]), raw, -jnp.inf)
    new_raw = dot_nt(q, new)
    new_scores = jnp.where(owned(new_raw.shape, 1), new_raw, -jnp.inf)
    best = jnp.maximum(jnp.max(scores, axis=1, keepdims=True), jnp.max(new_scores, axis=1, keepdims=True))
    weight = jnp.exp2((scores - best) * SCALE2).astype(jnp.bfloat16).astype(jnp.float32)
    new_weight = jnp.exp2((new_scores - best) * SCALE2).astype(jnp.bfloat16).astype(jnp.float32)
    total = jnp.sum(weight, axis=1, keepdims=True) + jnp.sum(new_weight, axis=1, keepdims=True)
    moved = pltpu.roll(weight, KVH, 1).astype(jnp.bfloat16)
    new_moved = jnp.concatenate([new_weight[:, KVH:], new_weight[:, :KVH]], axis=1).astype(jnp.bfloat16)
    out_ref[...] = (dot(moved, cache) + dot(new_moved, new)) / total
    lse_ref[...] = jnp.broadcast_to(best * SCALE2 + log2(total), lse_ref.shape)


def fan_kernel(q_ref, out_ref, sems):
    copies = [
        pltpu.make_async_copy(q_ref, out_ref.at[group, :, chip], sems.at[group, chip])
        for group in range(out_ref.shape[0])
        for chip in range(out_ref.shape[2])
    ]
    for copy in copies:
        copy.start()
    for copy in copies:
        copy.wait()


def merge_kernel(served, part_ref, suffix_ref, lse_ref, out_ref):
    sums = dot(part_ref[...], jnp.ones((HD, HD), jnp.bfloat16)).reshape(len(served), 2 * HALF, HD)
    rows = part_ref[...].astype(jnp.float32).reshape(len(served), 2 * HALF, HD)
    blocks = []
    for block in range(H // HALF):
        span = slice(block * HALF, (block + 1) * HALF)
        own = [slot for slot, its in enumerate(served) if its == block]
        own_lse = lse_ref[span]
        best = own_lse
        for slot in own:
            best = jnp.maximum(best, sums[slot, HALF:])
        total = jnp.exp2(own_lse - best)
        numerator = total * suffix_ref[span]
        for slot in own:
            factor = jnp.exp2(sums[slot, HALF:] - best)
            total = total + factor
            numerator = numerator + factor * rows[slot, :HALF]
        blocks.append(numerator / total)
    out_ref[0] = jnp.concatenate(blocks, axis=0).astype(jnp.bfloat16)


def call(kernel, name, outs, operands, specs=None, **cost):
    return pl.pallas_call(
        kernel,
        out_shape=outs,
        in_specs=specs or [VMEM] * len(operands),
        out_specs=jax.tree.map(lambda _: VMEM, outs),
        name=name,
        compiler_params=pltpu.CompilerParams(vmem_limit_bytes=LIMIT),
        cost_estimate=pl.CostEstimate(**cost) if cost else None,
    )(*operands)


def local(queries, prefix_kv, suffix_kv, new_kv, suffix_len):
    groups = lax.axis_size("grp")
    members = lax.axis_size("blk")
    per_head = members // KVH
    devices = groups * members
    span = prefix_kv.shape[2]
    chips = per_head // CORES
    served = [device % members // per_head * CORES + device % CORES for device in range(devices)]

    def one(rows, dtype=jnp.float32):
        return jax.ShapeDtypeStruct((rows, HD), dtype)

    def exchange(array):
        return lax.all_to_all(array, ("grp", "blk"), 0, 0, tiled=True)

    other = lax.ppermute(prefix_kv, "blk", [(i, i ^ 1) for i in range(members)])
    outgoing = pl.pallas_call(
        fan_kernel,
        out_shape=jax.ShapeDtypeStruct((groups, KVH, chips, SHARE, HD), jnp.bfloat16),
        in_specs=[pl.BlockSpec(memory_space=pl.ANY)],
        out_specs=pl.BlockSpec(memory_space=pl.ANY),
        scratch_shapes=[pltpu.SemaphoreType.DMA((groups, chips))],
        name="fan",
    )(queries.reshape(KVH, SHARE, HD))
    arrived = exchange(outgoing.reshape(devices, HALF, HD)).reshape(devices * HALF, HD)

    new = new_kv.reshape(1, -1, HD)
    suffix = call(
        suffix_kernel,
        "suffix",
        [one(H)] * 2,
        (suffix_len, queries, suffix_kv.reshape(1, -1, HD), new),
        [pl.BlockSpec(memory_space=pltpu.SMEM), VMEM, VMEM, VMEM],
        flops=70_000_000,
        bytes_accessed=600_000,
        transcendentals=140_000,
    )
    arrived, suffix = lax.optimization_barrier((arrived, suffix))
    partial = call(
        prefix_kernel,
        "prefix",
        one(devices * 2 * HALF, jnp.bfloat16),
        (arrived, prefix_kv.reshape(2, span, HD), other.reshape(2, span, HD)),
        flops=12 * devices * HALF * span * HD,
        bytes_accessed=1_600_000,
        transcendentals=2 * devices * HALF * span,
    )
    returned = exchange(partial.reshape(devices, 2 * HALF, HD)).reshape(-1, HD)
    return call(
        functools.partial(merge_kernel, served),
        "merge",
        jax.ShapeDtypeStruct((1, H, HD), jnp.bfloat16),
        (returned, *suffix),
    )


def solution(mesh):
    in_specs = (
        P(("grp", "blk"), None, None),
        P(None, "grp", "blk", None),
        P(("grp", "blk"), None, None, None, None),
        P(("grp", "blk"), None, None, None),
        P(("grp", "blk")),
    )
    out_specs = P(("grp", "blk"), None, None)
    return jax.shard_map(local, mesh=mesh, in_specs=in_specs, out_specs=out_specs, check_vma=False)
```

```python
import functools
import math

import jax
import jax.numpy as jnp
from jax import lax
from jax.experimental import pallas as pl
from jax.experimental.pallas import tpu as pltpu
from jax.sharding import PartitionSpec as P

H = 64
KVH = 4
HD = 128
SHARE = H // KVH
SCALE2 = HD ** (-0.5) * math.log2(math.e)
VMEM = pl.BlockSpec(memory_space=pltpu.VMEM)
HBM = pl.BlockSpec(memory_space=pltpu.HBM)
ROWS = 128
CORES = 2
HALF = SHARE // CORES
LIMIT = 24 * 1024 * 1024
NT = (((1,), (1,)), ((), ()))


def dot_nt(a, b):
    return lax.dot_general(a, b, NT, preferred_element_type=jnp.float32)


def dot(a, b):
    return jnp.dot(a, b, preferred_element_type=jnp.float32)


def log2(x):
    return jnp.log(x) * math.log2(math.e)


def split3(x):
    hi = x.astype(jnp.bfloat16).astype(jnp.float32)
    rest = x - hi
    mid = rest.astype(jnp.bfloat16).astype(jnp.float32)
    low = (rest - mid).astype(jnp.bfloat16).astype(jnp.float32)
    return hi, mid, low


def load_kernel(q_ref, kv_ref, cache_ref, new_ref, len_ref, fan_ref, q_out, kv_out, cache_out, new_out, live_ref, len_vmem, sems):
    pairs = [(q_ref, q_out), (len_ref, len_vmem), (new_ref, new_out), (kv_ref, kv_out), (cache_ref, cache_out)]
    copies = [pltpu.make_async_copy(source, target, sems.at[i]) for i, (source, target) in enumerate(pairs)]
    for copy in copies:
        copy.start()
    copies[0].wait()
    q = q_out[...].reshape(KVH, SHARE, HD)
    for group in range(fan_ref.shape[0]):
        for chip in range(fan_ref.shape[2]):
            fan_ref[group, :, chip] = q
    for copy in copies[1:]:
        copy.wait()
    live_ref[...] = jnp.broadcast_to(len_vmem[...], live_ref.shape)


def prefix_step(rows, kv_ref, other_ref):
    def extended(ref):
        return jnp.concatenate([ref[1], jnp.ones_like(ref[1])], axis=1)

    scores = dot_nt(rows, kv_ref[0])
    other_scores = dot_nt(rows, other_ref[0])
    best = jnp.max(jnp.maximum(scores, other_scores), axis=1, keepdims=True)
    weight = jnp.exp2((scores - best) * SCALE2).astype(jnp.bfloat16)
    other_weight = jnp.exp2((other_scores - best) * SCALE2).astype(jnp.bfloat16)
    both = dot(weight, extended(kv_ref)) + dot(other_weight, extended(other_ref))
    total = both[:, HD:]
    result = both[:, :HD] / total
    hi, mid, low = split3(best * SCALE2 + log2(total))
    lane = lax.broadcasted_iota(jnp.int32, (ROWS, HD), 1)
    stats = jnp.where(lane == 0, hi, jnp.where(lane == 1, mid, jnp.where(lane == 2, low, 0.0)))
    shape = (ROWS // HALF, HALF, HD)
    message = jnp.concatenate([result.reshape(shape), stats.reshape(shape)], axis=1)
    return message.reshape(2 * ROWS, HD).astype(jnp.bfloat16)


def suffix_part(q, cache, new, live):
    def owned(shape, limit):
        at = lax.broadcasted_iota(jnp.int32, shape, 1)
        head = lax.broadcasted_iota(jnp.int32, shape, 0) // SHARE
        return (at % (2 * KVH) == head) & (at < limit)

    raw = dot_nt(q, cache)
    limit = jnp.concatenate([live[:1] * (2 * KVH)] * (raw.shape[1] // HD), axis=1)
    scores = jnp.where(owned(raw.shape, limit), raw, -jnp.inf)
    new_raw = dot_nt(q, new)
    new_scores = jnp.where(owned(new_raw.shape, 2 * KVH), new_raw, -jnp.inf)
    best = jnp.maximum(jnp.max(scores, axis=1, keepdims=True), jnp.max(new_scores, axis=1, keepdims=True))
    weight = jnp.exp2((scores - best) * SCALE2).astype(jnp.bfloat16).astype(jnp.float32)
    new_weight = jnp.exp2((new_scores - best) * SCALE2).astype(jnp.bfloat16).astype(jnp.float32)
    total = jnp.sum(weight, axis=1, keepdims=True) + jnp.sum(new_weight, axis=1, keepdims=True)
    moved = pltpu.roll(weight, KVH, 1).astype(jnp.bfloat16)
    new_moved = jnp.concatenate([new_weight[:, KVH:], new_weight[:, :KVH]], axis=1).astype(jnp.bfloat16)
    return (dot(moved, cache) + dot(new_moved, new)) / total, best * SCALE2 + log2(total)


def attend_kernel(arrived_ref, kv_ref, other_ref, q_ref, cache_ref, new_ref, live_ref, out_ref, suffix_ref, lse_ref):
    trips = arrived_ref.shape[0] // ROWS

    def step(trip):
        out_ref[pl.ds(trip * 2 * ROWS, 2 * ROWS)] = prefix_step(arrived_ref[pl.ds(trip * ROWS, ROWS)], kv_ref, other_ref)

    if trips <= 4:
        for trip in range(trips):
            step(trip)
    else:

        def body(trip, unused):
            step(trip)
            return unused

        lax.fori_loop(0, trips, body, 0)
    suffix, lse = suffix_part(q_ref[...], cache_ref[...], new_ref[...], live_ref[...])
    suffix_ref[...] = suffix
    lse_ref[...] = jnp.broadcast_to(lse, lse_ref.shape)


def merge_kernel(served, part_ref, suffix_ref, lse_ref, out_ref):
    sums = dot(part_ref[...], jnp.ones((HD, HD), jnp.bfloat16)).reshape(len(served), 2 * HALF, HD)
    rows = part_ref[...].astype(jnp.float32).reshape(len(served), 2 * HALF, HD)
    blocks = []
    for block in range(H // HALF):
        span = slice(block * HALF, (block + 1) * HALF)
        own = [slot for slot, its in enumerate(served) if its == block]
        own_lse = lse_ref[span]
        best = own_lse
        for slot in own:
            best = jnp.maximum(best, sums[slot, HALF:])
        total = jnp.exp2(own_lse - best)
        numerator = total * suffix_ref[span]
        for slot in own:
            factor = jnp.exp2(sums[slot, HALF:] - best)
            total = total + factor
            numerator = numerator + factor * rows[slot, :HALF]
        blocks.append(numerator / total)
    out_ref[0] = jnp.concatenate(blocks, axis=0).astype(jnp.bfloat16)


def call(kernel, name, outs, operands, space=VMEM, scratch=(), **cost):
    if space is HBM:
        operands = [pltpu.with_memory_space_constraint(x, pltpu.HBM) if x.size > 1 else x for x in operands]
    return pl.pallas_call(
        kernel,
        out_shape=outs,
        in_specs=[space] * len(operands),
        out_specs=jax.tree.map(lambda _: VMEM, outs),
        scratch_shapes=scratch,
        name=name,
        compiler_params=pltpu.CompilerParams(vmem_limit_bytes=LIMIT),
        cost_estimate=pl.CostEstimate(**cost) if cost else None,
    )(*operands)


def local(queries, prefix_kv, suffix_kv, new_kv, suffix_len):
    groups = lax.axis_size("grp")
    members = lax.axis_size("blk")
    per_head = members // KVH
    devices = groups * members
    span = prefix_kv.shape[2]
    cache_rows = suffix_kv.shape[1] * 2 * KVH
    chips = per_head // CORES
    served = [device % members // per_head * CORES + device % CORES for device in range(devices)]

    def half(*shape):
        return jax.ShapeDtypeStruct((*shape, HD), jnp.bfloat16)

    def full(*shape):
        return jax.ShapeDtypeStruct((*shape, HD), jnp.float32)

    def exchange(array):
        array = array.reshape(devices, -1, HD)
        return lax.all_to_all(array, ("grp", "blk"), 0, 0, tiled=True).reshape(-1, HD)

    other = lax.ppermute(prefix_kv, "blk", [(i, i ^ 1) for i in range(members)])
    outgoing, q, kv, cache, new, live = call(
        load_kernel,
        "load",
        [
            half(groups, KVH, chips, SHARE),
            half(H),
            half(2, span),
            half(cache_rows),
            half(2 * KVH),
            jax.ShapeDtypeStruct((8, HD), jnp.int32),
        ],
        (
            queries.reshape(H, HD),
            prefix_kv.reshape(2, span, HD),
            suffix_kv.reshape(cache_rows, HD),
            new_kv.reshape(2 * KVH, HD),
            suffix_len.reshape(1, 1),
        ),
        HBM,
        [pltpu.VMEM((1, 1), jnp.int32), pltpu.SemaphoreType.DMA((5,))],
    )
    arrived = exchange(outgoing)
    partial, suffix, lse = call(
        attend_kernel,
        "attend",
        [half(devices * 2 * HALF), full(H), full(H)],
        (arrived, kv, other.reshape(2, span, HD), q, cache, new, live),
        flops=12 * devices * HALF * span * HD,
        bytes_accessed=1_600_000,
        transcendentals=2 * devices * HALF * span,
    )
    returned = exchange(partial)
    return call(
        functools.partial(merge_kernel, served),
        "merge",
        jax.ShapeDtypeStruct((1, H, HD), jnp.bfloat16),
        (returned, suffix, lse),
    )


def solution(mesh):
    in_specs = (
        P(("grp", "blk"), None, None),
        P(None, "grp", "blk", None),
        P(("grp", "blk"), None, None, None, None),
        P(("grp", "blk"), None, None, None),
        P(("grp", "blk")),
    )
    out_specs = P(("grp", "blk"), None, None)
    return jax.shard_map(local, mesh=mesh, in_specs=in_specs, out_specs=out_specs, check_vma=False)
```

```python
import functools
import math

import jax
import jax.numpy as jnp
from jax import lax
from jax.experimental import pallas as pl
from jax.experimental.pallas import tpu as pltpu
from jax.sharding import PartitionSpec as P

H = 64
KVH = 4
HD = 128
SHARE = H // KVH
SCALE2 = HD ** (-0.5) * math.log2(math.e)
VMEM = pl.BlockSpec(memory_space=pltpu.VMEM)
ROWS = 128
CORES = 2
HALF = SHARE // CORES
LIMIT = 24 * 1024 * 1024
NT = (((1,), (1,)), ((), ()))


def dot_nt(a, b):
    return lax.dot_general(a, b, NT, preferred_element_type=jnp.float32)


def dot(a, b):
    return jnp.dot(a, b, preferred_element_type=jnp.float32)


def log2(x):
    return jnp.log(x) * math.log2(math.e)


def split3(x):
    hi = x.astype(jnp.bfloat16).astype(jnp.float32)
    rest = x - hi
    mid = rest.astype(jnp.bfloat16).astype(jnp.float32)
    low = (rest - mid).astype(jnp.bfloat16).astype(jnp.float32)
    return hi, mid, low


def prefix_kernel(q_ref, kv_ref, other_ref, out_ref):
    per_step = ROWS // HALF
    lane = lax.broadcasted_iota(jnp.int32, (ROWS, HD), 1)

    def extended(ref):
        return jnp.concatenate([ref[1], jnp.ones_like(ref[1])], axis=1)

    def step(at):
        rows = q_ref[pl.ds(at * HALF, ROWS)]
        scores = dot_nt(rows, kv_ref[0])
        other_scores = dot_nt(rows, other_ref[0])
        best = jnp.max(jnp.maximum(scores, other_scores), axis=1, keepdims=True)
        weight = jnp.exp2((scores - best) * SCALE2).astype(jnp.bfloat16)
        other_weight = jnp.exp2((other_scores - best) * SCALE2).astype(jnp.bfloat16)
        both = dot(weight, extended(kv_ref)) + dot(other_weight, extended(other_ref))
        total = both[:, HD:]
        result = both[:, :HD] / total
        hi, mid, low = split3(best * SCALE2 + log2(total))
        stats = jnp.where(lane == 0, hi, jnp.where(lane == 1, mid, jnp.where(lane == 2, low, 0.0)))
        shape = (per_step, HALF, HD)
        message = jnp.concatenate([result.reshape(shape), stats.reshape(shape)], axis=1)
        out_ref[pl.ds(at * 2 * HALF, 2 * ROWS)] = message.reshape(2 * ROWS, HD).astype(jnp.bfloat16)

    trips = q_ref.shape[0] // ROWS
    if trips <= 4:
        for trip in range(trips):
            step(trip * per_step)
    else:

        def body(trip, unused):
            step(pl.multiple_of(trip * per_step, per_step))
            return unused

        lax.fori_loop(0, trips, body, 0)


def owned(shape, limit):
    at = lax.broadcasted_iota(jnp.int32, shape, 1)
    head = lax.broadcasted_iota(jnp.int32, shape, 0) // SHARE
    return (at % (2 * KVH) == head) & (at < limit * (2 * KVH))


def suffix_kernel(len_ref, q_ref, cache_ref, new_ref, out_ref, lse_ref):
    q = q_ref[0]
    cache = cache_ref[0]
    new = new_ref[0]
    raw = dot_nt(q, cache)
    scores = jnp.where(owned(raw.shape, len_ref[0]), raw, -jnp.inf)
    new_raw = dot_nt(q, new)
    new_scores = jnp.where(owned(new_raw.shape, 1), new_raw, -jnp.inf)
    best = jnp.maximum(jnp.max(scores, axis=1, keepdims=True), jnp.max(new_scores, axis=1, keepdims=True))
    weight = jnp.exp2((scores - best) * SCALE2).astype(jnp.bfloat16).astype(jnp.float32)
    new_weight = jnp.exp2((new_scores - best) * SCALE2).astype(jnp.bfloat16).astype(jnp.float32)
    total = jnp.sum(weight, axis=1, keepdims=True) + jnp.sum(new_weight, axis=1, keepdims=True)
    moved = pltpu.roll(weight, KVH, 1).astype(jnp.bfloat16)
    new_moved = jnp.concatenate([new_weight[:, KVH:], new_weight[:, :KVH]], axis=1).astype(jnp.bfloat16)
    out_ref[...] = (dot(moved, cache) + dot(new_moved, new)) / total
    lse_ref[...] = jnp.broadcast_to(best * SCALE2 + log2(total), lse_ref.shape)


def fan_kernel(q_ref, out_ref, q_vmem, sem, sems):
    load = pltpu.make_async_copy(q_ref, q_vmem, sem)
    load.start()
    load.wait()
    copies = [
        pltpu.make_async_copy(q_vmem, out_ref.at[group, :, chip], sems.at[group, chip])
        for group in range(out_ref.shape[0])
        for chip in range(out_ref.shape[2])
    ]
    for copy in copies:
        copy.start()
    for copy in copies:
        copy.wait()


def merge_kernel(served, part_ref, suffix_ref, lse_ref, out_ref):
    sums = dot(part_ref[...], jnp.ones((HD, HD), jnp.bfloat16)).reshape(len(served), 2 * HALF, HD)
    rows = part_ref[...].astype(jnp.float32).reshape(len(served), 2 * HALF, HD)
    blocks = []
    for block in range(H // HALF):
        span = slice(block * HALF, (block + 1) * HALF)
        own = [slot for slot, its in enumerate(served) if its == block]
        own_lse = lse_ref[span]
        best = own_lse
        for slot in own:
            best = jnp.maximum(best, sums[slot, HALF:])
        total = jnp.exp2(own_lse - best)
        numerator = total * suffix_ref[span]
        for slot in own:
            factor = jnp.exp2(sums[slot, HALF:] - best)
            total = total + factor
            numerator = numerator + factor * rows[slot, :HALF]
        blocks.append(numerator / total)
    out_ref[0] = jnp.concatenate(blocks, axis=0).astype(jnp.bfloat16)


def call(kernel, name, outs, operands, specs=None, **cost):
    return pl.pallas_call(
        kernel,
        out_shape=outs,
        in_specs=specs or [VMEM] * len(operands),
        out_specs=jax.tree.map(lambda _: VMEM, outs),
        name=name,
        compiler_params=pltpu.CompilerParams(vmem_limit_bytes=LIMIT),
        cost_estimate=pl.CostEstimate(**cost) if cost else None,
    )(*operands)


def local(queries, prefix_kv, suffix_kv, new_kv, suffix_len):
    groups = lax.axis_size("grp")
    members = lax.axis_size("blk")
    per_head = members // KVH
    devices = groups * members
    span = prefix_kv.shape[2]
    chips = per_head // CORES
    served = [device % members // per_head * CORES + device % CORES for device in range(devices)]

    def one(rows, dtype=jnp.float32):
        return jax.ShapeDtypeStruct((rows, HD), dtype)

    def exchange(array):
        return lax.all_to_all(array, ("grp", "blk"), 0, 0, tiled=True)

    other = lax.ppermute(prefix_kv, "blk", [(i, i ^ 1) for i in range(members)])
    outgoing = pl.pallas_call(
        fan_kernel,
        out_shape=jax.ShapeDtypeStruct((groups, KVH, chips, SHARE, HD), jnp.bfloat16),
        in_specs=[pl.BlockSpec(memory_space=pl.ANY)],
        out_specs=pl.BlockSpec(memory_space=pl.ANY),
        scratch_shapes=[
            pltpu.VMEM((KVH, SHARE, HD), jnp.bfloat16),
            pltpu.SemaphoreType.DMA,
            pltpu.SemaphoreType.DMA((groups, chips)),
        ],
        name="fan",
    )(pltpu.with_memory_space_constraint(queries.reshape(KVH, SHARE, HD), pltpu.HBM))
    arrived = exchange(outgoing.reshape(devices, HALF, HD)).reshape(devices * HALF, HD)

    new = new_kv.reshape(1, -1, HD)
    suffix = call(
        suffix_kernel,
        "suffix",
        [one(H)] * 2,
        (suffix_len, queries, suffix_kv.reshape(1, -1, HD), new),
        [pl.BlockSpec(memory_space=pltpu.SMEM), VMEM, VMEM, VMEM],
        flops=70_000_000,
        bytes_accessed=600_000,
        transcendentals=140_000,
    )
    arrived, suffix = lax.optimization_barrier((arrived, suffix))
    partial = call(
        prefix_kernel,
        "prefix",
        one(devices * 2 * HALF, jnp.bfloat16),
        (arrived, prefix_kv.reshape(2, span, HD), other.reshape(2, span, HD)),
        flops=12 * devices * HALF * span * HD,
        bytes_accessed=1_600_000,
        transcendentals=2 * devices * HALF * span,
    )
    returned = exchange(partial.reshape(devices, 2 * HALF, HD)).reshape(-1, HD)
    return call(
        functools.partial(merge_kernel, served),
        "merge",
        jax.ShapeDtypeStruct((1, H, HD), jnp.bfloat16),
        (returned, *suffix),
    )


def solution(mesh):
    in_specs = (
        P(("grp", "blk"), None, None),
        P(None, "grp", "blk", None),
        P(("grp", "blk"), None, None, None, None),
        P(("grp", "blk"), None, None, None),
        P(("grp", "blk")),
    )
    out_specs = P(("grp", "blk"), None, None)
    return jax.shard_map(local, mesh=mesh, in_specs=in_specs, out_specs=out_specs, check_vma=False)
```

```python
import functools
import math

import jax
import jax.numpy as jnp
from jax import lax
from jax.experimental import pallas as pl
from jax.experimental.pallas import tpu as pltpu
from jax.sharding import PartitionSpec as P

H = 64
KVH = 4
HD = 128
SHARE = H // KVH
SCALE2 = HD ** (-0.5) * math.log2(math.e)
VMEM = pl.BlockSpec(memory_space=pltpu.VMEM)
ROWS = 256
CORES = 2
HALF = SHARE // CORES
LIMIT = 24 * 1024 * 1024
NT = (((1,), (1,)), ((), ()))


def dot_nt(a, b):
    return lax.dot_general(a, b, NT, preferred_element_type=jnp.float32)


def dot(a, b):
    return jnp.dot(a, b, preferred_element_type=jnp.float32)


def log2(x):
    return jnp.log(x) * math.log2(math.e)


def split3(x):
    hi = x.astype(jnp.bfloat16).astype(jnp.float32)
    rest = x - hi
    mid = rest.astype(jnp.bfloat16).astype(jnp.float32)
    low = (rest - mid).astype(jnp.bfloat16).astype(jnp.float32)
    return hi, mid, low


def prefix_kernel(q_ref, kv_ref, other_ref, out_ref):
    per_step = ROWS // HALF
    lane = lax.broadcasted_iota(jnp.int32, (ROWS, HD), 1)

    def extended(ref):
        return jnp.concatenate([ref[1], jnp.ones_like(ref[1])], axis=1)

    def step(at):
        rows = q_ref[pl.ds(at * HALF, ROWS)]
        scores = dot_nt(rows, kv_ref[0])
        other_scores = dot_nt(rows, other_ref[0])
        best = jnp.max(jnp.maximum(scores, other_scores), axis=1, keepdims=True)
        weight = jnp.exp2((scores - best) * SCALE2).astype(jnp.bfloat16)
        other_weight = jnp.exp2((other_scores - best) * SCALE2).astype(jnp.bfloat16)
        both = dot(weight, extended(kv_ref)) + dot(other_weight, extended(other_ref))
        total = both[:, HD:]
        result = both[:, :HD] / total
        hi, mid, low = split3(best * SCALE2 + log2(total))
        stats = jnp.where(lane == 0, hi, jnp.where(lane == 1, mid, jnp.where(lane == 2, low, 0.0)))
        shape = (per_step, HALF, HD)
        message = jnp.concatenate([result.reshape(shape), stats.reshape(shape)], axis=1)
        out_ref[pl.ds(at * 2 * HALF, 2 * ROWS)] = message.reshape(2 * ROWS, HD).astype(jnp.bfloat16)

    trips = q_ref.shape[0] // ROWS
    if trips <= 4:
        for trip in range(trips):
            step(trip * per_step)
    else:

        def body(trip, unused):
            step(pl.multiple_of(trip * per_step, per_step))
            return unused

        lax.fori_loop(0, trips, body, 0)


def owned(shape, limit):
    at = lax.broadcasted_iota(jnp.int32, shape, 1)
    head = lax.broadcasted_iota(jnp.int32, shape, 0) // SHARE
    return (at % (2 * KVH) == head) & (at < limit * (2 * KVH))


def suffix_kernel(len_ref, q_ref, cache_ref, new_ref, out_ref, lse_ref):
    q = q_ref[0]
    cache = cache_ref[0]
    new = new_ref[0]
    raw = dot_nt(q, cache)
    scores = jnp.where(owned(raw.shape, len_ref[0]), raw, -jnp.inf)
    new_raw = dot_nt(q, new)
    new_scores = jnp.where(owned(new_raw.shape, 1), new_raw, -jnp.inf)
    best = jnp.maximum(jnp.max(scores, axis=1, keepdims=True), jnp.max(new_scores, axis=1, keepdims=True))
    weight = jnp.exp2((scores - best) * SCALE2).astype(jnp.bfloat16).astype(jnp.float32)
    new_weight = jnp.exp2((new_scores - best) * SCALE2).astype(jnp.bfloat16).astype(jnp.float32)
    total = jnp.sum(weight, axis=1, keepdims=True) + jnp.sum(new_weight, axis=1, keepdims=True)
    moved = pltpu.roll(weight, KVH, 1).astype(jnp.bfloat16)
    new_moved = jnp.concatenate([new_weight[:, KVH:], new_weight[:, :KVH]], axis=1).astype(jnp.bfloat16)
    out_ref[...] = (dot(moved, cache) + dot(new_moved, new)) / total
    lse_ref[...] = jnp.broadcast_to(best * SCALE2 + log2(total), lse_ref.shape)


def fan_kernel(q_ref, out_ref, q_vmem, sem):
    load = pltpu.make_async_copy(q_ref, q_vmem, sem)
    load.start()
    load.wait()
    for group in range(out_ref.shape[0]):
        for chip in range(out_ref.shape[2]):
            out_ref[group, :, chip] = q_vmem[...]


def merge_kernel(served, part_ref, suffix_ref, lse_ref, out_ref):
    sums = dot(part_ref[...], jnp.ones((HD, HD), jnp.bfloat16)).reshape(len(served), 2 * HALF, HD)
    rows = part_ref[...].astype(jnp.float32).reshape(len(served), 2 * HALF, HD)
    blocks = []
    for block in range(H // HALF):
        span = slice(block * HALF, (block + 1) * HALF)
        own = [slot for slot, its in enumerate(served) if its == block]
        own_lse = lse_ref[span]
        best = own_lse
        for slot in own:
            best = jnp.maximum(best, sums[slot, HALF:])
        total = jnp.exp2(own_lse - best)
        numerator = total * suffix_ref[span]
        for slot in own:
            factor = jnp.exp2(sums[slot, HALF:] - best)
            total = total + factor
            numerator = numerator + factor * rows[slot, :HALF]
        blocks.append(numerator / total)
    out_ref[0] = jnp.concatenate(blocks, axis=0).astype(jnp.bfloat16)


def call(kernel, name, outs, operands, specs=None, **cost):
    return pl.pallas_call(
        kernel,
        out_shape=outs,
        in_specs=specs or [VMEM] * len(operands),
        out_specs=jax.tree.map(lambda _: VMEM, outs),
        name=name,
        compiler_params=pltpu.CompilerParams(vmem_limit_bytes=LIMIT),
        cost_estimate=pl.CostEstimate(**cost) if cost else None,
    )(*operands)


def local(queries, prefix_kv, suffix_kv, new_kv, suffix_len):
    groups = lax.axis_size("grp")
    members = lax.axis_size("blk")
    per_head = members // KVH
    devices = groups * members
    span = prefix_kv.shape[2]
    chips = per_head // CORES
    served = [device % members // per_head * CORES + device % CORES for device in range(devices)]

    def one(rows, dtype=jnp.float32):
        return jax.ShapeDtypeStruct((rows, HD), dtype)

    def exchange(array):
        return lax.all_to_all(array, ("grp", "blk"), 0, 0, tiled=True)

    other = lax.ppermute(prefix_kv, "blk", [(i, i ^ 1) for i in range(members)])
    outgoing = pl.pallas_call(
        fan_kernel,
        out_shape=pltpu.VMEM((groups, KVH, chips, SHARE, HD), jnp.bfloat16),
        in_specs=[pl.BlockSpec(memory_space=pltpu.HBM)],
        out_specs=VMEM,
        scratch_shapes=[pltpu.VMEM((KVH, SHARE, HD), jnp.bfloat16), pltpu.SemaphoreType.DMA],
        name="fan",
        compiler_params=pltpu.CompilerParams(vmem_limit_bytes=LIMIT),
    )(pltpu.with_memory_space_constraint(queries.reshape(KVH, SHARE, HD), pltpu.HBM))
    arrived = exchange(outgoing.reshape(devices, HALF, HD)).reshape(devices * HALF, HD)

    new = new_kv.reshape(1, -1, HD)
    suffix = call(
        suffix_kernel,
        "suffix",
        [one(H)] * 2,
        (suffix_len, queries, suffix_kv.reshape(1, -1, HD), new),
        [pl.BlockSpec(memory_space=pltpu.SMEM), VMEM, VMEM, VMEM],
        flops=70_000_000,
        bytes_accessed=600_000,
        transcendentals=140_000,
    )
    arrived, suffix = lax.optimization_barrier((arrived, suffix))
    partial = call(
        prefix_kernel,
        "prefix",
        one(devices * 2 * HALF, jnp.bfloat16),
        (arrived, prefix_kv.reshape(2, span, HD), other.reshape(2, span, HD)),
        flops=12 * devices * HALF * span * HD,
        bytes_accessed=1_600_000,
        transcendentals=2 * devices * HALF * span,
    )
    returned = exchange(partial.reshape(devices, 2 * HALF, HD)).reshape(-1, HD)
    return call(
        functools.partial(merge_kernel, served),
        "merge",
        jax.ShapeDtypeStruct((1, H, HD), jnp.bfloat16),
        (returned, *suffix),
    )


def solution(mesh):
    in_specs = (
        P(("grp", "blk"), None, None),
        P(None, "grp", "blk", None),
        P(("grp", "blk"), None, None, None, None),
        P(("grp", "blk"), None, None, None),
        P(("grp", "blk")),
    )
    out_specs = P(("grp", "blk"), None, None)
    return jax.shard_map(local, mesh=mesh, in_specs=in_specs, out_specs=out_specs, check_vma=False)
```

```python
import functools
import math

import jax
import jax.numpy as jnp
from jax import lax
from jax.experimental import pallas as pl
from jax.experimental.pallas import tpu as pltpu
from jax.sharding import PartitionSpec as P

H = 64
KVH = 4
HD = 128
SHARE = H // KVH
SCALE2 = HD ** (-0.5) * math.log2(math.e)
VMEM = pl.BlockSpec(memory_space=pltpu.VMEM)
ROWS = 256
CHUNK = 512
CORES = 2
HALF = SHARE // CORES
LIMIT = 24 * 1024 * 1024
NT = (((1,), (1,)), ((), ()))


def dot_nt(a, b):
    return lax.dot_general(a, b, NT, preferred_element_type=jnp.float32)


def dot(a, b):
    return jnp.dot(a, b, preferred_element_type=jnp.float32)


def log2(x):
    return jnp.log(x) * math.log2(math.e)


def split3(x):
    hi = x.astype(jnp.bfloat16).astype(jnp.float32)
    rest = x - hi
    mid = rest.astype(jnp.bfloat16).astype(jnp.float32)
    low = (rest - mid).astype(jnp.bfloat16).astype(jnp.float32)
    return hi, mid, low


def prefix_kernel(q_ref, keys_ref, other_keys_ref, kv_ref, other_ref, out_ref):
    lane = lax.broadcasted_iota(jnp.int32, (ROWS, HD), 1)
    shape = (ROWS // HALF, HALF, HD)
    pairs = [(other_keys_ref, other_ref), (keys_ref, kv_ref)]
    chunks = [(keys, ref, at) for keys, ref in pairs for at in range(0, ref.shape[1], CHUNK)]

    def block(at):
        rows = q_ref[pl.ds(at, ROWS)]

        def score(keys, ref, first):
            return dot(rows, keys[:, first : first + CHUNK])

        parts = []
        ahead = score(*chunks[0])
        for index, (keys, ref, first) in enumerate(chunks):
            scores = ahead
            if index + 1 < len(chunks):
                ahead = score(*chunks[index + 1])
            best = jnp.max(scores, axis=1, keepdims=True)
            weight = jnp.exp2((scores - best) * SCALE2).astype(jnp.bfloat16)
            values = ref[1, first : first + CHUNK]
            parts.append((best, dot(weight, jnp.concatenate([values, jnp.ones_like(values)], axis=1))))
        best = functools.reduce(jnp.maximum, [part[0] for part in parts])
        both = sum(jnp.exp2((its - best) * SCALE2) * sums for its, sums in parts)
        total = both[:, HD:]
        result = both[:, :HD] / total
        hi, mid, low = split3(best * SCALE2 + log2(total))
        stats = jnp.where(lane == 0, hi, jnp.where(lane == 1, mid, jnp.where(lane == 2, low, 0.0)))
        message = jnp.concatenate([result.reshape(shape), stats.reshape(shape)], axis=1)
        out_ref[pl.ds(at * 2, 2 * ROWS)] = message.reshape(2 * ROWS, HD).astype(jnp.bfloat16)

    trips = q_ref.shape[0] // ROWS
    if trips == 1:
        block(0)
    else:

        def body(trip, unused):
            block(pl.multiple_of(trip * ROWS, ROWS))
            return unused

        lax.fori_loop(0, trips, body, 0)


def owned(shape, limit):
    at = lax.broadcasted_iota(jnp.int32, shape, 1)
    head = lax.broadcasted_iota(jnp.int32, shape, 0) // SHARE
    return (at % (2 * KVH) == head) & (at < limit * (2 * KVH))


def aside_kernel(
    len_ref, q_hbm, cache_hbm, new_hbm, kv_hbm, other_ref, out_ref, lse_ref, keys_ref, other_keys_ref, kv_ref, q_ref, cache_ref, new_ref, sems
):
    pairs = [(kv_hbm, kv_ref), (cache_hbm, cache_ref), (q_hbm, q_ref), (new_hbm, new_ref)]
    copies = [pltpu.make_async_copy(source, target, sems.at[i]) for i, (source, target) in enumerate(pairs)]
    for copy in copies:
        copy.start()
    other_keys_ref[...] = other_ref[0].T
    for copy in copies:
        copy.wait()
    keys_ref[...] = kv_ref[0].T
    q = q_ref[...]
    cache = cache_ref[...]
    new = new_ref[...]
    raw = dot_nt(q, cache)
    scores = jnp.where(owned(raw.shape, len_ref[0]), raw, -jnp.inf)
    new_raw = dot_nt(q, new)
    new_scores = jnp.where(owned(new_raw.shape, 1), new_raw, -jnp.inf)
    best = jnp.maximum(jnp.max(scores, axis=1, keepdims=True), jnp.max(new_scores, axis=1, keepdims=True))
    weight = jnp.exp2((scores - best) * SCALE2).astype(jnp.bfloat16).astype(jnp.float32)
    new_weight = jnp.exp2((new_scores - best) * SCALE2).astype(jnp.bfloat16).astype(jnp.float32)
    total = jnp.sum(weight, axis=1, keepdims=True) + jnp.sum(new_weight, axis=1, keepdims=True)
    moved = pltpu.roll(weight, KVH, 1).astype(jnp.bfloat16)
    new_moved = jnp.concatenate([new_weight[:, KVH:], new_weight[:, :KVH]], axis=1).astype(jnp.bfloat16)
    out_ref[...] = (dot(moved, cache) + dot(new_moved, new)) / total
    lse_ref[...] = jnp.broadcast_to(best * SCALE2 + log2(total), lse_ref.shape)


def fan_kernel(q_ref, out_ref, q_vmem, sem, sems):
    load = pltpu.make_async_copy(q_ref, q_vmem, sem)
    load.start()
    load.wait()
    copies = [
        pltpu.make_async_copy(q_vmem, out_ref.at[group, :, chip], sems.at[group, chip])
        for group in range(out_ref.shape[0])
        for chip in range(out_ref.shape[2])
    ]
    for copy in copies:
        copy.start()
    for copy in copies:
        copy.wait()


def merge_kernel(served, part_ref, suffix_ref, lse_ref, out_ref):
    sums = dot(part_ref[...], jnp.ones((HD, HD), jnp.bfloat16)).reshape(len(served), 2 * HALF, HD)
    rows = part_ref[...].astype(jnp.float32).reshape(len(served), 2 * HALF, HD)
    blocks = []
    for block in range(H // HALF):
        span = slice(block * HALF, (block + 1) * HALF)
        own = [slot for slot, its in enumerate(served) if its == block]
        own_lse = lse_ref[span]
        best = own_lse
        for slot in own:
            best = jnp.maximum(best, sums[slot, HALF:])
        total = jnp.exp2(own_lse - best)
        numerator = total * suffix_ref[span]
        for slot in own:
            factor = jnp.exp2(sums[slot, HALF:] - best)
            total = total + factor
            numerator = numerator + factor * rows[slot, :HALF]
        blocks.append(numerator / total)
    out_ref[0] = jnp.concatenate(blocks, axis=0).astype(jnp.bfloat16)


def call(kernel, name, outs, operands, specs=None, **cost):
    return pl.pallas_call(
        kernel,
        out_shape=outs,
        in_specs=specs or [VMEM] * len(operands),
        out_specs=jax.tree.map(lambda _: VMEM, outs),
        name=name,
        compiler_params=pltpu.CompilerParams(vmem_limit_bytes=LIMIT),
        cost_estimate=pl.CostEstimate(**cost) if cost else None,
    )(*operands)


def local(queries, prefix_kv, suffix_kv, new_kv, suffix_len):
    groups = lax.axis_size("grp")
    members = lax.axis_size("blk")
    per_head = members // KVH
    devices = groups * members
    span = prefix_kv.shape[2]
    cache_rows = suffix_kv.shape[1] * 2 * KVH
    chips = per_head // CORES
    served = [device % members // per_head * CORES + device % CORES for device in range(devices)]

    def one(rows):
        return jax.ShapeDtypeStruct((rows, HD), jnp.float32)

    def half(*shape):
        return jax.ShapeDtypeStruct((*shape, HD), jnp.bfloat16)

    def exchange(array):
        return lax.all_to_all(array, ("grp", "blk"), 0, 0, tiled=True)

    other = lax.ppermute(prefix_kv, "blk", [(i, i ^ 1) for i in range(members)])
    outgoing = pl.pallas_call(
        fan_kernel,
        out_shape=jax.ShapeDtypeStruct((groups, KVH, chips, SHARE, HD), jnp.bfloat16),
        in_specs=[pl.BlockSpec(memory_space=pl.ANY)],
        out_specs=pl.BlockSpec(memory_space=pl.ANY),
        scratch_shapes=[
            pltpu.VMEM((KVH, SHARE, HD), jnp.bfloat16),
            pltpu.SemaphoreType.DMA,
            pltpu.SemaphoreType.DMA((groups, chips)),
        ],
        name="fan",
    )(pltpu.with_memory_space_constraint(queries.reshape(KVH, SHARE, HD), pltpu.HBM))
    arrived = exchange(outgoing.reshape(devices, HALF, HD)).reshape(devices * HALF, HD)

    other = other.reshape(2, span, HD)
    bound = [
        pltpu.with_memory_space_constraint(array, pltpu.HBM)
        for array in (
            queries.reshape(H, HD),
            suffix_kv.reshape(cache_rows, HD),
            new_kv.reshape(2 * KVH, HD),
            prefix_kv.reshape(2, span, HD),
        )
    ]
    aside = pl.pallas_call(
        aside_kernel,
        out_shape=[one(H), one(H), *[jax.ShapeDtypeStruct((HD, span), jnp.bfloat16)] * 2, half(2, span)],
        in_specs=[pl.BlockSpec(memory_space=pltpu.SMEM), *[pl.BlockSpec(memory_space=pltpu.HBM)] * 4, VMEM],
        out_specs=[VMEM] * 5,
        scratch_shapes=[
            pltpu.VMEM((H, HD), jnp.bfloat16),
            pltpu.VMEM((cache_rows, HD), jnp.bfloat16),
            pltpu.VMEM((2 * KVH, HD), jnp.bfloat16),
            pltpu.SemaphoreType.DMA((4,)),
        ],
        name="aside",
        compiler_params=pltpu.CompilerParams(vmem_limit_bytes=LIMIT),
        cost_estimate=pl.CostEstimate(flops=70_000_000, bytes_accessed=1_200_000, transcendentals=140_000),
    )(suffix_len, *bound, other)
    arrived, aside = lax.optimization_barrier((arrived, aside))
    suffix, suffix_lse, keys, other_keys, kv = aside
    partial = call(
        prefix_kernel,
        "prefix",
        half(devices * 2 * HALF),
        (arrived, keys, other_keys, kv, other),
        flops=12 * devices * HALF * span * HD,
        bytes_accessed=1_600_000,
        transcendentals=2 * devices * HALF * span,
    )
    returned = exchange(partial.reshape(devices, 2 * HALF, HD)).reshape(-1, HD)
    return call(
        functools.partial(merge_kernel, served),
        "merge",
        jax.ShapeDtypeStruct((1, H, HD), jnp.bfloat16),
        (returned, suffix, suffix_lse),
    )


def solution(mesh):
    in_specs = (
        P(("grp", "blk"), None, None),
        P(None, "grp", "blk", None),
        P(("grp", "blk"), None, None, None, None),
        P(("grp", "blk"), None, None, None),
        P(("grp", "blk")),
    )
    out_specs = P(("grp", "blk"), None, None)
    return jax.shard_map(local, mesh=mesh, in_specs=in_specs, out_specs=out_specs, check_vma=False)
```

```python
import functools
import math

import jax
import jax.numpy as jnp
from jax import lax
from jax.experimental import pallas as pl
from jax.experimental.pallas import tpu as pltpu
from jax.sharding import PartitionSpec as P

H = 64
KVH = 4
HD = 128
SHARE = H // KVH
SCALE2 = HD ** (-0.5) * math.log2(math.e)
VMEM = pl.BlockSpec(memory_space=pltpu.VMEM)
ROWS = 256
CHUNK = 512
CORES = 2
HALF = SHARE // CORES
LIMIT = 24 * 1024 * 1024
NT = (((1,), (1,)), ((), ()))


def dot_nt(a, b):
    return lax.dot_general(a, b, NT, preferred_element_type=jnp.float32)


def dot(a, b):
    return jnp.dot(a, b, preferred_element_type=jnp.float32)


def log2(x):
    return jnp.log(x) * math.log2(math.e)


def split3(x):
    hi = x.astype(jnp.bfloat16).astype(jnp.float32)
    rest = x - hi
    mid = rest.astype(jnp.bfloat16).astype(jnp.float32)
    low = (rest - mid).astype(jnp.bfloat16).astype(jnp.float32)
    return hi, mid, low


def prefix_part(q_ref, kv_ref, other_ref, out_ref):
    lane = lax.broadcasted_iota(jnp.int32, (ROWS, HD), 1)
    shape = (ROWS // HALF, HALF, HD)
    chunks = [(ref, at) for ref in (other_ref, kv_ref) for at in range(0, ref.shape[1], CHUNK)]

    def block(at):
        rows = q_ref[pl.ds(at, ROWS)]

        def score(ref, first):
            return dot_nt(rows, ref[0, first : first + CHUNK])

        parts = []
        ahead = score(*chunks[0])
        for index, (ref, first) in enumerate(chunks):
            scores = ahead
            if index + 1 < len(chunks):
                ahead = score(*chunks[index + 1])
            best = jnp.max(scores, axis=1, keepdims=True)
            weight = jnp.exp2((scores - best) * SCALE2).astype(jnp.bfloat16)
            values = ref[1, first : first + CHUNK]
            parts.append((best, dot(weight, jnp.concatenate([values, jnp.ones_like(values)], axis=1))))
        best = functools.reduce(jnp.maximum, [part[0] for part in parts])
        both = sum(jnp.exp2((its - best) * SCALE2) * sums for its, sums in parts)
        total = both[:, HD:]
        result = both[:, :HD] / total
        hi, mid, low = split3(best * SCALE2 + log2(total))
        stats = jnp.where(lane == 0, hi, jnp.where(lane == 1, mid, jnp.where(lane == 2, low, 0.0)))
        message = jnp.concatenate([result.reshape(shape), stats.reshape(shape)], axis=1)
        out_ref[pl.ds(at * 2, 2 * ROWS)] = message.reshape(2 * ROWS, HD).astype(jnp.bfloat16)

    trips = q_ref.shape[0] // ROWS
    if trips == 1:
        block(0)
    else:

        def body(trip, unused):
            block(pl.multiple_of(trip * ROWS, ROWS))
            return unused

        lax.fori_loop(0, trips, body, 0)


def owned(shape, limit):
    at = lax.broadcasted_iota(jnp.int32, shape, 1)
    head = lax.broadcasted_iota(jnp.int32, shape, 0) // SHARE
    return (at % (2 * KVH) == head) & (at < limit * (2 * KVH))


def suffix_part(q, cache, new, live, out_ref, lse_ref):
    raw = dot_nt(q, cache)
    scores = jnp.where(owned(raw.shape, live), raw, -jnp.inf)
    new_raw = dot_nt(q, new)
    new_scores = jnp.where(owned(new_raw.shape, 1), new_raw, -jnp.inf)
    best = jnp.maximum(jnp.max(scores, axis=1, keepdims=True), jnp.max(new_scores, axis=1, keepdims=True))
    weight = jnp.exp2((scores - best) * SCALE2).astype(jnp.bfloat16).astype(jnp.float32)
    new_weight = jnp.exp2((new_scores - best) * SCALE2).astype(jnp.bfloat16).astype(jnp.float32)
    total = jnp.sum(weight, axis=1, keepdims=True) + jnp.sum(new_weight, axis=1, keepdims=True)
    moved = pltpu.roll(weight, KVH, 1).astype(jnp.bfloat16)
    new_moved = jnp.concatenate([new_weight[:, KVH:], new_weight[:, :KVH]], axis=1).astype(jnp.bfloat16)
    out_ref[...] = (dot(moved, cache) + dot(new_moved, new)) / total
    lse_ref[...] = jnp.broadcast_to(best * SCALE2 + log2(total), lse_ref.shape)


def attend_kernel(
    arrived_ref, kv_ref, other_ref, q_hbm, cache_hbm, new_hbm, len_hbm, out_ref, suffix_ref, lse_ref, q_ref, cache_ref, new_ref, len_ref, sems
):
    pairs = [(cache_hbm, cache_ref), (q_hbm, q_ref), (new_hbm, new_ref), (len_hbm, len_ref)]
    copies = [pltpu.make_async_copy(source, target, sems.at[i]) for i, (source, target) in enumerate(pairs)]
    for copy in copies:
        copy.start()
    prefix_part(arrived_ref, kv_ref, other_ref, out_ref)
    for copy in copies:
        copy.wait()
    suffix_part(q_ref[...], cache_ref[...], new_ref[...], len_ref[...], suffix_ref, lse_ref)


def merge_kernel(served, part_ref, suffix_ref, lse_ref, out_ref):
    sums = dot(part_ref[...], jnp.ones((HD, HD), jnp.bfloat16)).reshape(len(served), 2 * HALF, HD)
    rows = part_ref[...].astype(jnp.float32).reshape(len(served), 2 * HALF, HD)
    blocks = []
    for block in range(H // HALF):
        span = slice(block * HALF, (block + 1) * HALF)
        own = [slot for slot, its in enumerate(served) if its == block]
        own_lse = lse_ref[span]
        best = own_lse
        for slot in own:
            best = jnp.maximum(best, sums[slot, HALF:])
        total = jnp.exp2(own_lse - best)
        numerator = total * suffix_ref[span]
        for slot in own:
            factor = jnp.exp2(sums[slot, HALF:] - best)
            total = total + factor
            numerator = numerator + factor * rows[slot, :HALF]
        blocks.append(numerator / total)
    out_ref[0] = jnp.concatenate(blocks, axis=0).astype(jnp.bfloat16)


def call(kernel, name, outs, operands, specs=None, **cost):
    return pl.pallas_call(
        kernel,
        out_shape=outs,
        in_specs=specs or [VMEM] * len(operands),
        out_specs=jax.tree.map(lambda _: VMEM, outs),
        name=name,
        compiler_params=pltpu.CompilerParams(vmem_limit_bytes=LIMIT),
        cost_estimate=pl.CostEstimate(**cost) if cost else None,
    )(*operands)


def local(queries, prefix_kv, suffix_kv, new_kv, suffix_len):
    groups = lax.axis_size("grp")
    members = lax.axis_size("blk")
    per_head = members // KVH
    devices = groups * members
    span = prefix_kv.shape[2]
    cache_rows = suffix_kv.shape[1] * 2 * KVH
    chips = per_head // CORES
    served = [device % members // per_head * CORES + device % CORES for device in range(devices)]

    def half(*shape):
        return jax.ShapeDtypeStruct((*shape, HD), jnp.bfloat16)

    def full(*shape):
        return jax.ShapeDtypeStruct((*shape, HD), jnp.float32)

    def exchange(array):
        array = array.reshape(devices, -1, HD)
        return lax.all_to_all(array, ("grp", "blk"), 0, 0, tiled=True).reshape(-1, HD)

    def fetch(array, step=0):
        return lax.ppermute(array, "blk", [(i, i ^ step) for i in range(members)])

    other = fetch(prefix_kv, 1).reshape(2, span, HD)
    kv = fetch(prefix_kv).reshape(2, span, HD)
    live = fetch(suffix_len).reshape(1, 1)
    outgoing = queries.reshape(1, KVH, 1, SHARE, HD)
    arrived = exchange(jnp.broadcast_to(outgoing, (groups, KVH, chips, SHARE, HD)))
    bound = [
        pltpu.with_memory_space_constraint(array, pltpu.HBM)
        for array in (queries.reshape(H, HD), suffix_kv.reshape(cache_rows, HD), new_kv.reshape(2 * KVH, HD), live)
    ]
    partial, suffix, lse = pl.pallas_call(
        attend_kernel,
        out_shape=[half(devices * 2 * HALF), full(H), full(H)],
        in_specs=[VMEM] * 3 + [pl.BlockSpec(memory_space=pltpu.HBM)] * 4,
        out_specs=[VMEM] * 3,
        scratch_shapes=[
            pltpu.VMEM((H, HD), jnp.bfloat16),
            pltpu.VMEM((cache_rows, HD), jnp.bfloat16),
            pltpu.VMEM((2 * KVH, HD), jnp.bfloat16),
            pltpu.VMEM((1, 1), jnp.int32),
            pltpu.SemaphoreType.DMA((4,)),
        ],
        name="attend",
        compiler_params=pltpu.CompilerParams(vmem_limit_bytes=LIMIT),
        cost_estimate=pl.CostEstimate(
            flops=12 * devices * HALF * span * HD,
            bytes_accessed=1_600_000,
            transcendentals=2 * devices * HALF * span,
        ),
    )(arrived, kv, other, *bound)
    returned = exchange(partial)
    return call(
        functools.partial(merge_kernel, served),
        "merge",
        jax.ShapeDtypeStruct((1, H, HD), jnp.bfloat16),
        (returned, suffix, lse),
    )


def solution(mesh):
    in_specs = (
        P(("grp", "blk"), None, None),
        P(None, "grp", "blk", None),
        P(("grp", "blk"), None, None, None, None),
        P(("grp", "blk"), None, None, None),
        P(("grp", "blk")),
    )
    out_specs = P(("grp", "blk"), None, None)
    return jax.shard_map(local, mesh=mesh, in_specs=in_specs, out_specs=out_specs, check_vma=False)
```

```python
import functools
import math

import jax
import jax.numpy as jnp
from jax import lax
from jax.experimental import pallas as pl
from jax.experimental.pallas import tpu as pltpu
from jax.sharding import PartitionSpec as P

H = 64
KVH = 4
HD = 128
SHARE = H // KVH
SCALE2 = HD ** (-0.5) * math.log2(math.e)
VMEM = pl.BlockSpec(memory_space=pltpu.VMEM)
ROWS = 256
CHUNK = 512
CORES = 2
HALF = SHARE // CORES
MESSAGE = HALF + 2
LANES = HD // HALF
LIMIT = 24 * 1024 * 1024
NT = (((1,), (1,)), ((), ()))


def dot_nt(a, b):
    return lax.dot_general(a, b, NT, preferred_element_type=jnp.float32)


def dot(a, b):
    return jnp.dot(a, b, preferred_element_type=jnp.float32)


def log2(x):
    return jnp.log(x) * math.log2(math.e)


def pack_stats(x):
    hi = x.astype(jnp.bfloat16).astype(jnp.float32)
    rest = x - hi
    mid = rest.astype(jnp.bfloat16).astype(jnp.float32)
    low = rest - mid
    row = lax.broadcasted_iota(jnp.int32, x.shape, 1)
    lane = lax.broadcasted_iota(jnp.int32, x.shape, 2) - row * LANES
    return jnp.sum(jnp.where(lane == 0, hi, jnp.where(lane == 1, mid, jnp.where(lane == 2, low, 0.0))), axis=1)


def unpack_stats(rows):
    shape = (HALF, HD)
    mine = lax.broadcasted_iota(jnp.int32, shape, 1) // LANES == lax.broadcasted_iota(jnp.int32, shape, 0)
    pieces = [jnp.where(mine, jnp.broadcast_to(row, shape), 0.0) for row in rows]
    return dot(jnp.concatenate(pieces, axis=0).astype(jnp.bfloat16), jnp.ones((HD, HD), jnp.bfloat16))


def prefix_kernel(q_ref, kv_ref, other_ref, out_ref):
    chunks = [(ref, at) for ref in (other_ref, kv_ref) for at in range(0, ref.shape[1], CHUNK)]

    def block(trip):
        rows = q_ref[pl.ds(trip * ROWS, ROWS)]

        def score(ref, first):
            return dot_nt(rows, ref[0, first : first + CHUNK])

        parts = []
        ahead = score(*chunks[0])
        for index, (ref, first) in enumerate(chunks):
            scores = ahead
            if index + 1 < len(chunks):
                ahead = score(*chunks[index + 1])
            best = jnp.max(scores, axis=1, keepdims=True)
            weight = jnp.exp2((scores - best) * SCALE2).astype(jnp.bfloat16)
            values = ref[1, first : first + CHUNK]
            parts.append((best, dot(weight, jnp.concatenate([values, jnp.ones_like(values)], axis=1))))
        best = functools.reduce(jnp.maximum, [part[0] for part in parts])
        both = sum(jnp.exp2((its - best) * SCALE2) * sums for its, sums in parts)
        total = both[:, HD:]
        result = both[:, :HD] / total
        slots = ROWS // HALF
        stats = pack_stats((best * SCALE2 + log2(total)).reshape(slots, HALF, HD))
        empty = jnp.zeros((1, HD), jnp.float32)
        pieces = []
        for slot in range(slots):
            pieces += [result[slot * HALF : (slot + 1) * HALF], stats[slot : slot + 1], empty]
        out_ref[pl.ds(trip * slots * MESSAGE, slots * MESSAGE)] = jnp.concatenate(pieces, axis=0).astype(jnp.bfloat16)

    trips = q_ref.shape[0] // ROWS
    if trips == 1:
        block(0)
    else:

        def body(trip, unused):
            block(trip)
            return unused

        lax.fori_loop(0, trips, body, 0)


def owned(shape, limit):
    at = lax.broadcasted_iota(jnp.int32, shape, 1)
    head = lax.broadcasted_iota(jnp.int32, shape, 0) // SHARE
    return (at % (2 * KVH) == head) & (at < limit * (2 * KVH))


def aside_kernel(len_ref, new_ref, q_hbm, cache_hbm, kv_hbm, out_ref, lse_ref, kv_ref, q_ref, cache_ref, sems):
    pairs = [(q_hbm, q_ref), (cache_hbm, cache_ref), (kv_hbm, kv_ref)]
    copies = [pltpu.make_async_copy(source, target, sems.at[i]) for i, (source, target) in enumerate(pairs)]
    for copy in copies:
        copy.start()
    copies[0].wait()
    copies[1].wait()
    q = q_ref[...]
    cache = cache_ref[...]
    new = new_ref[...]
    raw = dot_nt(q, cache)
    scores = jnp.where(owned(raw.shape, len_ref[0]), raw, -jnp.inf)
    new_raw = dot_nt(q, new)
    new_scores = jnp.where(owned(new_raw.shape, 1), new_raw, -jnp.inf)
    best = jnp.maximum(jnp.max(scores, axis=1, keepdims=True), jnp.max(new_scores, axis=1, keepdims=True))
    weight = jnp.exp2((scores - best) * SCALE2).astype(jnp.bfloat16).astype(jnp.float32)
    new_weight = jnp.exp2((new_scores - best) * SCALE2).astype(jnp.bfloat16).astype(jnp.float32)
    total = jnp.sum(weight, axis=1, keepdims=True) + jnp.sum(new_weight, axis=1, keepdims=True)
    moved = pltpu.roll(weight, KVH, 1).astype(jnp.bfloat16)
    new_moved = jnp.concatenate([new_weight[:, KVH:], new_weight[:, :KVH]], axis=1).astype(jnp.bfloat16)
    out_ref[...] = (dot(moved, cache) + dot(new_moved, new)) / total
    lse_ref[...] = jnp.broadcast_to(best * SCALE2 + log2(total), lse_ref.shape)
    copies[2].wait()


def fan_kernel(q_ref, out_ref, q_vmem, sem, sems):
    load = pltpu.make_async_copy(q_ref, q_vmem, sem)
    load.start()
    load.wait()
    copies = [
        pltpu.make_async_copy(q_vmem, out_ref.at[group, :, chip], sems.at[group, chip])
        for group in range(out_ref.shape[0])
        for chip in range(out_ref.shape[2])
    ]
    for copy in copies:
        copy.start()
    for copy in copies:
        copy.wait()


def merge_kernel(served, part_ref, suffix_ref, lse_ref, out_ref):
    part = part_ref[...].astype(jnp.float32)
    starts = range(0, len(served) * MESSAGE, MESSAGE)
    rows = [part[at : at + HALF] for at in starts]
    sums = unpack_stats([part[at + HALF : at + HALF + 1] for at in starts]).reshape(len(served), HALF, HD)
    blocks = []
    for block in range(H // HALF):
        span = slice(block * HALF, (block + 1) * HALF)
        own = [slot for slot, its in enumerate(served) if its == block]
        own_lse = lse_ref[span]
        best = own_lse
        for slot in own:
            best = jnp.maximum(best, sums[slot])
        total = jnp.exp2(own_lse - best)
        numerator = total * suffix_ref[span]
        for slot in own:
            factor = jnp.exp2(sums[slot] - best)
            total = total + factor
            numerator = numerator + factor * rows[slot]
        blocks.append(numerator / total)
    out_ref[0] = jnp.concatenate(blocks, axis=0).astype(jnp.bfloat16)


def call(kernel, name, outs, operands, specs=None, **cost):
    return pl.pallas_call(
        kernel,
        out_shape=outs,
        in_specs=specs or [VMEM] * len(operands),
        out_specs=jax.tree.map(lambda _: VMEM, outs),
        name=name,
        compiler_params=pltpu.CompilerParams(vmem_limit_bytes=LIMIT),
        cost_estimate=pl.CostEstimate(**cost) if cost else None,
    )(*operands)


def local(queries, prefix_kv, suffix_kv, new_kv, suffix_len):
    groups = lax.axis_size("grp")
    members = lax.axis_size("blk")
    per_head = members // KVH
    devices = groups * members
    span = prefix_kv.shape[2]
    cache_rows = suffix_kv.shape[1] * 2 * KVH
    chips = per_head // CORES
    served = [device % members // per_head * CORES + device % CORES for device in range(devices)]

    def one(rows):
        return jax.ShapeDtypeStruct((rows, HD), jnp.float32)

    def half(*shape):
        return jax.ShapeDtypeStruct((*shape, HD), jnp.bfloat16)

    def exchange(array):
        return lax.all_to_all(array, ("grp", "blk"), 0, 0, tiled=True)

    other = lax.ppermute(prefix_kv, "blk", [(i, i ^ 1) for i in range(members)])
    outgoing = pl.pallas_call(
        fan_kernel,
        out_shape=jax.ShapeDtypeStruct((groups, KVH, chips, SHARE, HD), jnp.bfloat16),
        in_specs=[pl.BlockSpec(memory_space=pl.ANY)],
        out_specs=pl.BlockSpec(memory_space=pl.ANY),
        scratch_shapes=[
            pltpu.VMEM((KVH, SHARE, HD), jnp.bfloat16),
            pltpu.SemaphoreType.DMA,
            pltpu.SemaphoreType.DMA((groups, chips)),
        ],
        name="fan",
    )(pltpu.with_memory_space_constraint(queries.reshape(KVH, SHARE, HD), pltpu.HBM))
    arrived = exchange(outgoing.reshape(devices, HALF, HD)).reshape(devices * HALF, HD)

    other = other.reshape(2, span, HD)
    bound = [
        pltpu.with_memory_space_constraint(array, pltpu.HBM)
        for array in (queries.reshape(H, HD), suffix_kv.reshape(cache_rows, HD), prefix_kv.reshape(2, span, HD))
    ]
    aside = pl.pallas_call(
        aside_kernel,
        out_shape=[one(H), one(H), half(2, span)],
        in_specs=[pl.BlockSpec(memory_space=pltpu.SMEM), VMEM, *[pl.BlockSpec(memory_space=pltpu.HBM)] * 3],
        out_specs=[VMEM] * 3,
        scratch_shapes=[
            pltpu.VMEM((H, HD), jnp.bfloat16),
            pltpu.VMEM((cache_rows, HD), jnp.bfloat16),
            pltpu.SemaphoreType.DMA((3,)),
        ],
        name="aside",
        compiler_params=pltpu.CompilerParams(vmem_limit_bytes=LIMIT),
        cost_estimate=pl.CostEstimate(flops=70_000_000, bytes_accessed=1_200_000, transcendentals=140_000),
    )(suffix_len, new_kv.reshape(2 * KVH, HD), *bound)
    arrived, aside = lax.optimization_barrier((arrived, aside))
    suffix, suffix_lse, kv = aside
    partial = call(
        prefix_kernel,
        "prefix",
        half(devices * MESSAGE),
        (arrived, kv, other),
        flops=12 * devices * HALF * span * HD,
        bytes_accessed=1_600_000,
        transcendentals=2 * devices * HALF * span,
    )
    returned = exchange(partial.reshape(devices, MESSAGE // 2, 2, HD)).reshape(-1, HD)
    return call(
        functools.partial(merge_kernel, served),
        "merge",
        jax.ShapeDtypeStruct((1, H, HD), jnp.bfloat16),
        (returned, suffix, suffix_lse),
    )


def solution(mesh):
    in_specs = (
        P(("grp", "blk"), None, None),
        P(None, "grp", "blk", None),
        P(("grp", "blk"), None, None, None, None),
        P(("grp", "blk"), None, None, None),
        P(("grp", "blk")),
    )
    out_specs = P(("grp", "blk"), None, None)
    return jax.shard_map(local, mesh=mesh, in_specs=in_specs, out_specs=out_specs, check_vma=False)
```

```python
import functools
import math

import jax
import jax.numpy as jnp
from jax import lax
from jax.experimental import pallas as pl
from jax.experimental.pallas import tpu as pltpu
from jax.sharding import PartitionSpec as P

H = 64
KVH = 4
HD = 128
SHARE = H // KVH
SCALE2 = HD ** (-0.5) * math.log2(math.e)
VMEM = pl.BlockSpec(memory_space=pltpu.VMEM)
ROWS = 256
CHUNK = 512
CORES = 2
HALF = SHARE // CORES
MESSAGE = HALF + 2
LANES = HD // HALF
LIMIT = 24 * 1024 * 1024
NT = (((1,), (1,)), ((), ()))


def dot_nt(a, b):
    return lax.dot_general(a, b, NT, preferred_element_type=jnp.float32)


def dot(a, b):
    return jnp.dot(a, b, preferred_element_type=jnp.float32)


def log2(x):
    return jnp.log(x) * math.log2(math.e)


def pack_stats(x):
    hi = x.astype(jnp.bfloat16).astype(jnp.float32)
    rest = x - hi
    mid = rest.astype(jnp.bfloat16).astype(jnp.float32)
    low = rest - mid
    row = lax.broadcasted_iota(jnp.int32, x.shape, 1)
    lane = lax.broadcasted_iota(jnp.int32, x.shape, 2) - row * LANES
    return jnp.sum(jnp.where(lane == 0, hi, jnp.where(lane == 1, mid, jnp.where(lane == 2, low, 0.0))), axis=1)


def unpack_stats(rows):
    shape = (HALF, HD)
    mine = lax.broadcasted_iota(jnp.int32, shape, 1) // LANES == lax.broadcasted_iota(jnp.int32, shape, 0)
    pieces = [jnp.where(mine, jnp.broadcast_to(row, shape), 0.0) for row in rows]
    return dot(jnp.concatenate(pieces, axis=0).astype(jnp.bfloat16), jnp.ones((HD, HD), jnp.bfloat16))


def prefix_kernel(q_ref, kv_ref, other_ref, out_ref):
    chunks = [(ref, at) for ref in (other_ref, kv_ref) for at in range(0, ref.shape[1], CHUNK)]

    def block(trip):
        rows = q_ref[pl.ds(trip * ROWS, ROWS)]

        def score(ref, first):
            return dot_nt(rows, ref[0, first : first + CHUNK])

        parts = []
        ahead = score(*chunks[0])
        for index, (ref, first) in enumerate(chunks):
            scores = ahead
            if index + 1 < len(chunks):
                ahead = score(*chunks[index + 1])
            best = jnp.max(scores, axis=1, keepdims=True)
            weight = jnp.exp2((scores - best) * SCALE2).astype(jnp.bfloat16)
            values = ref[1, first : first + CHUNK]
            parts.append((best, dot(weight, jnp.concatenate([values, jnp.ones_like(values)], axis=1))))
        best = functools.reduce(jnp.maximum, [part[0] for part in parts])
        both = sum(jnp.exp2((its - best) * SCALE2) * sums for its, sums in parts)
        total = both[:, HD:]
        result = both[:, :HD] / total
        slots = ROWS // HALF
        stats = pack_stats((best * SCALE2 + log2(total)).reshape(slots, HALF, HD))
        empty = jnp.zeros((1, HD), jnp.float32)
        pieces = []
        for slot in range(slots):
            pieces += [result[slot * HALF : (slot + 1) * HALF], stats[slot : slot + 1], empty]
        out_ref[pl.ds(trip * slots * MESSAGE, slots * MESSAGE)] = jnp.concatenate(pieces, axis=0).astype(jnp.bfloat16)

    trips = q_ref.shape[0] // ROWS
    if trips == 1:
        block(0)
    else:

        def body(trip, unused):
            block(trip)
            return unused

        lax.fori_loop(0, trips, body, 0)


def owned(shape, limit):
    at = lax.broadcasted_iota(jnp.int32, shape, 1)
    head = lax.broadcasted_iota(jnp.int32, shape, 0) // SHARE
    return (at % (2 * KVH) == head) & (at < limit * (2 * KVH))


def suffix_kernel(len_ref, new_ref, q_ref, cache_ref, out_ref, lse_ref):
    q = q_ref[...].reshape(H, HD)
    cache = cache_ref[...]
    new = new_ref[...]
    raw = dot_nt(q, cache)
    scores = jnp.where(owned(raw.shape, len_ref[0]), raw, -jnp.inf)
    new_raw = dot_nt(q, new)
    new_scores = jnp.where(owned(new_raw.shape, 1), new_raw, -jnp.inf)
    best = jnp.maximum(jnp.max(scores, axis=1, keepdims=True), jnp.max(new_scores, axis=1, keepdims=True))
    weight = jnp.exp2((scores - best) * SCALE2).astype(jnp.bfloat16).astype(jnp.float32)
    new_weight = jnp.exp2((new_scores - best) * SCALE2).astype(jnp.bfloat16).astype(jnp.float32)
    total = jnp.sum(weight, axis=1, keepdims=True) + jnp.sum(new_weight, axis=1, keepdims=True)
    moved = pltpu.roll(weight, KVH, 1).astype(jnp.bfloat16)
    new_moved = jnp.concatenate([new_weight[:, KVH:], new_weight[:, :KVH]], axis=1).astype(jnp.bfloat16)
    out_ref[...] = (dot(moved, cache) + dot(new_moved, new)) / total
    lse_ref[...] = jnp.broadcast_to(best * SCALE2 + log2(total), lse_ref.shape)


def fan_kernel(q_hbm, kv_hbm, cache_hbm, out_ref, q_ref, kv_ref, cache_ref, sems, fan_sems):
    pairs = [(q_hbm, q_ref), (cache_hbm, cache_ref), (kv_hbm, kv_ref)]
    loads = [pltpu.make_async_copy(source, target, sems.at[i]) for i, (source, target) in enumerate(pairs)]
    for load in loads:
        load.start()
    loads[0].wait()
    copies = [
        pltpu.make_async_copy(q_ref, out_ref.at[group, :, chip], fan_sems.at[group, chip])
        for group in range(out_ref.shape[0])
        for chip in range(out_ref.shape[2])
    ]
    for copy in copies:
        copy.start()
    for copy in copies + loads[1:]:
        copy.wait()


def merge_kernel(served, part_ref, suffix_ref, lse_ref, out_ref):
    part = part_ref[...].astype(jnp.float32)
    starts = range(0, len(served) * MESSAGE, MESSAGE)
    rows = [part[at : at + HALF] for at in starts]
    sums = unpack_stats([part[at + HALF : at + HALF + 1] for at in starts]).reshape(len(served), HALF, HD)
    blocks = []
    for block in range(H // HALF):
        span = slice(block * HALF, (block + 1) * HALF)
        own = [slot for slot, its in enumerate(served) if its == block]
        own_lse = lse_ref[span]
        best = own_lse
        for slot in own:
            best = jnp.maximum(best, sums[slot])
        total = jnp.exp2(own_lse - best)
        numerator = total * suffix_ref[span]
        for slot in own:
            factor = jnp.exp2(sums[slot] - best)
            total = total + factor
            numerator = numerator + factor * rows[slot]
        blocks.append(numerator / total)
    out_ref[0] = jnp.concatenate(blocks, axis=0).astype(jnp.bfloat16)


def call(kernel, name, outs, operands, specs=None, **cost):
    return pl.pallas_call(
        kernel,
        out_shape=outs,
        in_specs=specs or [VMEM] * len(operands),
        out_specs=jax.tree.map(lambda _: VMEM, outs),
        name=name,
        compiler_params=pltpu.CompilerParams(vmem_limit_bytes=LIMIT),
        cost_estimate=pl.CostEstimate(**cost) if cost else None,
    )(*operands)


def local(queries, prefix_kv, suffix_kv, new_kv, suffix_len):
    groups = lax.axis_size("grp")
    members = lax.axis_size("blk")
    per_head = members // KVH
    devices = groups * members
    span = prefix_kv.shape[2]
    cache_rows = suffix_kv.shape[1] * 2 * KVH
    chips = per_head // CORES
    served = [device % members // per_head * CORES + device % CORES for device in range(devices)]

    def one(rows):
        return jax.ShapeDtypeStruct((rows, HD), jnp.float32)

    def half(*shape):
        return jax.ShapeDtypeStruct((*shape, HD), jnp.bfloat16)

    def exchange(array):
        return lax.all_to_all(array, ("grp", "blk"), 0, 0, tiled=True)

    other = lax.ppermute(prefix_kv, "blk", [(i, i ^ 1) for i in range(members)]).reshape(2, span, HD)
    bound = [
        pltpu.with_memory_space_constraint(array, pltpu.HBM)
        for array in (
            queries.reshape(KVH, SHARE, HD),
            prefix_kv.reshape(2, span, HD),
            suffix_kv.reshape(cache_rows, HD),
        )
    ]
    outgoing, q, kv, cache = pl.pallas_call(
        fan_kernel,
        out_shape=[half(groups, KVH, chips, SHARE), half(KVH, SHARE), half(2, span), half(cache_rows)],
        in_specs=[pl.BlockSpec(memory_space=pltpu.HBM)] * 3,
        out_specs=[pl.BlockSpec(memory_space=pl.ANY), VMEM, VMEM, VMEM],
        scratch_shapes=[pltpu.SemaphoreType.DMA((3,)), pltpu.SemaphoreType.DMA((groups, chips))],
        name="fan",
        compiler_params=pltpu.CompilerParams(vmem_limit_bytes=LIMIT),
    )(*bound)
    arrived = exchange(outgoing.reshape(devices, HALF, HD)).reshape(devices * HALF, HD)
    suffix = call(
        suffix_kernel,
        "suffix",
        [one(H)] * 2,
        (suffix_len, new_kv.reshape(2 * KVH, HD), q, cache),
        [pl.BlockSpec(memory_space=pltpu.SMEM), VMEM, VMEM, VMEM],
        flops=70_000_000,
        bytes_accessed=600_000,
        transcendentals=140_000,
    )
    arrived, suffix = lax.optimization_barrier((arrived, suffix))
    partial = call(
        prefix_kernel,
        "prefix",
        half(devices * MESSAGE),
        (arrived, kv, other),
        flops=12 * devices * HALF * span * HD,
        bytes_accessed=1_600_000,
        transcendentals=2 * devices * HALF * span,
    )
    returned = exchange(partial.reshape(devices, MESSAGE // 2, 2, HD)).reshape(-1, HD)
    return call(
        functools.partial(merge_kernel, served),
        "merge",
        jax.ShapeDtypeStruct((1, H, HD), jnp.bfloat16),
        (returned, *suffix),
    )


def solution(mesh):
    in_specs = (
        P(("grp", "blk"), None, None),
        P(None, "grp", "blk", None),
        P(("grp", "blk"), None, None, None, None),
        P(("grp", "blk"), None, None, None),
        P(("grp", "blk")),
    )
    out_specs = P(("grp", "blk"), None, None)
    return jax.shard_map(local, mesh=mesh, in_specs=in_specs, out_specs=out_specs, check_vma=False)
```

```python
import functools
import math

import jax
import jax.numpy as jnp
from jax import lax
from jax.experimental import pallas as pl
from jax.experimental.pallas import tpu as pltpu
from jax.sharding import PartitionSpec as P

H = 64
KVH = 4
HD = 128
SHARE = H // KVH
SCALE2 = HD ** (-0.5) * math.log2(math.e)
VMEM = pl.BlockSpec(memory_space=pltpu.VMEM)
ROWS = 256
CHUNK = 1024
CORES = 2
HALF = SHARE // CORES
MESSAGE = HALF + 2
LANES = HD // HALF
LIMIT = 24 * 1024 * 1024
NT = (((1,), (1,)), ((), ()))


def dot_nt(a, b):
    return lax.dot_general(a, b, NT, preferred_element_type=jnp.float32)


def dot(a, b):
    return jnp.dot(a, b, preferred_element_type=jnp.float32)


def log2(x):
    return jnp.log(x) * math.log2(math.e)


def compact(x):
    x = x.reshape(-1, HALF, HD)
    mine = lax.broadcasted_iota(jnp.int32, x.shape, 2) // LANES == lax.broadcasted_iota(jnp.int32, x.shape, 1)
    return jnp.sum(jnp.where(mine, x, 0.0), axis=1)


def pieces_of(x):
    hi = x.astype(jnp.bfloat16).astype(jnp.float32)
    rest = x - hi
    mid = rest.astype(jnp.bfloat16).astype(jnp.float32)
    low = rest - mid
    lane = lax.broadcasted_iota(jnp.int32, x.shape, 1) % LANES
    return jnp.where(lane == 0, hi, jnp.where(lane == 1, mid, jnp.where(lane == 2, low, 0.0)))


def unpack_stats(rows):
    shape = (HALF, HD)
    mine = lax.broadcasted_iota(jnp.int32, shape, 1) // LANES == lax.broadcasted_iota(jnp.int32, shape, 0)
    pieces = [jnp.where(mine, jnp.broadcast_to(row, shape), 0.0) for row in rows]
    return dot(jnp.concatenate(pieces, axis=0).astype(jnp.bfloat16), jnp.ones((HD, HD), jnp.bfloat16))


def prefix_kernel(q_ref, kv_ref, other_ref, out_ref):
    chunks = [(ref, at) for ref in (other_ref, kv_ref) for at in range(0, ref.shape[1], CHUNK)]

    def block(trip):
        rows = q_ref[pl.ds(trip * ROWS, ROWS)]

        def score(ref, first):
            return dot_nt(rows, ref[0, first : first + CHUNK])

        parts = []
        ahead = score(*chunks[0])
        for index, (ref, first) in enumerate(chunks):
            scores = ahead
            if index + 1 < len(chunks):
                ahead = score(*chunks[index + 1])
            best = jnp.max(scores, axis=1, keepdims=True)
            weight = jnp.exp2((scores - best) * SCALE2).astype(jnp.bfloat16)
            values = ref[1, first : first + CHUNK]
            parts.append((best, dot(weight, jnp.concatenate([values, jnp.ones_like(values)], axis=1))))
        best = functools.reduce(jnp.maximum, [part[0] for part in parts])
        both = sum(jnp.exp2((its - best) * SCALE2) * sums for its, sums in parts)
        total = both[:, HD:]
        result = both[:, :HD] / total
        slots = ROWS // HALF
        best = jnp.broadcast_to(best, total.shape)
        stats = pieces_of(compact(best) * SCALE2 + log2(compact(total)))
        empty = jnp.zeros((1, HD), jnp.float32)
        pieces = []
        for slot in range(slots):
            pieces += [result[slot * HALF : (slot + 1) * HALF], stats[slot : slot + 1], empty]
        out_ref[pl.ds(trip * slots * MESSAGE, slots * MESSAGE)] = jnp.concatenate(pieces, axis=0).astype(jnp.bfloat16)

    trips = q_ref.shape[0] // ROWS
    if trips == 1:
        block(0)
    else:

        def body(trip, unused):
            block(trip)
            return unused

        lax.fori_loop(0, trips, body, 0)


def owned(shape, limit):
    at = lax.broadcasted_iota(jnp.int32, shape, 1)
    head = lax.broadcasted_iota(jnp.int32, shape, 0) // SHARE
    return (at % (2 * KVH) == head) & (at < limit * (2 * KVH))


def suffix_kernel(len_ref, new_ref, q_ref, cache_ref, out_ref, lse_ref):
    q = q_ref[...].reshape(H, HD)
    cache = cache_ref[...]
    new = new_ref[...]
    raw = dot_nt(q, cache)
    scores = jnp.where(owned(raw.shape, len_ref[0]), raw, -jnp.inf)
    new_raw = dot_nt(q, new)
    new_scores = jnp.where(owned(new_raw.shape, 1), new_raw, -jnp.inf)
    best = jnp.maximum(jnp.max(scores, axis=1, keepdims=True), jnp.max(new_scores, axis=1, keepdims=True))
    weight = jnp.exp2((scores - best) * SCALE2).astype(jnp.bfloat16).astype(jnp.float32)
    new_weight = jnp.exp2((new_scores - best) * SCALE2).astype(jnp.bfloat16).astype(jnp.float32)
    total = jnp.sum(weight, axis=1, keepdims=True) + jnp.sum(new_weight, axis=1, keepdims=True)
    moved = pltpu.roll(weight, KVH, 1).astype(jnp.bfloat16)
    new_moved = jnp.concatenate([new_weight[:, KVH:], new_weight[:, :KVH]], axis=1).astype(jnp.bfloat16)
    out_ref[...] = (dot(moved, cache) + dot(new_moved, new)) / total
    lse_ref[...] = jnp.broadcast_to(best * SCALE2 + log2(total), lse_ref.shape)


def fan_kernel(q_hbm, kv_hbm, cache_hbm, out_ref, q_ref, kv_ref, cache_ref, sems, fan_sems):
    pairs = [(q_hbm, q_ref), (cache_hbm, cache_ref), (kv_hbm, kv_ref)]
    loads = [pltpu.make_async_copy(source, target, sems.at[i]) for i, (source, target) in enumerate(pairs)]
    for load in loads:
        load.start()
    loads[0].wait()
    copies = [
        pltpu.make_async_copy(q_ref, out_ref.at[group, :, chip], fan_sems.at[group, chip])
        for group in range(out_ref.shape[0])
        for chip in range(out_ref.shape[2])
    ]
    for copy in copies:
        copy.start()
    for copy in copies + loads[1:]:
        copy.wait()


def merge_kernel(served, part_ref, suffix_ref, lse_ref, out_ref):
    part = part_ref[...].astype(jnp.float32)
    starts = range(0, len(served) * MESSAGE, MESSAGE)
    rows = [part[at : at + HALF] for at in starts]
    sums = unpack_stats([part[at + HALF : at + HALF + 1] for at in starts]).reshape(len(served), HALF, HD)
    blocks = []
    for block in range(H // HALF):
        span = slice(block * HALF, (block + 1) * HALF)
        own = [slot for slot, its in enumerate(served) if its == block]
        own_lse = lse_ref[span]
        best = own_lse
        for slot in own:
            best = jnp.maximum(best, sums[slot])
        total = jnp.exp2(own_lse - best)
        numerator = total * suffix_ref[span]
        for slot in own:
            factor = jnp.exp2(sums[slot] - best)
            total = total + factor
            numerator = numerator + factor * rows[slot]
        blocks.append(numerator / total)
    out_ref[0] = jnp.concatenate(blocks, axis=0).astype(jnp.bfloat16)


def call(kernel, name, outs, operands, specs=None, **cost):
    return pl.pallas_call(
        kernel,
        out_shape=outs,
        in_specs=specs or [VMEM] * len(operands),
        out_specs=jax.tree.map(lambda _: VMEM, outs),
        name=name,
        compiler_params=pltpu.CompilerParams(vmem_limit_bytes=LIMIT),
        cost_estimate=pl.CostEstimate(**cost) if cost else None,
    )(*operands)


def local(queries, prefix_kv, suffix_kv, new_kv, suffix_len):
    groups = lax.axis_size("grp")
    members = lax.axis_size("blk")
    per_head = members // KVH
    devices = groups * members
    span = prefix_kv.shape[2]
    cache_rows = suffix_kv.shape[1] * 2 * KVH
    chips = per_head // CORES
    served = [device % members // per_head * CORES + device % CORES for device in range(devices)]

    def one(rows):
        return jax.ShapeDtypeStruct((rows, HD), jnp.float32)

    def half(*shape):
        return jax.ShapeDtypeStruct((*shape, HD), jnp.bfloat16)

    def exchange(array):
        return lax.all_to_all(array, ("grp", "blk"), 0, 0, tiled=True)

    other = lax.ppermute(prefix_kv, "blk", [(i, i ^ 1) for i in range(members)]).reshape(2, span, HD)
    bound = [
        pltpu.with_memory_space_constraint(array, pltpu.HBM)
        for array in (
            queries.reshape(KVH, SHARE, HD),
            prefix_kv.reshape(2, span, HD),
            suffix_kv.reshape(cache_rows, HD),
        )
    ]
    outgoing, q, kv, cache = pl.pallas_call(
        fan_kernel,
        out_shape=[half(groups, KVH, chips, SHARE), half(KVH, SHARE), half(2, span), half(cache_rows)],
        in_specs=[pl.BlockSpec(memory_space=pltpu.HBM)] * 3,
        out_specs=[pl.BlockSpec(memory_space=pl.ANY), VMEM, VMEM, VMEM],
        scratch_shapes=[pltpu.SemaphoreType.DMA((3,)), pltpu.SemaphoreType.DMA((groups, chips))],
        name="fan",
        compiler_params=pltpu.CompilerParams(vmem_limit_bytes=LIMIT),
    )(*bound)
    arrived = exchange(outgoing.reshape(devices, HALF, HD)).reshape(devices * HALF, HD)
    suffix = call(
        suffix_kernel,
        "suffix",
        [one(H)] * 2,
        (suffix_len, new_kv.reshape(2 * KVH, HD), q, cache),
        [pl.BlockSpec(memory_space=pltpu.SMEM), VMEM, VMEM, VMEM],
        flops=70_000_000,
        bytes_accessed=600_000,
        transcendentals=140_000,
    )
    arrived, suffix = lax.optimization_barrier((arrived, suffix))
    partial = call(
        prefix_kernel,
        "prefix",
        half(devices * MESSAGE),
        (arrived, kv, other),
        flops=12 * devices * HALF * span * HD,
        bytes_accessed=1_600_000,
        transcendentals=2 * devices * HALF * span,
    )
    returned = exchange(partial.reshape(devices, MESSAGE // 2, 2, HD)).reshape(-1, HD)
    return call(
        functools.partial(merge_kernel, served),
        "merge",
        jax.ShapeDtypeStruct((1, H, HD), jnp.bfloat16),
        (returned, *suffix),
    )


def solution(mesh):
    in_specs = (
        P(("grp", "blk"), None, None),
        P(None, "grp", "blk", None),
        P(("grp", "blk"), None, None, None, None),
        P(("grp", "blk"), None, None, None),
        P(("grp", "blk")),
    )
    out_specs = P(("grp", "blk"), None, None)
    return jax.shard_map(local, mesh=mesh, in_specs=in_specs, out_specs=out_specs, check_vma=False)
```

```python
import functools
import math

import jax
import jax.numpy as jnp
from jax import lax
from jax.experimental import pallas as pl
from jax.experimental.pallas import tpu as pltpu
from jax.sharding import PartitionSpec as P

H = 64
KVH = 4
HD = 128
SHARE = H // KVH
SCALE2 = HD ** (-0.5) * math.log2(math.e)
VMEM = pl.BlockSpec(memory_space=pltpu.VMEM)
ROWS = 256
CHUNK = 512
CORES = 2
HALF = SHARE // CORES
MESSAGE = HALF + 2
LANES = HD // HALF
LIMIT = 24 * 1024 * 1024
NT = (((1,), (1,)), ((), ()))


def dot_nt(a, b):
    return lax.dot_general(a, b, NT, preferred_element_type=jnp.float32)


def dot(a, b):
    return jnp.dot(a, b, preferred_element_type=jnp.float32)


def log2(x):
    return jnp.log(x) * math.log2(math.e)


def compact(x):
    x = x.reshape(-1, HALF, HD)
    mine = lax.broadcasted_iota(jnp.int32, x.shape, 2) // LANES == lax.broadcasted_iota(jnp.int32, x.shape, 1)
    return jnp.sum(jnp.where(mine, x, 0.0), axis=1)


def pieces_of(x):
    hi = x.astype(jnp.bfloat16).astype(jnp.float32)
    rest = x - hi
    mid = rest.astype(jnp.bfloat16).astype(jnp.float32)
    low = rest - mid
    lane = lax.broadcasted_iota(jnp.int32, x.shape, 1) % LANES
    return jnp.where(lane == 0, hi, jnp.where(lane == 1, mid, jnp.where(lane == 2, low, 0.0)))


def unpack_stats(rows):
    shape = (HALF, HD)
    mine = lax.broadcasted_iota(jnp.int32, shape, 1) // LANES == lax.broadcasted_iota(jnp.int32, shape, 0)
    pieces = [jnp.where(mine, jnp.broadcast_to(row, shape), 0.0) for row in rows]
    return dot(jnp.concatenate(pieces, axis=0).astype(jnp.bfloat16), jnp.ones((HD, HD), jnp.bfloat16))


def prefix_kernel(q_ref, kv_ref, other_ref, out_ref):
    chunks = [(ref, at) for ref in (other_ref, kv_ref) for at in range(0, ref.shape[1], CHUNK)]

    def block(trip):
        rows = q_ref[pl.ds(trip * ROWS, ROWS)]

        def score(ref, first):
            return dot_nt(rows, ref[0, first : first + CHUNK])

        parts = []
        ahead = score(*chunks[0])
        for index, (ref, first) in enumerate(chunks):
            scores = ahead
            if index + 1 < len(chunks):
                ahead = score(*chunks[index + 1])
            best = jnp.max(scores, axis=1, keepdims=True)
            weight = jnp.exp2((scores - best) * SCALE2).astype(jnp.bfloat16)
            values = ref[1, first : first + CHUNK]
            parts.append((best, dot(weight, jnp.concatenate([values, jnp.ones_like(values)], axis=1))))
        best = functools.reduce(jnp.maximum, [part[0] for part in parts])
        both = sum(jnp.exp2((its - best) * SCALE2) * sums for its, sums in parts)
        total = both[:, HD:]
        result = both[:, :HD] / total
        slots = ROWS // HALF
        best = jnp.broadcast_to(best, total.shape)
        stats = pieces_of(compact(best) * SCALE2 + log2(compact(total)))
        empty = jnp.zeros((1, HD), jnp.float32)
        pieces = []
        for slot in range(slots):
            pieces += [result[slot * HALF : (slot + 1) * HALF], stats[slot : slot + 1], empty]
        out_ref[pl.ds(trip * slots * MESSAGE, slots * MESSAGE)] = jnp.concatenate(pieces, axis=0).astype(jnp.bfloat16)

    trips = q_ref.shape[0] // ROWS
    if trips == 1:
        block(0)
    else:

        def body(trip, unused):
            block(trip)
            return unused

        lax.fori_loop(0, trips, body, 0)


def owned(shape, limit):
    at = lax.broadcasted_iota(jnp.int32, shape, 1)
    head = lax.broadcasted_iota(jnp.int32, shape, 0) // SHARE
    return (at % (2 * KVH) == head) & (at < limit * (2 * KVH))


def suffix_kernel(len_ref, new_ref, q_ref, cache_ref, out_ref, lse_ref):
    q = q_ref[...].reshape(H, HD)
    cache = cache_ref[...]
    new = new_ref[...]
    raw = dot_nt(q, cache)
    scores = jnp.where(owned(raw.shape, len_ref[0]), raw, -jnp.inf)
    new_raw = dot_nt(q, new)
    new_scores = jnp.where(owned(new_raw.shape, 1), new_raw, -jnp.inf)
    best = jnp.maximum(jnp.max(scores, axis=1, keepdims=True), jnp.max(new_scores, axis=1, keepdims=True))
    weight = jnp.exp2((scores - best) * SCALE2).astype(jnp.bfloat16).astype(jnp.float32)
    new_weight = jnp.exp2((new_scores - best) * SCALE2).astype(jnp.bfloat16).astype(jnp.float32)
    total = jnp.sum(weight, axis=1, keepdims=True) + jnp.sum(new_weight, axis=1, keepdims=True)
    moved = pltpu.roll(weight, KVH, 1).astype(jnp.bfloat16)
    new_moved = jnp.concatenate([new_weight[:, KVH:], new_weight[:, :KVH]], axis=1).astype(jnp.bfloat16)
    out_ref[...] = (dot(moved, cache) + dot(new_moved, new)) / total
    lse_ref[...] = jnp.broadcast_to(best * SCALE2 + log2(total), lse_ref.shape)


def fan_kernel(q_hbm, kv_hbm, cache_hbm, out_ref, q_ref, kv_ref, cache_ref, sems, fan_sems):
    pairs = [(q_hbm, q_ref), (cache_hbm, cache_ref), (kv_hbm, kv_ref)]
    loads = [pltpu.make_async_copy(source, target, sems.at[i]) for i, (source, target) in enumerate(pairs)]
    for load in loads:
        load.start()
    loads[0].wait()
    copies = [
        pltpu.make_async_copy(q_ref, out_ref.at[group, :, chip], fan_sems.at[group, chip])
        for group in range(out_ref.shape[0])
        for chip in range(out_ref.shape[2])
    ]
    for copy in copies:
        copy.start()
    for copy in copies + loads[1:]:
        copy.wait()


def merge_kernel(served, part_ref, suffix_ref, lse_ref, out_ref):
    part = part_ref[...].astype(jnp.float32)
    starts = range(0, len(served) * MESSAGE, MESSAGE)
    rows = [part[at : at + HALF] for at in starts]
    sums = unpack_stats([part[at + HALF : at + HALF + 1] for at in starts]).reshape(len(served), HALF, HD)
    blocks = []
    for block in range(H // HALF):
        span = slice(block * HALF, (block + 1) * HALF)
        own = [slot for slot, its in enumerate(served) if its == block]
        own_lse = lse_ref[span]
        best = own_lse
        for slot in own:
            best = jnp.maximum(best, sums[slot])
        total = jnp.exp2(own_lse - best)
        numerator = total * suffix_ref[span]
        for slot in own:
            factor = jnp.exp2(sums[slot] - best)
            total = total + factor
            numerator = numerator + factor * rows[slot]
        blocks.append(numerator / total)
    out_ref[0] = jnp.concatenate(blocks, axis=0).astype(jnp.bfloat16)


def call(kernel, name, outs, operands, specs=None, **cost):
    return pl.pallas_call(
        kernel,
        out_shape=outs,
        in_specs=specs or [VMEM] * len(operands),
        out_specs=jax.tree.map(lambda _: VMEM, outs),
        name=name,
        compiler_params=pltpu.CompilerParams(vmem_limit_bytes=LIMIT),
        cost_estimate=pl.CostEstimate(**cost) if cost else None,
    )(*operands)


def local(queries, prefix_kv, suffix_kv, new_kv, suffix_len):
    groups = lax.axis_size("grp")
    members = lax.axis_size("blk")
    per_head = members // KVH
    devices = groups * members
    span = prefix_kv.shape[2]
    cache_rows = suffix_kv.shape[1] * 2 * KVH
    chips = per_head // CORES
    served = [device % members // per_head * CORES + device % CORES for device in range(devices)]

    def one(rows):
        return jax.ShapeDtypeStruct((rows, HD), jnp.float32)

    def half(*shape):
        return jax.ShapeDtypeStruct((*shape, HD), jnp.bfloat16)

    def exchange(array):
        return lax.all_to_all(array, ("grp", "blk"), 0, 0, tiled=True)

    other = lax.ppermute(prefix_kv, "blk", [(i, i ^ 1) for i in range(members)]).reshape(2, span, HD)
    bound = [
        pltpu.with_memory_space_constraint(array, pltpu.HBM)
        for array in (
            queries.reshape(KVH, SHARE, HD),
            prefix_kv.reshape(2, span, HD),
            suffix_kv.reshape(cache_rows, HD),
        )
    ]
    outgoing, q, kv, cache = pl.pallas_call(
        fan_kernel,
        out_shape=[half(groups, KVH, chips, SHARE), half(KVH, SHARE), half(2, span), half(cache_rows)],
        in_specs=[pl.BlockSpec(memory_space=pltpu.HBM)] * 3,
        out_specs=[pl.BlockSpec(memory_space=pl.ANY), VMEM, VMEM, VMEM],
        scratch_shapes=[pltpu.SemaphoreType.DMA((3,)), pltpu.SemaphoreType.DMA((groups, chips))],
        name="fan",
        compiler_params=pltpu.CompilerParams(vmem_limit_bytes=LIMIT),
    )(*bound)
    arrived = exchange(outgoing.reshape(devices, HALF, HD)).reshape(devices * HALF, HD)
    suffix = call(
        suffix_kernel,
        "suffix",
        [one(H)] * 2,
        (suffix_len, new_kv.reshape(2 * KVH, HD), q, cache),
        [pl.BlockSpec(memory_space=pltpu.SMEM), VMEM, VMEM, VMEM],
        flops=70_000_000,
        bytes_accessed=600_000,
        transcendentals=140_000,
    )
    arrived, suffix = lax.optimization_barrier((arrived, suffix))
    partial = call(
        prefix_kernel,
        "prefix",
        half(devices * MESSAGE),
        (arrived, kv, other),
        flops=12 * devices * HALF * span * HD,
        bytes_accessed=1_600_000,
        transcendentals=2 * devices * HALF * span,
    )
    returned = exchange(partial.reshape(devices, MESSAGE // 2, 2, HD)).reshape(-1, HD)
    return call(
        functools.partial(merge_kernel, served),
        "merge",
        jax.ShapeDtypeStruct((1, H, HD), jnp.bfloat16),
        (returned, *suffix),
    )


def solution(mesh):
    in_specs = (
        P(("grp", "blk"), None, None),
        P(None, "grp", "blk", None),
        P(("grp", "blk"), None, None, None, None),
        P(("grp", "blk"), None, None, None),
        P(("grp", "blk")),
    )
    out_specs = P(("grp", "blk"), None, None)
    return jax.shard_map(local, mesh=mesh, in_specs=in_specs, out_specs=out_specs, check_vma=False)
```

```python
import functools
import math

import jax
import jax.numpy as jnp
from jax import lax
from jax.experimental import pallas as pl
from jax.experimental.pallas import tpu as pltpu
from jax.sharding import PartitionSpec as P

H = 64
KVH = 4
HD = 128
SHARE = H // KVH
SCALE2 = HD ** (-0.5) * math.log2(math.e)
VMEM = pl.BlockSpec(memory_space=pltpu.VMEM)
ROWS = 256
CHUNK = 256
AHEAD = 2
CORES = 2
HALF = SHARE // CORES
MESSAGE = HALF + 2
LANES = HD // HALF
LIMIT = 24 * 1024 * 1024
NT = (((1,), (1,)), ((), ()))


def dot_nt(a, b):
    return lax.dot_general(a, b, NT, preferred_element_type=jnp.float32)


def dot(a, b):
    return jnp.dot(a, b, preferred_element_type=jnp.float32)


def log2(x):
    return jnp.log(x) * math.log2(math.e)


def pack_stats(x):
    hi = x.astype(jnp.bfloat16).astype(jnp.float32)
    rest = x - hi
    mid = rest.astype(jnp.bfloat16).astype(jnp.float32)
    low = rest - mid
    row = lax.broadcasted_iota(jnp.int32, x.shape, 1)
    lane = lax.broadcasted_iota(jnp.int32, x.shape, 2) - row * LANES
    return jnp.sum(jnp.where(lane == 0, hi, jnp.where(lane == 1, mid, jnp.where(lane == 2, low, 0.0))), axis=1)


def unpack_stats(rows):
    shape = (HALF, HD)
    mine = lax.broadcasted_iota(jnp.int32, shape, 1) // LANES == lax.broadcasted_iota(jnp.int32, shape, 0)
    pieces = [jnp.where(mine, jnp.broadcast_to(row, shape), 0.0) for row in rows]
    return dot(jnp.concatenate(pieces, axis=0).astype(jnp.bfloat16), jnp.ones((HD, HD), jnp.bfloat16))


def prefix_kernel(q_ref, kv_ref, other_ref, out_ref):
    chunks = [(ref, at) for ref in (other_ref, kv_ref) for at in range(0, ref.shape[1], CHUNK)]

    def block(trip):
        rows = q_ref[pl.ds(trip * ROWS, ROWS)]

        def score(ref, first):
            return dot_nt(rows, ref[0, first : first + CHUNK])

        parts = []
        ahead = [score(*chunk) for chunk in chunks[:AHEAD]]
        for index, (ref, first) in enumerate(chunks):
            if index + AHEAD < len(chunks):
                ahead.append(score(*chunks[index + AHEAD]))
            scores = ahead.pop(0)
            best = jnp.max(scores, axis=1, keepdims=True)
            weight = jnp.exp2((scores - best) * SCALE2).astype(jnp.bfloat16)
            values = ref[1, first : first + CHUNK]
            parts.append((best, dot(weight, jnp.concatenate([values, jnp.ones_like(values)], axis=1))))
        best = functools.reduce(jnp.maximum, [part[0] for part in parts])
        both = sum(jnp.exp2((its - best) * SCALE2) * sums for its, sums in parts)
        total = both[:, HD:]
        result = both[:, :HD] / total
        slots = ROWS // HALF
        stats = pack_stats((best * SCALE2 + log2(total)).reshape(slots, HALF, HD))
        empty = jnp.zeros((1, HD), jnp.float32)
        pieces = []
        for slot in range(slots):
            pieces += [result[slot * HALF : (slot + 1) * HALF], stats[slot : slot + 1], empty]
        out_ref[pl.ds(trip * slots * MESSAGE, slots * MESSAGE)] = jnp.concatenate(pieces, axis=0).astype(jnp.bfloat16)

    trips = q_ref.shape[0] // ROWS
    if trips == 1:
        block(0)
    else:

        def body(trip, unused):
            block(trip)
            return unused

        lax.fori_loop(0, trips, body, 0)


def owned(shape, limit):
    at = lax.broadcasted_iota(jnp.int32, shape, 1)
    head = lax.broadcasted_iota(jnp.int32, shape, 0) // SHARE
    return (at % (2 * KVH) == head) & (at < limit * (2 * KVH))


def suffix_kernel(len_ref, new_ref, q_ref, cache_ref, out_ref, lse_ref):
    q = q_ref[...].reshape(H, HD)
    cache = cache_ref[...]
    new = new_ref[...]
    raw = dot_nt(q, cache)
    scores = jnp.where(owned(raw.shape, len_ref[0]), raw, -jnp.inf)
    new_raw = dot_nt(q, new)
    new_scores = jnp.where(owned(new_raw.shape, 1), new_raw, -jnp.inf)
    best = jnp.maximum(jnp.max(scores, axis=1, keepdims=True), jnp.max(new_scores, axis=1, keepdims=True))
    weight = jnp.exp2((scores - best) * SCALE2).astype(jnp.bfloat16).astype(jnp.float32)
    new_weight = jnp.exp2((new_scores - best) * SCALE2).astype(jnp.bfloat16).astype(jnp.float32)
    total = jnp.sum(weight, axis=1, keepdims=True) + jnp.sum(new_weight, axis=1, keepdims=True)
    moved = pltpu.roll(weight, KVH, 1).astype(jnp.bfloat16)
    new_moved = jnp.concatenate([new_weight[:, KVH:], new_weight[:, :KVH]], axis=1).astype(jnp.bfloat16)
    out_ref[...] = (dot(moved, cache) + dot(new_moved, new)) / total
    lse_ref[...] = jnp.broadcast_to(best * SCALE2 + log2(total), lse_ref.shape)


def fan_kernel(q_hbm, kv_hbm, cache_hbm, out_ref, q_ref, kv_ref, cache_ref, sems, fan_sems):
    pairs = [(q_hbm, q_ref), (cache_hbm, cache_ref), (kv_hbm, kv_ref)]
    loads = [pltpu.make_async_copy(source, target, sems.at[i]) for i, (source, target) in enumerate(pairs)]
    for load in loads:
        load.start()
    loads[0].wait()
    copies = [
        pltpu.make_async_copy(q_ref, out_ref.at[group, :, chip], fan_sems.at[group, chip])
        for group in range(out_ref.shape[0])
        for chip in range(out_ref.shape[2])
    ]
    for copy in copies:
        copy.start()
    for copy in copies + loads[1:]:
        copy.wait()


def merge_kernel(served, part_ref, suffix_ref, lse_ref, out_ref):
    part = part_ref[...].astype(jnp.float32)
    starts = range(0, len(served) * MESSAGE, MESSAGE)
    rows = [part[at : at + HALF] for at in starts]
    sums = unpack_stats([part[at + HALF : at + HALF + 1] for at in starts]).reshape(len(served), HALF, HD)
    blocks = []
    for block in range(H // HALF):
        span = slice(block * HALF, (block + 1) * HALF)
        own = [slot for slot, its in enumerate(served) if its == block]
        own_lse = lse_ref[span]
        best = own_lse
        for slot in own:
            best = jnp.maximum(best, sums[slot])
        total = jnp.exp2(own_lse - best)
        numerator = total * suffix_ref[span]
        for slot in own:
            factor = jnp.exp2(sums[slot] - best)
            total = total + factor
            numerator = numerator + factor * rows[slot]
        blocks.append(numerator / total)
    out_ref[0] = jnp.concatenate(blocks, axis=0).astype(jnp.bfloat16)


def call(kernel, name, outs, operands, specs=None, **cost):
    return pl.pallas_call(
        kernel,
        out_shape=outs,
        in_specs=specs or [VMEM] * len(operands),
        out_specs=jax.tree.map(lambda _: VMEM, outs),
        name=name,
        compiler_params=pltpu.CompilerParams(vmem_limit_bytes=LIMIT),
        cost_estimate=pl.CostEstimate(**cost) if cost else None,
    )(*operands)


def local(queries, prefix_kv, suffix_kv, new_kv, suffix_len):
    groups = lax.axis_size("grp")
    members = lax.axis_size("blk")
    per_head = members // KVH
    devices = groups * members
    span = prefix_kv.shape[2]
    cache_rows = suffix_kv.shape[1] * 2 * KVH
    chips = per_head // CORES
    served = [device % members // per_head * CORES + device % CORES for device in range(devices)]

    def one(rows):
        return jax.ShapeDtypeStruct((rows, HD), jnp.float32)

    def half(*shape):
        return jax.ShapeDtypeStruct((*shape, HD), jnp.bfloat16)

    def exchange(array):
        return lax.all_to_all(array, ("grp", "blk"), 0, 0, tiled=True)

    other = lax.ppermute(prefix_kv, "blk", [(i, i ^ 1) for i in range(members)]).reshape(2, span, HD)
    bound = [
        pltpu.with_memory_space_constraint(array, pltpu.HBM)
        for array in (
            queries.reshape(KVH, SHARE, HD),
            prefix_kv.reshape(2, span, HD),
            suffix_kv.reshape(cache_rows, HD),
        )
    ]
    outgoing, q, kv, cache = pl.pallas_call(
        fan_kernel,
        out_shape=[half(groups, KVH, chips, SHARE), half(KVH, SHARE), half(2, span), half(cache_rows)],
        in_specs=[pl.BlockSpec(memory_space=pltpu.HBM)] * 3,
        out_specs=[pl.BlockSpec(memory_space=pl.ANY), VMEM, VMEM, VMEM],
        scratch_shapes=[pltpu.SemaphoreType.DMA((3,)), pltpu.SemaphoreType.DMA((groups, chips))],
        name="fan",
        compiler_params=pltpu.CompilerParams(vmem_limit_bytes=LIMIT),
    )(*bound)
    arrived = exchange(outgoing.reshape(devices, HALF, HD)).reshape(devices * HALF, HD)
    suffix = call(
        suffix_kernel,
        "suffix",
        [one(H)] * 2,
        (suffix_len, new_kv.reshape(2 * KVH, HD), q, cache),
        [pl.BlockSpec(memory_space=pltpu.SMEM), VMEM, VMEM, VMEM],
        flops=70_000_000,
        bytes_accessed=600_000,
        transcendentals=140_000,
    )
    arrived, suffix = lax.optimization_barrier((arrived, suffix))
    partial = call(
        prefix_kernel,
        "prefix",
        half(devices * MESSAGE),
        (arrived, kv, other),
        flops=12 * devices * HALF * span * HD,
        bytes_accessed=1_600_000,
        transcendentals=2 * devices * HALF * span,
    )
    returned = exchange(partial.reshape(devices, MESSAGE // 2, 2, HD)).reshape(-1, HD)
    return call(
        functools.partial(merge_kernel, served),
        "merge",
        jax.ShapeDtypeStruct((1, H, HD), jnp.bfloat16),
        (returned, *suffix),
    )


def solution(mesh):
    in_specs = (
        P(("grp", "blk"), None, None),
        P(None, "grp", "blk", None),
        P(("grp", "blk"), None, None, None, None),
        P(("grp", "blk"), None, None, None),
        P(("grp", "blk")),
    )
    out_specs = P(("grp", "blk"), None, None)
    return jax.shard_map(local, mesh=mesh, in_specs=in_specs, out_specs=out_specs, check_vma=False)
```

```python
import functools
import math

import jax
import jax.numpy as jnp
from jax import lax
from jax.experimental import pallas as pl
from jax.experimental.pallas import tpu as pltpu
from jax.sharding import PartitionSpec as P

H = 64
KVH = 4
HD = 128
SHARE = H // KVH
SCALE2 = HD ** (-0.5) * math.log2(math.e)
VMEM = pl.BlockSpec(memory_space=pltpu.VMEM)
ROWS = 256
CHUNK = 512
CORES = 2
HALF = SHARE // CORES
MESSAGE = HALF + 2
LANES = HD // HALF
LIMIT = 24 * 1024 * 1024
NT = (((1,), (1,)), ((), ()))


def dot_nt(a, b):
    return lax.dot_general(a, b, NT, preferred_element_type=jnp.float32)


def dot(a, b):
    return jnp.dot(a, b, preferred_element_type=jnp.float32)


def log2(x):
    return jnp.log(x) * math.log2(math.e)


def pack_stats(x):
    hi = x.astype(jnp.bfloat16).astype(jnp.float32)
    rest = x - hi
    mid = rest.astype(jnp.bfloat16).astype(jnp.float32)
    low = rest - mid
    row = lax.broadcasted_iota(jnp.int32, x.shape, 1)
    lane = lax.broadcasted_iota(jnp.int32, x.shape, 2) - row * LANES
    return jnp.sum(jnp.where(lane == 0, hi, jnp.where(lane == 1, mid, jnp.where(lane == 2, low, 0.0))), axis=1)


def unpack_stats(rows):
    shape = (HALF, HD)
    mine = lax.broadcasted_iota(jnp.int32, shape, 1) // LANES == lax.broadcasted_iota(jnp.int32, shape, 0)
    pieces = [jnp.where(mine, jnp.broadcast_to(row, shape), 0.0) for row in rows]
    return dot(jnp.concatenate(pieces, axis=0).astype(jnp.bfloat16), jnp.ones((HD, HD), jnp.bfloat16))


def prefix_kernel(q_ref, kv_ref, other_ref, out_ref):
    chunks = [(ref, at) for ref in (other_ref, kv_ref) for at in range(0, ref.shape[1], CHUNK)]

    def block(trip):
        rows = q_ref[pl.ds(trip * ROWS, ROWS)]

        def score(ref, first):
            return dot_nt(rows, ref[0, first : first + CHUNK])

        parts = []
        ahead = score(*chunks[0])
        for index, (ref, first) in enumerate(chunks):
            scores = ahead
            if index + 1 < len(chunks):
                ahead = score(*chunks[index + 1])
            best = jnp.max(scores, axis=1, keepdims=True)
            weight = jnp.exp2((scores - best) * SCALE2).astype(jnp.bfloat16)
            values = ref[1, first : first + CHUNK]
            parts.append((best, dot(weight, jnp.concatenate([values, jnp.ones_like(values)], axis=1))))
        best = functools.reduce(jnp.maximum, [part[0] for part in parts])
        both = sum(jnp.exp2((its - best) * SCALE2) * sums for its, sums in parts)
        total = both[:, HD:]
        result = both[:, :HD] / total
        slots = ROWS // HALF
        stats = pack_stats((best * SCALE2 + log2(total)).reshape(slots, HALF, HD))
        empty = jnp.zeros((1, HD), jnp.float32)
        pieces = []
        for slot in range(slots):
            pieces += [result[slot * HALF : (slot + 1) * HALF], stats[slot : slot + 1], empty]
        out_ref[pl.ds(trip * slots * MESSAGE, slots * MESSAGE)] = jnp.concatenate(pieces, axis=0).astype(jnp.bfloat16)

    trips = q_ref.shape[0] // ROWS
    if trips == 1:
        block(0)
    else:

        def body(trip, unused):
            block(trip)
            return unused

        lax.fori_loop(0, trips, body, 0)


def owned(shape, limit):
    at = lax.broadcasted_iota(jnp.int32, shape, 1)
    head = lax.broadcasted_iota(jnp.int32, shape, 0) // SHARE
    return (at % (2 * KVH) == head) & (at < limit * (2 * KVH))


def suffix_kernel(len_ref, new_ref, q_ref, cache_ref, out_ref, lse_ref):
    q = q_ref[...].reshape(H, HD)
    cache = cache_ref[...]
    new = new_ref[...]
    raw = dot_nt(q, cache)
    scores = jnp.where(owned(raw.shape, len_ref[0]), raw, -jnp.inf)
    new_raw = dot_nt(q, new)
    new_scores = jnp.where(owned(new_raw.shape, 1), new_raw, -jnp.inf)
    best = jnp.maximum(jnp.max(scores, axis=1, keepdims=True), jnp.max(new_scores, axis=1, keepdims=True))
    weight = jnp.exp2((scores - best) * SCALE2).astype(jnp.bfloat16).astype(jnp.float32)
    new_weight = jnp.exp2((new_scores - best) * SCALE2).astype(jnp.bfloat16).astype(jnp.float32)
    total = jnp.sum(weight, axis=1, keepdims=True) + jnp.sum(new_weight, axis=1, keepdims=True)
    moved = pltpu.roll(weight, KVH, 1).astype(jnp.bfloat16)
    new_moved = jnp.concatenate([new_weight[:, KVH:], new_weight[:, :KVH]], axis=1).astype(jnp.bfloat16)
    out_ref[...] = (dot(moved, cache) + dot(new_moved, new)) / total
    lse_ref[...] = jnp.broadcast_to(best * SCALE2 + log2(total), lse_ref.shape)


def fan_kernel(q_hbm, kv_hbm, cache_hbm, out_ref, q_ref, kv_ref, cache_ref, sems, fan_sems):
    pairs = [(q_hbm, q_ref), (cache_hbm, cache_ref), (kv_hbm, kv_ref)]
    loads = [pltpu.make_async_copy(source, target, sems.at[i]) for i, (source, target) in enumerate(pairs)]
    for load in loads:
        load.start()
    loads[0].wait()
    copies = [
        pltpu.make_async_copy(q_ref, out_ref.at[group, :, chip], fan_sems.at[group, chip])
        for group in range(out_ref.shape[0])
        for chip in range(out_ref.shape[2])
    ]
    for copy in copies:
        copy.start()
    for copy in copies + loads[1:]:
        copy.wait()


def merge_kernel(served, part_ref, suffix_ref, lse_ref, out_ref):
    part = part_ref[...].astype(jnp.float32)
    starts = range(0, len(served) * MESSAGE, MESSAGE)
    rows = [part[at : at + HALF] for at in starts]
    sums = unpack_stats([part[at + HALF : at + HALF + 1] for at in starts]).reshape(len(served), HALF, HD)
    blocks = []
    for block in range(H // HALF):
        span = slice(block * HALF, (block + 1) * HALF)
        own = [slot for slot, its in enumerate(served) if its == block]
        own_lse = lse_ref[span]
        best = own_lse
        for slot in own:
            best = jnp.maximum(best, sums[slot])
        total = jnp.exp2(own_lse - best)
        numerator = total * suffix_ref[span]
        for slot in own:
            factor = jnp.exp2(sums[slot] - best)
            total = total + factor
            numerator = numerator + factor * rows[slot]
        blocks.append(numerator / total)
    out_ref[0] = jnp.concatenate(blocks, axis=0).astype(jnp.bfloat16)


def call(kernel, name, outs, operands, specs=None, **cost):
    return pl.pallas_call(
        kernel,
        out_shape=outs,
        in_specs=specs or [VMEM] * len(operands),
        out_specs=jax.tree.map(lambda _: VMEM, outs),
        name=name,
        compiler_params=pltpu.CompilerParams(vmem_limit_bytes=LIMIT),
        cost_estimate=pl.CostEstimate(**cost) if cost else None,
    )(*operands)


def local(queries, prefix_kv, suffix_kv, new_kv, suffix_len):
    groups = lax.axis_size("grp")
    members = lax.axis_size("blk")
    per_head = members // KVH
    devices = groups * members
    span = prefix_kv.shape[2]
    cache_rows = suffix_kv.shape[1] * 2 * KVH
    chips = per_head // CORES
    served = [device % members // per_head * CORES + device % CORES for device in range(devices)]

    def one(rows):
        return jax.ShapeDtypeStruct((rows, HD), jnp.float32)

    def half(*shape):
        return jax.ShapeDtypeStruct((*shape, HD), jnp.bfloat16)

    def exchange(array):
        return lax.all_to_all(array, ("grp", "blk"), 0, 0, tiled=True)

    bound = [
        pltpu.with_memory_space_constraint(array, pltpu.HBM)
        for array in (
            queries.reshape(KVH, SHARE, HD),
            prefix_kv.reshape(2, span, HD),
            suffix_kv.reshape(cache_rows, HD),
        )
    ]
    outgoing, q, kv, cache = pl.pallas_call(
        fan_kernel,
        out_shape=[half(groups, KVH, chips, SHARE), half(KVH, SHARE), half(2, span), half(cache_rows)],
        in_specs=[pl.BlockSpec(memory_space=pltpu.HBM)] * 3,
        out_specs=[pl.BlockSpec(memory_space=pl.ANY), VMEM, VMEM, VMEM],
        scratch_shapes=[pltpu.SemaphoreType.DMA((3,)), pltpu.SemaphoreType.DMA((groups, chips))],
        name="fan",
        compiler_params=pltpu.CompilerParams(vmem_limit_bytes=LIMIT),
    )(*bound)
    arrived = exchange(outgoing.reshape(devices, HALF, HD)).reshape(devices * HALF, HD)
    other = lax.ppermute(kv, "blk", [(i, i ^ 1) for i in range(members)])
    suffix = call(
        suffix_kernel,
        "suffix",
        [one(H)] * 2,
        (suffix_len, new_kv.reshape(2 * KVH, HD), q, cache),
        [pl.BlockSpec(memory_space=pltpu.SMEM), VMEM, VMEM, VMEM],
        flops=70_000_000,
        bytes_accessed=600_000,
        transcendentals=140_000,
    )
    arrived, suffix = lax.optimization_barrier((arrived, suffix))
    partial = call(
        prefix_kernel,
        "prefix",
        half(devices * MESSAGE),
        (arrived, kv, other),
        flops=12 * devices * HALF * span * HD,
        bytes_accessed=1_600_000,
        transcendentals=2 * devices * HALF * span,
    )
    returned = exchange(partial.reshape(devices, MESSAGE // 2, 2, HD)).reshape(-1, HD)
    return call(
        functools.partial(merge_kernel, served),
        "merge",
        jax.ShapeDtypeStruct((1, H, HD), jnp.bfloat16),
        (returned, *suffix),
    )


def solution(mesh):
    in_specs = (
        P(("grp", "blk"), None, None),
        P(None, "grp", "blk", None),
        P(("grp", "blk"), None, None, None, None),
        P(("grp", "blk"), None, None, None),
        P(("grp", "blk")),
    )
    out_specs = P(("grp", "blk"), None, None)
    return jax.shard_map(local, mesh=mesh, in_specs=in_specs, out_specs=out_specs, check_vma=False)
```

```python
import functools
import math

import jax
import jax.numpy as jnp
from jax import lax
from jax.experimental import pallas as pl
from jax.experimental.pallas import tpu as pltpu
from jax.sharding import PartitionSpec as P

H = 64
KVH = 4
HD = 128
SHARE = H // KVH
SCALE2 = HD ** (-0.5) * math.log2(math.e)
VMEM = pl.BlockSpec(memory_space=pltpu.VMEM)
ROWS = 256
CHUNK = 512
CORES = 2
HALF = SHARE // CORES
MESSAGE = HALF + 2
LANES = HD // HALF
LIMIT = 24 * 1024 * 1024
NT = (((1,), (1,)), ((), ()))


def dot_nt(a, b):
    return lax.dot_general(a, b, NT, preferred_element_type=jnp.float32)


def dot(a, b):
    return jnp.dot(a, b, preferred_element_type=jnp.float32)


def log2(x):
    return jnp.log(x) * math.log2(math.e)


def pack_stats(x):
    hi = x.astype(jnp.bfloat16).astype(jnp.float32)
    rest = x - hi
    mid = rest.astype(jnp.bfloat16).astype(jnp.float32)
    low = rest - mid
    row = lax.broadcasted_iota(jnp.int32, x.shape, 1)
    lane = lax.broadcasted_iota(jnp.int32, x.shape, 2) - row * LANES
    return jnp.sum(jnp.where(lane == 0, hi, jnp.where(lane == 1, mid, jnp.where(lane == 2, low, 0.0))), axis=1)


def unpack_stats(rows):
    shape = (HALF, HD)
    mine = lax.broadcasted_iota(jnp.int32, shape, 1) // LANES == lax.broadcasted_iota(jnp.int32, shape, 0)
    pieces = [jnp.where(mine, jnp.broadcast_to(row, shape), 0.0) for row in rows]
    return dot(jnp.concatenate(pieces, axis=0).astype(jnp.bfloat16), jnp.ones((HD, HD), jnp.bfloat16))


def prefix_kernel(q_ref, kv_ref, other_ref, out_ref):
    chunks = [(ref, at) for ref in (other_ref, kv_ref) for at in range(0, ref.shape[1], CHUNK)]

    def block(trip):
        rows = q_ref[pl.ds(trip * ROWS, ROWS)]

        def score(ref, first):
            return dot_nt(rows, ref[0, first : first + CHUNK])

        parts = []
        ahead = score(*chunks[0])
        for index, (ref, first) in enumerate(chunks):
            scores = ahead
            if index + 1 < len(chunks):
                ahead = score(*chunks[index + 1])
            best = jnp.max(scores, axis=1, keepdims=True)
            weight = jnp.exp2((scores - best) * SCALE2).astype(jnp.bfloat16)
            total = jnp.sum(weight.astype(jnp.float32), axis=1, keepdims=True)
            parts.append((best, total, dot(weight, ref[1, first : first + CHUNK])))
        best = functools.reduce(jnp.maximum, [part[0] for part in parts])
        factors = [jnp.exp2((part[0] - best) * SCALE2) for part in parts]
        total = sum(factor * part[1] for factor, part in zip(factors, parts))
        result = sum(factor * part[2] for factor, part in zip(factors, parts)) / total
        slots = ROWS // HALF
        lse = jnp.broadcast_to(best * SCALE2 + log2(total), result.shape)
        stats = pack_stats(lse.reshape(slots, HALF, HD))
        empty = jnp.zeros((1, HD), jnp.float32)
        pieces = []
        for slot in range(slots):
            pieces += [result[slot * HALF : (slot + 1) * HALF], stats[slot : slot + 1], empty]
        out_ref[pl.ds(trip * slots * MESSAGE, slots * MESSAGE)] = jnp.concatenate(pieces, axis=0).astype(jnp.bfloat16)

    trips = q_ref.shape[0] // ROWS
    if trips == 1:
        block(0)
    else:

        def body(trip, unused):
            block(trip)
            return unused

        lax.fori_loop(0, trips, body, 0)


def owned(shape, limit):
    at = lax.broadcasted_iota(jnp.int32, shape, 1)
    head = lax.broadcasted_iota(jnp.int32, shape, 0) // SHARE
    return (at % (2 * KVH) == head) & (at < limit * (2 * KVH))


def suffix_kernel(len_ref, new_ref, q_ref, cache_ref, out_ref, lse_ref):
    q = q_ref[...].reshape(H, HD)
    cache = cache_ref[...]
    new = new_ref[...]
    raw = dot_nt(q, cache)
    scores = jnp.where(owned(raw.shape, len_ref[0]), raw, -jnp.inf)
    new_raw = dot_nt(q, new)
    new_scores = jnp.where(owned(new_raw.shape, 1), new_raw, -jnp.inf)
    best = jnp.maximum(jnp.max(scores, axis=1, keepdims=True), jnp.max(new_scores, axis=1, keepdims=True))
    weight = jnp.exp2((scores - best) * SCALE2).astype(jnp.bfloat16).astype(jnp.float32)
    new_weight = jnp.exp2((new_scores - best) * SCALE2).astype(jnp.bfloat16).astype(jnp.float32)
    total = jnp.sum(weight, axis=1, keepdims=True) + jnp.sum(new_weight, axis=1, keepdims=True)
    moved = pltpu.roll(weight, KVH, 1).astype(jnp.bfloat16)
    new_moved = jnp.concatenate([new_weight[:, KVH:], new_weight[:, :KVH]], axis=1).astype(jnp.bfloat16)
    out_ref[...] = (dot(moved, cache) + dot(new_moved, new)) / total
    lse_ref[...] = jnp.broadcast_to(best * SCALE2 + log2(total), lse_ref.shape)


def fan_kernel(q_hbm, kv_hbm, cache_hbm, out_ref, q_ref, kv_ref, cache_ref, sems, fan_sems):
    pairs = [(q_hbm, q_ref), (cache_hbm, cache_ref), (kv_hbm, kv_ref)]
    loads = [pltpu.make_async_copy(source, target, sems.at[i]) for i, (source, target) in enumerate(pairs)]
    for load in loads:
        load.start()
    loads[0].wait()
    copies = [
        pltpu.make_async_copy(q_ref, out_ref.at[group, :, chip], fan_sems.at[group, chip])
        for group in range(out_ref.shape[0])
        for chip in range(out_ref.shape[2])
    ]
    for copy in copies:
        copy.start()
    for copy in copies + loads[1:]:
        copy.wait()


def merge_kernel(served, part_ref, suffix_ref, lse_ref, out_ref):
    part = part_ref[...].astype(jnp.float32)
    starts = range(0, len(served) * MESSAGE, MESSAGE)
    rows = [part[at : at + HALF] for at in starts]
    sums = unpack_stats([part[at + HALF : at + HALF + 1] for at in starts]).reshape(len(served), HALF, HD)
    blocks = []
    for block in range(H // HALF):
        span = slice(block * HALF, (block + 1) * HALF)
        own = [slot for slot, its in enumerate(served) if its == block]
        own_lse = lse_ref[span]
        best = own_lse
        for slot in own:
            best = jnp.maximum(best, sums[slot])
        total = jnp.exp2(own_lse - best)
        numerator = total * suffix_ref[span]
        for slot in own:
            factor = jnp.exp2(sums[slot] - best)
            total = total + factor
            numerator = numerator + factor * rows[slot]
        blocks.append(numerator / total)
    out_ref[0] = jnp.concatenate(blocks, axis=0).astype(jnp.bfloat16)


def call(kernel, name, outs, operands, specs=None, **cost):
    return pl.pallas_call(
        kernel,
        out_shape=outs,
        in_specs=specs or [VMEM] * len(operands),
        out_specs=jax.tree.map(lambda _: VMEM, outs),
        name=name,
        compiler_params=pltpu.CompilerParams(vmem_limit_bytes=LIMIT),
        cost_estimate=pl.CostEstimate(**cost) if cost else None,
    )(*operands)


def local(queries, prefix_kv, suffix_kv, new_kv, suffix_len):
    groups = lax.axis_size("grp")
    members = lax.axis_size("blk")
    per_head = members // KVH
    devices = groups * members
    span = prefix_kv.shape[2]
    cache_rows = suffix_kv.shape[1] * 2 * KVH
    chips = per_head // CORES
    served = [device % members // per_head * CORES + device % CORES for device in range(devices)]

    def one(rows):
        return jax.ShapeDtypeStruct((rows, HD), jnp.float32)

    def half(*shape):
        return jax.ShapeDtypeStruct((*shape, HD), jnp.bfloat16)

    def exchange(array):
        return lax.all_to_all(array, ("grp", "blk"), 0, 0, tiled=True)

    other = lax.ppermute(prefix_kv, "blk", [(i, i ^ 1) for i in range(members)]).reshape(2, span, HD)
    bound = [
        pltpu.with_memory_space_constraint(array, pltpu.HBM)
        for array in (
            queries.reshape(KVH, SHARE, HD),
            prefix_kv.reshape(2, span, HD),
            suffix_kv.reshape(cache_rows, HD),
        )
    ]
    outgoing, q, kv, cache = pl.pallas_call(
        fan_kernel,
        out_shape=[half(groups, KVH, chips, SHARE), half(KVH, SHARE), half(2, span), half(cache_rows)],
        in_specs=[pl.BlockSpec(memory_space=pltpu.HBM)] * 3,
        out_specs=[pl.BlockSpec(memory_space=pl.ANY), VMEM, VMEM, VMEM],
        scratch_shapes=[pltpu.SemaphoreType.DMA((3,)), pltpu.SemaphoreType.DMA((groups, chips))],
        name="fan",
        compiler_params=pltpu.CompilerParams(vmem_limit_bytes=LIMIT),
    )(*bound)
    arrived = exchange(outgoing.reshape(devices, HALF, HD)).reshape(devices * HALF, HD)
    suffix = call(
        suffix_kernel,
        "suffix",
        [one(H)] * 2,
        (suffix_len, new_kv.reshape(2 * KVH, HD), q, cache),
        [pl.BlockSpec(memory_space=pltpu.SMEM), VMEM, VMEM, VMEM],
        flops=70_000_000,
        bytes_accessed=600_000,
        transcendentals=140_000,
    )
    arrived, suffix = lax.optimization_barrier((arrived, suffix))
    partial = call(
        prefix_kernel,
        "prefix",
        half(devices * MESSAGE),
        (arrived, kv, other),
        flops=12 * devices * HALF * span * HD,
        bytes_accessed=1_600_000,
        transcendentals=2 * devices * HALF * span,
    )
    returned = exchange(partial.reshape(devices, MESSAGE // 2, 2, HD)).reshape(-1, HD)
    return call(
        functools.partial(merge_kernel, served),
        "merge",
        jax.ShapeDtypeStruct((1, H, HD), jnp.bfloat16),
        (returned, *suffix),
    )


def solution(mesh):
    in_specs = (
        P(("grp", "blk"), None, None),
        P(None, "grp", "blk", None),
        P(("grp", "blk"), None, None, None, None),
        P(("grp", "blk"), None, None, None),
        P(("grp", "blk")),
    )
    out_specs = P(("grp", "blk"), None, None)
    return jax.shard_map(local, mesh=mesh, in_specs=in_specs, out_specs=out_specs, check_vma=False)
```

```python
import functools
import math

import jax
import jax.numpy as jnp
from jax import lax
from jax.experimental import pallas as pl
from jax.experimental.pallas import tpu as pltpu
from jax.sharding import PartitionSpec as P

H = 64
KVH = 4
HD = 128
SHARE = H // KVH
SCALE2 = HD ** (-0.5) * math.log2(math.e)
VMEM = pl.BlockSpec(memory_space=pltpu.VMEM)
ROWS = 256
CHUNK = 512
CORES = 2
HALF = SHARE // CORES
MESSAGE = HALF + 2
LANES = HD // HALF
PIECES = 3
LIMIT = 24 * 1024 * 1024
NT = (((1,), (1,)), ((), ()))


def dot_nt(a, b):
    return lax.dot_general(a, b, NT, preferred_element_type=jnp.float32)


def dot(a, b):
    return jnp.dot(a, b, preferred_element_type=jnp.float32)


def log2(x):
    return jnp.log(x) * math.log2(math.e)


def split3(x):
    hi = x.astype(jnp.bfloat16).astype(jnp.float32)
    rest = x - hi
    mid = rest.astype(jnp.bfloat16).astype(jnp.float32)
    return hi, mid, rest - mid


def pack_stats(best, total):
    row = lax.broadcasted_iota(jnp.int32, best.shape, 1)
    lane = lax.broadcasted_iota(jnp.int32, best.shape, 2) - row * LANES
    packed = jnp.zeros_like(best)
    for at, piece in enumerate((*split3(best), *split3(total))):
        packed = jnp.where(lane == at, piece, packed)
    return jnp.sum(packed, axis=1)


def unpack_stats(rows):
    shape = (HALF, HD)
    mine = lax.broadcasted_iota(jnp.int32, shape, 1) // LANES == lax.broadcasted_iota(jnp.int32, shape, 0)
    pieces = [jnp.where(mine, jnp.broadcast_to(row, shape), 0.0) for row in rows]
    shape = (HD, 2 * HD)
    which = lax.broadcasted_iota(jnp.int32, shape, 0) % LANES // PIECES
    select = jnp.where(which == lax.broadcasted_iota(jnp.int32, shape, 1) // HD, 1.0, 0.0)
    return dot(jnp.concatenate(pieces, axis=0).astype(jnp.bfloat16), select.astype(jnp.bfloat16))


def prefix_kernel(q_ref, kv_ref, other_ref, out_ref):
    chunks = [(ref, at) for ref in (other_ref, kv_ref) for at in range(0, ref.shape[1], CHUNK)]

    def block(trip):
        rows = q_ref[pl.ds(trip * ROWS, ROWS)]

        def score(ref, first):
            return dot_nt(rows, ref[0, first : first + CHUNK])

        parts = []
        ahead = score(*chunks[0])
        for index, (ref, first) in enumerate(chunks):
            scores = ahead
            if index + 1 < len(chunks):
                ahead = score(*chunks[index + 1])
            best = jnp.max(scores, axis=1, keepdims=True)
            weight = jnp.exp2((scores - best) * SCALE2).astype(jnp.bfloat16)
            values = ref[1, first : first + CHUNK]
            parts.append((best, dot(weight, jnp.concatenate([values, jnp.ones_like(values)], axis=1))))
        best = functools.reduce(jnp.maximum, [part[0] for part in parts])
        both = sum(jnp.exp2((its - best) * SCALE2) * sums for its, sums in parts)
        numerator = both[:, :HD]
        slots = ROWS // HALF
        shape = (slots, HALF, HD)
        best = jnp.broadcast_to(best * SCALE2, numerator.shape)
        stats = pack_stats(best.reshape(shape), both[:, HD:].reshape(shape))
        empty = jnp.zeros((1, HD), jnp.float32)
        pieces = []
        for slot in range(slots):
            pieces += [numerator[slot * HALF : (slot + 1) * HALF], stats[slot : slot + 1], empty]
        out_ref[pl.ds(trip * slots * MESSAGE, slots * MESSAGE)] = jnp.concatenate(pieces, axis=0).astype(jnp.bfloat16)

    trips = q_ref.shape[0] // ROWS
    if trips == 1:
        block(0)
    else:

        def body(trip, unused):
            block(trip)
            return unused

        lax.fori_loop(0, trips, body, 0)


def owned(shape, limit):
    at = lax.broadcasted_iota(jnp.int32, shape, 1)
    head = lax.broadcasted_iota(jnp.int32, shape, 0) // SHARE
    return (at % (2 * KVH) == head) & (at < limit * (2 * KVH))


def suffix_kernel(len_ref, new_ref, q_ref, cache_ref, out_ref, lse_ref):
    q = q_ref[...].reshape(H, HD)
    cache = cache_ref[...]
    new = new_ref[...]
    raw = dot_nt(q, cache)
    scores = jnp.where(owned(raw.shape, len_ref[0]), raw, -jnp.inf)
    new_raw = dot_nt(q, new)
    new_scores = jnp.where(owned(new_raw.shape, 1), new_raw, -jnp.inf)
    best = jnp.maximum(jnp.max(scores, axis=1, keepdims=True), jnp.max(new_scores, axis=1, keepdims=True))
    weight = jnp.exp2((scores - best) * SCALE2).astype(jnp.bfloat16).astype(jnp.float32)
    new_weight = jnp.exp2((new_scores - best) * SCALE2).astype(jnp.bfloat16).astype(jnp.float32)
    total = jnp.sum(weight, axis=1, keepdims=True) + jnp.sum(new_weight, axis=1, keepdims=True)
    moved = pltpu.roll(weight, KVH, 1).astype(jnp.bfloat16)
    new_moved = jnp.concatenate([new_weight[:, KVH:], new_weight[:, :KVH]], axis=1).astype(jnp.bfloat16)
    out_ref[...] = (dot(moved, cache) + dot(new_moved, new)) / total
    lse_ref[...] = jnp.broadcast_to(best * SCALE2 + log2(total), lse_ref.shape)


def fan_kernel(q_hbm, kv_hbm, cache_hbm, out_ref, q_ref, kv_ref, cache_ref, sems, fan_sems):
    pairs = [(q_hbm, q_ref), (cache_hbm, cache_ref), (kv_hbm, kv_ref)]
    loads = [pltpu.make_async_copy(source, target, sems.at[i]) for i, (source, target) in enumerate(pairs)]
    for load in loads:
        load.start()
    loads[0].wait()
    copies = [
        pltpu.make_async_copy(q_ref, out_ref.at[group, :, chip], fan_sems.at[group, chip])
        for group in range(out_ref.shape[0])
        for chip in range(out_ref.shape[2])
    ]
    for copy in copies:
        copy.start()
    for copy in copies + loads[1:]:
        copy.wait()


def merge_kernel(served, part_ref, suffix_ref, lse_ref, out_ref):
    part = part_ref[...].astype(jnp.float32)
    starts = range(0, len(served) * MESSAGE, MESSAGE)
    rows = [part[at : at + HALF] for at in starts]
    sums = unpack_stats([part[at + HALF : at + HALF + 1] for at in starts]).reshape(len(served), HALF, 2 * HD)
    blocks = []
    for block in range(H // HALF):
        span = slice(block * HALF, (block + 1) * HALF)
        own = [slot for slot, its in enumerate(served) if its == block]
        own_lse = lse_ref[span]
        best = own_lse
        for slot in own:
            best = jnp.maximum(best, sums[slot, :, :HD])
        total = jnp.exp2(own_lse - best)
        numerator = total * suffix_ref[span]
        for slot in own:
            factor = jnp.exp2(sums[slot, :, :HD] - best)
            total = total + factor * sums[slot, :, HD:]
            numerator = numerator + factor * rows[slot]
        blocks.append(numerator / total)
    out_ref[0] = jnp.concatenate(blocks, axis=0).astype(jnp.bfloat16)


def call(kernel, name, outs, operands, specs=None, **cost):
    return pl.pallas_call(
        kernel,
        out_shape=outs,
        in_specs=specs or [VMEM] * len(operands),
        out_specs=jax.tree.map(lambda _: VMEM, outs),
        name=name,
        compiler_params=pltpu.CompilerParams(vmem_limit_bytes=LIMIT),
        cost_estimate=pl.CostEstimate(**cost) if cost else None,
    )(*operands)


def local(queries, prefix_kv, suffix_kv, new_kv, suffix_len):
    groups = lax.axis_size("grp")
    members = lax.axis_size("blk")
    per_head = members // KVH
    devices = groups * members
    span = prefix_kv.shape[2]
    cache_rows = suffix_kv.shape[1] * 2 * KVH
    chips = per_head // CORES
    served = [device % members // per_head * CORES + device % CORES for device in range(devices)]

    def one(rows):
        return jax.ShapeDtypeStruct((rows, HD), jnp.float32)

    def half(*shape):
        return jax.ShapeDtypeStruct((*shape, HD), jnp.bfloat16)

    def exchange(array):
        return lax.all_to_all(array, ("grp", "blk"), 0, 0, tiled=True)

    other = lax.ppermute(prefix_kv, "blk", [(i, i ^ 1) for i in range(members)]).reshape(2, span, HD)
    bound = [
        pltpu.with_memory_space_constraint(array, pltpu.HBM)
        for array in (
            queries.reshape(KVH, SHARE, HD),
            prefix_kv.reshape(2, span, HD),
            suffix_kv.reshape(cache_rows, HD),
        )
    ]
    outgoing, q, kv, cache = pl.pallas_call(
        fan_kernel,
        out_shape=[half(groups, KVH, chips, SHARE), half(KVH, SHARE), half(2, span), half(cache_rows)],
        in_specs=[pl.BlockSpec(memory_space=pltpu.HBM)] * 3,
        out_specs=[pl.BlockSpec(memory_space=pl.ANY), VMEM, VMEM, VMEM],
        scratch_shapes=[pltpu.SemaphoreType.DMA((3,)), pltpu.SemaphoreType.DMA((groups, chips))],
        name="fan",
        compiler_params=pltpu.CompilerParams(vmem_limit_bytes=LIMIT),
    )(*bound)
    arrived = exchange(outgoing.reshape(devices, HALF, HD)).reshape(devices * HALF, HD)
    suffix = call(
        suffix_kernel,
        "suffix",
        [one(H)] * 2,
        (suffix_len, new_kv.reshape(2 * KVH, HD), q, cache),
        [pl.BlockSpec(memory_space=pltpu.SMEM), VMEM, VMEM, VMEM],
        flops=70_000_000,
        bytes_accessed=600_000,
        transcendentals=140_000,
    )
    arrived, suffix = lax.optimization_barrier((arrived, suffix))
    partial = call(
        prefix_kernel,
        "prefix",
        half(devices * MESSAGE),
        (arrived, kv, other),
        flops=12 * devices * HALF * span * HD,
        bytes_accessed=1_600_000,
        transcendentals=2 * devices * HALF * span,
    )
    returned = exchange(partial.reshape(devices, MESSAGE // 2, 2, HD)).reshape(-1, HD)
    return call(
        functools.partial(merge_kernel, served),
        "merge",
        jax.ShapeDtypeStruct((1, H, HD), jnp.bfloat16),
        (returned, *suffix),
    )


def solution(mesh):
    in_specs = (
        P(("grp", "blk"), None, None),
        P(None, "grp", "blk", None),
        P(("grp", "blk"), None, None, None, None),
        P(("grp", "blk"), None, None, None),
        P(("grp", "blk")),
    )
    out_specs = P(("grp", "blk"), None, None)
    return jax.shard_map(local, mesh=mesh, in_specs=in_specs, out_specs=out_specs, check_vma=False)
```

```python
import functools
import math

import jax
import jax.numpy as jnp
from jax import lax
from jax.experimental import pallas as pl
from jax.experimental.pallas import tpu as pltpu
from jax.sharding import PartitionSpec as P

H = 64
KVH = 4
HD = 128
SHARE = H // KVH
SCALE2 = HD ** (-0.5) * math.log2(math.e)
VMEM = pl.BlockSpec(memory_space=pltpu.VMEM)
ROWS = 256
CHUNK = 512
AHEAD = 2
CORES = 2
HALF = SHARE // CORES
MESSAGE = HALF + 2
LANES = HD // HALF
LIMIT = 24 * 1024 * 1024
NT = (((1,), (1,)), ((), ()))


def dot_nt(a, b):
    return lax.dot_general(a, b, NT, preferred_element_type=jnp.float32)


def dot(a, b):
    return jnp.dot(a, b, preferred_element_type=jnp.float32)


def log2(x):
    return jnp.log(x) * math.log2(math.e)


def pack_stats(x):
    hi = x.astype(jnp.bfloat16).astype(jnp.float32)
    rest = x - hi
    mid = rest.astype(jnp.bfloat16).astype(jnp.float32)
    low = rest - mid
    row = lax.broadcasted_iota(jnp.int32, x.shape, 1)
    lane = lax.broadcasted_iota(jnp.int32, x.shape, 2) - row * LANES
    return jnp.sum(jnp.where(lane == 0, hi, jnp.where(lane == 1, mid, jnp.where(lane == 2, low, 0.0))), axis=1)


def unpack_stats(rows):
    shape = (HALF, HD)
    mine = lax.broadcasted_iota(jnp.int32, shape, 1) // LANES == lax.broadcasted_iota(jnp.int32, shape, 0)
    pieces = [jnp.where(mine, jnp.broadcast_to(row, shape), 0.0) for row in rows]
    return dot(jnp.concatenate(pieces, axis=0).astype(jnp.bfloat16), jnp.ones((HD, HD), jnp.bfloat16))


def prefix_kernel(q_ref, kv_ref, other_ref, out_ref):
    chunks = [(ref, at) for ref in (other_ref, kv_ref) for at in range(0, ref.shape[1], CHUNK)]

    def block(trip):
        rows = q_ref[pl.ds(trip * ROWS, ROWS)]

        def score(ref, first):
            return dot_nt(rows, ref[0, first : first + CHUNK])

        parts = []
        ahead = [score(*chunk) for chunk in chunks[:AHEAD]]
        for index, (ref, first) in enumerate(chunks):
            if index + AHEAD < len(chunks):
                ahead.append(score(*chunks[index + AHEAD]))
            scores = ahead.pop(0)
            best = jnp.max(scores, axis=1, keepdims=True)
            weight = jnp.exp2((scores - best) * SCALE2).astype(jnp.bfloat16)
            values = ref[1, first : first + CHUNK]
            parts.append((best, dot(weight, jnp.concatenate([values, jnp.ones_like(values)], axis=1))))
        best = functools.reduce(jnp.maximum, [part[0] for part in parts])
        both = sum(jnp.exp2((its - best) * SCALE2) * sums for its, sums in parts)
        total = both[:, HD:]
        result = both[:, :HD] / total
        slots = ROWS // HALF
        stats = pack_stats((best * SCALE2 + log2(total)).reshape(slots, HALF, HD))
        empty = jnp.zeros((1, HD), jnp.float32)
        pieces = []
        for slot in range(slots):
            pieces += [result[slot * HALF : (slot + 1) * HALF], stats[slot : slot + 1], empty]
        out_ref[pl.ds(trip * slots * MESSAGE, slots * MESSAGE)] = jnp.concatenate(pieces, axis=0).astype(jnp.bfloat16)

    trips = q_ref.shape[0] // ROWS
    if trips == 1:
        block(0)
    else:

        def body(trip, unused):
            block(trip)
            return unused

        lax.fori_loop(0, trips, body, 0)


def owned(shape, limit):
    at = lax.broadcasted_iota(jnp.int32, shape, 1)
    head = lax.broadcasted_iota(jnp.int32, shape, 0) // SHARE
    return (at % (2 * KVH) == head) & (at < limit * (2 * KVH))


def suffix_kernel(len_ref, new_ref, q_ref, cache_ref, out_ref, lse_ref):
    q = q_ref[...].reshape(H, HD)
    cache = cache_ref[...]
    new = new_ref[...]
    raw = dot_nt(q, cache)
    scores = jnp.where(owned(raw.shape, len_ref[0]), raw, -jnp.inf)
    new_raw = dot_nt(q, new)
    new_scores = jnp.where(owned(new_raw.shape, 1), new_raw, -jnp.inf)
    best = jnp.maximum(jnp.max(scores, axis=1, keepdims=True), jnp.max(new_scores, axis=1, keepdims=True))
    weight = jnp.exp2((scores - best) * SCALE2).astype(jnp.bfloat16).astype(jnp.float32)
    new_weight = jnp.exp2((new_scores - best) * SCALE2).astype(jnp.bfloat16).astype(jnp.float32)
    total = jnp.sum(weight, axis=1, keepdims=True) + jnp.sum(new_weight, axis=1, keepdims=True)
    moved = pltpu.roll(weight, KVH, 1).astype(jnp.bfloat16)
    new_moved = jnp.concatenate([new_weight[:, KVH:], new_weight[:, :KVH]], axis=1).astype(jnp.bfloat16)
    out_ref[...] = (dot(moved, cache) + dot(new_moved, new)) / total
    lse_ref[...] = jnp.broadcast_to(best * SCALE2 + log2(total), lse_ref.shape)


def fan_kernel(q_hbm, kv_hbm, cache_hbm, out_ref, q_ref, kv_ref, cache_ref, sems, fan_sems):
    pairs = [(q_hbm, q_ref), (cache_hbm, cache_ref), (kv_hbm, kv_ref)]
    loads = [pltpu.make_async_copy(source, target, sems.at[i]) for i, (source, target) in enumerate(pairs)]
    for load in loads:
        load.start()
    loads[0].wait()
    copies = [
        pltpu.make_async_copy(q_ref, out_ref.at[group, :, chip], fan_sems.at[group, chip])
        for group in range(out_ref.shape[0])
        for chip in range(out_ref.shape[2])
    ]
    for copy in copies:
        copy.start()
    for copy in copies + loads[1:]:
        copy.wait()


def merge_kernel(served, part_ref, suffix_ref, lse_ref, out_ref):
    part = part_ref[...].astype(jnp.float32)
    starts = range(0, len(served) * MESSAGE, MESSAGE)
    rows = [part[at : at + HALF] for at in starts]
    sums = unpack_stats([part[at + HALF : at + HALF + 1] for at in starts]).reshape(len(served), HALF, HD)
    blocks = []
    for block in range(H // HALF):
        span = slice(block * HALF, (block + 1) * HALF)
        own = [slot for slot, its in enumerate(served) if its == block]
        own_lse = lse_ref[span]
        best = own_lse
        for slot in own:
            best = jnp.maximum(best, sums[slot])
        total = jnp.exp2(own_lse - best)
        numerator = total * suffix_ref[span]
        for slot in own:
            factor = jnp.exp2(sums[slot] - best)
            total = total + factor
            numerator = numerator + factor * rows[slot]
        blocks.append(numerator / total)
    out_ref[0] = jnp.concatenate(blocks, axis=0).astype(jnp.bfloat16)


def call(kernel, name, outs, operands, specs=None, **cost):
    return pl.pallas_call(
        kernel,
        out_shape=outs,
        in_specs=specs or [VMEM] * len(operands),
        out_specs=jax.tree.map(lambda _: VMEM, outs),
        name=name,
        compiler_params=pltpu.CompilerParams(vmem_limit_bytes=LIMIT),
        cost_estimate=pl.CostEstimate(**cost) if cost else None,
    )(*operands)


def local(queries, prefix_kv, suffix_kv, new_kv, suffix_len):
    groups = lax.axis_size("grp")
    members = lax.axis_size("blk")
    per_head = members // KVH
    devices = groups * members
    span = prefix_kv.shape[2]
    cache_rows = suffix_kv.shape[1] * 2 * KVH
    chips = per_head // CORES
    served = [device % members // per_head * CORES + device % CORES for device in range(devices)]

    def one(rows):
        return jax.ShapeDtypeStruct((rows, HD), jnp.float32)

    def half(*shape):
        return jax.ShapeDtypeStruct((*shape, HD), jnp.bfloat16)

    def exchange(array):
        return lax.all_to_all(array, ("grp", "blk"), 0, 0, tiled=True)

    other = lax.ppermute(prefix_kv, "blk", [(i, i ^ 1) for i in range(members)]).reshape(2, span, HD)
    bound = [
        pltpu.with_memory_space_constraint(array, pltpu.HBM)
        for array in (
            queries.reshape(KVH, SHARE, HD),
            prefix_kv.reshape(2, span, HD),
            suffix_kv.reshape(cache_rows, HD),
        )
    ]
    outgoing, q, kv, cache = pl.pallas_call(
        fan_kernel,
        out_shape=[
            pltpu.HBM((groups, KVH, chips, SHARE, HD), jnp.bfloat16),
            half(KVH, SHARE),
            half(2, span),
            half(cache_rows),
        ],
        in_specs=[pl.BlockSpec(memory_space=pltpu.HBM)] * 3,
        out_specs=[pl.BlockSpec(memory_space=pltpu.HBM), VMEM, VMEM, VMEM],
        scratch_shapes=[pltpu.SemaphoreType.DMA((3,)), pltpu.SemaphoreType.DMA((groups, chips))],
        name="fan",
        compiler_params=pltpu.CompilerParams(vmem_limit_bytes=LIMIT),
    )(*bound)
    arrived = exchange(outgoing.reshape(devices, HALF, HD)).reshape(devices * HALF, HD)
    suffix = call(
        suffix_kernel,
        "suffix",
        [one(H)] * 2,
        (suffix_len, new_kv.reshape(2 * KVH, HD), q, cache),
        [pl.BlockSpec(memory_space=pltpu.SMEM), VMEM, VMEM, VMEM],
        flops=70_000_000,
        bytes_accessed=600_000,
        transcendentals=140_000,
    )
    arrived, suffix = lax.optimization_barrier((arrived, suffix))
    partial = call(
        prefix_kernel,
        "prefix",
        half(devices * MESSAGE),
        (arrived, kv, other),
        flops=12 * devices * HALF * span * HD,
        bytes_accessed=1_600_000,
        transcendentals=2 * devices * HALF * span,
    )
    returned = exchange(partial.reshape(devices, MESSAGE // 2, 2, HD)).reshape(-1, HD)
    return call(
        functools.partial(merge_kernel, served),
        "merge",
        jax.ShapeDtypeStruct((1, H, HD), jnp.bfloat16),
        (returned, *suffix),
    )


def solution(mesh):
    in_specs = (
        P(("grp", "blk"), None, None),
        P(None, "grp", "blk", None),
        P(("grp", "blk"), None, None, None, None),
        P(("grp", "blk"), None, None, None),
        P(("grp", "blk")),
    )
    out_specs = P(("grp", "blk"), None, None)
    return jax.shard_map(local, mesh=mesh, in_specs=in_specs, out_specs=out_specs, check_vma=False)
```

```python
import functools
import math

import jax
import jax.numpy as jnp
from jax import lax
from jax.experimental import pallas as pl
from jax.experimental.pallas import tpu as pltpu
from jax.sharding import PartitionSpec as P

H = 64
KVH = 4
HD = 128
SHARE = H // KVH
SCALE2 = HD ** (-0.5) * math.log2(math.e)
VMEM = pl.BlockSpec(memory_space=pltpu.VMEM)
ROWS = 256
CHUNK = 512
CORES = 2
HALF = SHARE // CORES
MESSAGE = HALF + 2
LANES = HD // HALF
LIMIT = 24 * 1024 * 1024
NT = (((1,), (1,)), ((), ()))


def dot_nt(a, b):
    return lax.dot_general(a, b, NT, preferred_element_type=jnp.float32)


def dot(a, b):
    return jnp.dot(a, b, preferred_element_type=jnp.float32)


def log2(x):
    return jnp.log(x) * math.log2(math.e)


def pack_stats(x):
    hi = x.astype(jnp.bfloat16).astype(jnp.float32)
    rest = x - hi
    mid = rest.astype(jnp.bfloat16).astype(jnp.float32)
    low = rest - mid
    row = lax.broadcasted_iota(jnp.int32, x.shape, 1)
    lane = lax.broadcasted_iota(jnp.int32, x.shape, 2) - row * LANES
    return jnp.sum(jnp.where(lane == 0, hi, jnp.where(lane == 1, mid, jnp.where(lane == 2, low, 0.0))), axis=1)


def unpack_stats(rows):
    shape = (HALF, HD)
    mine = lax.broadcasted_iota(jnp.int32, shape, 1) // LANES == lax.broadcasted_iota(jnp.int32, shape, 0)
    pieces = [jnp.where(mine, jnp.broadcast_to(row, shape), 0.0) for row in rows]
    return dot(jnp.concatenate(pieces, axis=0).astype(jnp.bfloat16), jnp.ones((HD, HD), jnp.bfloat16))


def prefix_kernel(q_ref, kv_ref, other_ref, out_ref):
    chunks = [(ref, at) for ref in (other_ref, kv_ref) for at in range(0, ref.shape[1], CHUNK)]

    def block(trip):
        rows = q_ref[pl.ds(trip * ROWS, ROWS)]

        def score(ref, first):
            return dot_nt(rows, ref[0, first : first + CHUNK])

        parts = []
        ahead = score(*chunks[0])
        for index, (ref, first) in enumerate(chunks):
            scores = ahead
            if index + 1 < len(chunks):
                ahead = score(*chunks[index + 1])
            best = jnp.max(scores, axis=1, keepdims=True)
            weight = jnp.exp2((scores - best) * SCALE2).astype(jnp.bfloat16)
            values = ref[1, first : first + CHUNK]
            parts.append((best, dot(weight, jnp.concatenate([values, jnp.ones_like(values)], axis=1))))
        best = functools.reduce(jnp.maximum, [part[0] for part in parts])
        both = sum(jnp.exp2((its - best) * SCALE2) * sums for its, sums in parts)
        total = both[:, HD:]
        result = both[:, :HD] / total
        slots = ROWS // HALF
        stats = pack_stats((best * SCALE2 + log2(total)).reshape(slots, HALF, HD))
        empty = jnp.zeros((1, HD), jnp.float32)
        pieces = []
        for slot in range(slots):
            pieces += [result[slot * HALF : (slot + 1) * HALF], stats[slot : slot + 1], empty]
        out_ref[pl.ds(trip * slots * MESSAGE, slots * MESSAGE)] = jnp.concatenate(pieces, axis=0).astype(jnp.bfloat16)

    trips = q_ref.shape[0] // ROWS
    if trips == 1:
        block(0)
    else:

        def body(trip, unused):
            block(trip)
            return unused

        lax.fori_loop(0, trips, body, 0)


def owned(shape, limit):
    at = lax.broadcasted_iota(jnp.int32, shape, 1)
    head = lax.broadcasted_iota(jnp.int32, shape, 0) // SHARE
    return (at % (2 * KVH) == head) & (at < limit * (2 * KVH))


def suffix_kernel(len_ref, new_ref, q_ref, cache_ref, out_ref, lse_ref):
    q = q_ref[...].reshape(H, HD)
    cache = cache_ref[...]
    new = new_ref[...]
    raw = dot_nt(q, cache)
    scores = jnp.where(owned(raw.shape, len_ref[0]), raw, -jnp.inf)
    new_raw = dot_nt(q, new)
    new_scores = jnp.where(owned(new_raw.shape, 1), new_raw, -jnp.inf)
    best = jnp.maximum(jnp.max(scores, axis=1, keepdims=True), jnp.max(new_scores, axis=1, keepdims=True))
    weight = jnp.exp2((scores - best) * SCALE2).astype(jnp.bfloat16).astype(jnp.float32)
    new_weight = jnp.exp2((new_scores - best) * SCALE2).astype(jnp.bfloat16).astype(jnp.float32)
    total = jnp.sum(weight, axis=1, keepdims=True) + jnp.sum(new_weight, axis=1, keepdims=True)
    moved = pltpu.roll(weight, KVH, 1).astype(jnp.bfloat16)
    new_moved = jnp.concatenate([new_weight[:, KVH:], new_weight[:, :KVH]], axis=1).astype(jnp.bfloat16)
    out_ref[...] = (dot(moved, cache) + dot(new_moved, new)) / total
    lse_ref[...] = jnp.broadcast_to(best * SCALE2 + log2(total), lse_ref.shape)


def fan_kernel(q_hbm, kv_hbm, cache_hbm, out_ref, q_ref, kv_ref, cache_ref, sems, fan_sems):
    pairs = [(q_hbm, q_ref), (cache_hbm, cache_ref), (kv_hbm, kv_ref)]
    loads = [pltpu.make_async_copy(source, target, sems.at[i]) for i, (source, target) in enumerate(pairs)]
    for load in loads:
        load.start()
    loads[0].wait()
    copies = [
        pltpu.make_async_copy(q_ref, out_ref.at[group, :, chip], fan_sems.at[group, chip])
        for group in range(out_ref.shape[0])
        for chip in range(out_ref.shape[2])
    ]
    for copy in copies:
        copy.start()
    for copy in copies + loads[1:]:
        copy.wait()


def merge_kernel(served, part_ref, suffix_ref, lse_ref, out_ref):
    part = part_ref[...].astype(jnp.float32)
    starts = range(0, len(served) * MESSAGE, MESSAGE)
    rows = [part[at : at + HALF] for at in starts]
    sums = unpack_stats([part[at + HALF : at + HALF + 1] for at in starts]).reshape(len(served), HALF, HD)
    blocks = []
    for block in range(H // HALF):
        span = slice(block * HALF, (block + 1) * HALF)
        own = [slot for slot, its in enumerate(served) if its == block]
        own_lse = lse_ref[span]
        best = own_lse
        for slot in own:
            best = jnp.maximum(best, sums[slot])
        total = jnp.exp2(own_lse - best)
        numerator = total * suffix_ref[span]
        for slot in own:
            factor = jnp.exp2(sums[slot] - best)
            total = total + factor
            numerator = numerator + factor * rows[slot]
        blocks.append(numerator / total)
    out_ref[0] = jnp.concatenate(blocks, axis=0).astype(jnp.bfloat16)


def call(kernel, name, outs, operands, specs=None, **cost):
    return pl.pallas_call(
        kernel,
        out_shape=outs,
        in_specs=specs or [VMEM] * len(operands),
        out_specs=jax.tree.map(lambda _: VMEM, outs),
        name=name,
        compiler_params=pltpu.CompilerParams(vmem_limit_bytes=LIMIT),
        cost_estimate=pl.CostEstimate(**cost) if cost else None,
    )(*operands)


def local(queries, prefix_kv, suffix_kv, new_kv, suffix_len):
    groups = lax.axis_size("grp")
    members = lax.axis_size("blk")
    per_head = members // KVH
    devices = groups * members
    span = prefix_kv.shape[2]
    cache_rows = suffix_kv.shape[1] * 2 * KVH
    chips = per_head // CORES
    served = [device % members // per_head * CORES + device % CORES for device in range(devices)]

    def one(rows):
        return jax.ShapeDtypeStruct((rows, HD), jnp.float32)

    def half(*shape):
        return jax.ShapeDtypeStruct((*shape, HD), jnp.bfloat16)

    def exchange(array):
        return lax.all_to_all(array, ("grp", "blk"), 0, 0, tiled=True)

    other = lax.ppermute(prefix_kv, "blk", [(i, i ^ 1) for i in range(members)]).reshape(2, span, HD)
    bound = [
        pltpu.with_memory_space_constraint(array, pltpu.HBM)
        for array in (
            queries.reshape(KVH, SHARE, HD),
            prefix_kv.reshape(2, span, HD),
            suffix_kv.reshape(cache_rows, HD),
        )
    ]
    outgoing, q, kv, cache = pl.pallas_call(
        fan_kernel,
        out_shape=[
            pltpu.HBM((groups, KVH, chips, SHARE, HD), jnp.bfloat16),
            half(KVH, SHARE),
            half(2, span),
            half(cache_rows),
        ],
        in_specs=[pl.BlockSpec(memory_space=pltpu.HBM)] * 3,
        out_specs=[pl.BlockSpec(memory_space=pltpu.HBM), VMEM, VMEM, VMEM],
        scratch_shapes=[pltpu.SemaphoreType.DMA((3,)), pltpu.SemaphoreType.DMA((groups, chips))],
        name="fan",
        compiler_params=pltpu.CompilerParams(vmem_limit_bytes=LIMIT),
    )(*bound)
    arrived = exchange(outgoing.reshape(devices, HALF, HD)).reshape(devices * HALF, HD)
    suffix = call(
        suffix_kernel,
        "suffix",
        [one(H)] * 2,
        (suffix_len, new_kv.reshape(2 * KVH, HD), q, cache),
        [pl.BlockSpec(memory_space=pltpu.SMEM), VMEM, VMEM, VMEM],
        flops=70_000_000,
        bytes_accessed=600_000,
        transcendentals=140_000,
    )
    arrived, suffix = lax.optimization_barrier((arrived, suffix))
    partial = call(
        prefix_kernel,
        "prefix",
        half(devices * MESSAGE),
        (arrived, kv, other),
        flops=12 * devices * HALF * span * HD,
        bytes_accessed=1_600_000,
        transcendentals=2 * devices * HALF * span,
    )
    returned = exchange(partial.reshape(devices, MESSAGE // 2, 2, HD)).reshape(-1, HD)
    return call(
        functools.partial(merge_kernel, served),
        "merge",
        jax.ShapeDtypeStruct((1, H, HD), jnp.bfloat16),
        (returned, *suffix),
    )


def solution(mesh):
    in_specs = (
        P(("grp", "blk"), None, None),
        P(None, "grp", "blk", None),
        P(("grp", "blk"), None, None, None, None),
        P(("grp", "blk"), None, None, None),
        P(("grp", "blk")),
    )
    out_specs = P(("grp", "blk"), None, None)
    return jax.shard_map(local, mesh=mesh, in_specs=in_specs, out_specs=out_specs, check_vma=False)
```

```python
import functools
import math

import jax
import jax.numpy as jnp
from jax import lax
from jax.experimental import pallas as pl
from jax.experimental.pallas import tpu as pltpu
from jax.sharding import PartitionSpec as P

H = 64
KVH = 4
HD = 128
SHARE = H // KVH
SCALE2 = HD ** (-0.5) * math.log2(math.e)
VMEM = pl.BlockSpec(memory_space=pltpu.VMEM)
ROWS = 256
CHUNK = 512
PIECE = 256
CORES = 2
HALF = SHARE // CORES
MESSAGE = HALF + 2
LANES = HD // HALF
LIMIT = 24 * 1024 * 1024
NT = (((1,), (1,)), ((), ()))


def dot_nt(a, b):
    return lax.dot_general(a, b, NT, preferred_element_type=jnp.float32)


def dot(a, b):
    return jnp.dot(a, b, preferred_element_type=jnp.float32)


def log2(x):
    return jnp.log(x) * math.log2(math.e)


def pack_stats(x):
    hi = x.astype(jnp.bfloat16).astype(jnp.float32)
    rest = x - hi
    mid = rest.astype(jnp.bfloat16).astype(jnp.float32)
    low = rest - mid
    row = lax.broadcasted_iota(jnp.int32, x.shape, 1)
    lane = lax.broadcasted_iota(jnp.int32, x.shape, 2) - row * LANES
    return jnp.sum(jnp.where(lane == 0, hi, jnp.where(lane == 1, mid, jnp.where(lane == 2, low, 0.0))), axis=1)


def unpack_stats(rows):
    shape = (HALF, HD)
    mine = lax.broadcasted_iota(jnp.int32, shape, 1) // LANES == lax.broadcasted_iota(jnp.int32, shape, 0)
    pieces = [jnp.where(mine, jnp.broadcast_to(row, shape), 0.0) for row in rows]
    return dot(jnp.concatenate(pieces, axis=0).astype(jnp.bfloat16), jnp.ones((HD, HD), jnp.bfloat16))


def prefix_kernel(q_ref, kv_ref, other_ref, out_ref):
    chunks = [(ref, at) for ref in (other_ref, kv_ref) for at in range(0, ref.shape[1], CHUNK)]

    def block(trip):
        rows = q_ref[pl.ds(trip * ROWS, ROWS)]

        def score(ref, first):
            return dot_nt(rows, ref[0, first : first + CHUNK])

        parts = []
        ahead = score(*chunks[0])
        for index, (ref, first) in enumerate(chunks):
            scores = ahead
            if index + 1 < len(chunks):
                ahead = score(*chunks[index + 1])
            best = jnp.max(scores, axis=1, keepdims=True)
            weight = jnp.exp2((scores - best) * SCALE2).astype(jnp.bfloat16)
            values = ref[1, first : first + CHUNK]
            parts.append((best, dot(weight, jnp.concatenate([values, jnp.ones_like(values)], axis=1))))
        best = functools.reduce(jnp.maximum, [part[0] for part in parts])
        both = sum(jnp.exp2((its - best) * SCALE2) * sums for its, sums in parts)
        total = both[:, HD:]
        result = both[:, :HD] / total
        slots = ROWS // HALF
        stats = pack_stats((best * SCALE2 + log2(total)).reshape(slots, HALF, HD))
        empty = jnp.zeros((1, HD), jnp.float32)
        pieces = []
        for slot in range(slots):
            pieces += [result[slot * HALF : (slot + 1) * HALF], stats[slot : slot + 1], empty]
        out_ref[pl.ds(trip * slots * MESSAGE, slots * MESSAGE)] = jnp.concatenate(pieces, axis=0).astype(jnp.bfloat16)

    trips = q_ref.shape[0] // ROWS
    if trips == 1:
        block(0)
    else:

        def body(trip, unused):
            block(trip)
            return unused

        lax.fori_loop(0, trips, body, 0)


def owned(shape, limit):
    at = lax.broadcasted_iota(jnp.int32, shape, 1)
    head = lax.broadcasted_iota(jnp.int32, shape, 0) // SHARE
    return (at % (2 * KVH) == head) & (at < limit * (2 * KVH))


def suffix_kernel(len_ref, new_ref, q_ref, cache_ref, out_ref, lse_ref):
    q = q_ref[...].reshape(H, HD)
    cache = cache_ref[...]
    new = new_ref[...]
    raw = dot_nt(q, cache)
    scores = jnp.where(owned(raw.shape, len_ref[0]), raw, -jnp.inf)
    new_raw = dot_nt(q, new)
    new_scores = jnp.where(owned(new_raw.shape, 1), new_raw, -jnp.inf)
    best = jnp.maximum(jnp.max(scores, axis=1, keepdims=True), jnp.max(new_scores, axis=1, keepdims=True))
    weight = jnp.exp2((scores - best) * SCALE2).astype(jnp.bfloat16).astype(jnp.float32)
    new_weight = jnp.exp2((new_scores - best) * SCALE2).astype(jnp.bfloat16).astype(jnp.float32)
    total = jnp.sum(weight, axis=1, keepdims=True) + jnp.sum(new_weight, axis=1, keepdims=True)
    moved = pltpu.roll(weight, KVH, 1).astype(jnp.bfloat16)
    new_moved = jnp.concatenate([new_weight[:, KVH:], new_weight[:, :KVH]], axis=1).astype(jnp.bfloat16)
    out_ref[...] = (dot(moved, cache) + dot(new_moved, new)) / total
    lse_ref[...] = jnp.broadcast_to(best * SCALE2 + log2(total), lse_ref.shape)


def fan_kernel(q_hbm, kv_hbm, cache_hbm, out_ref, q_ref, kv_ref, cache_ref, sems):
    groups, heads, chips = out_ref.shape[:3]
    places = [(group, head, chip) for group in range(groups) for chip in range(chips) for head in range(heads)]
    pairs = [(q_hbm.at[head], out_ref.at[group, head, chip]) for group, head, chip in places]
    pairs.append((q_hbm, q_ref))
    spans = [(i, pl.ds(at, PIECE)) for at in range(0, kv_ref.shape[1], PIECE) for i in range(2)]
    pairs += [(kv_hbm.at[i, span], kv_ref.at[i, span]) for i, span in spans]
    spans = [pl.ds(at, PIECE) for at in range(0, cache_ref.shape[0], PIECE)]
    pairs += [(cache_hbm.at[span], cache_ref.at[span]) for span in spans]
    copies = [pltpu.make_async_copy(source, target, sems.at[i]) for i, (source, target) in enumerate(pairs)]
    for copy in copies:
        copy.start()
    for copy in copies:
        copy.wait()


def merge_kernel(served, part_ref, suffix_ref, lse_ref, out_ref):
    part = part_ref[...].astype(jnp.float32)
    starts = range(0, len(served) * MESSAGE, MESSAGE)
    rows = [part[at : at + HALF] for at in starts]
    sums = unpack_stats([part[at + HALF : at + HALF + 1] for at in starts]).reshape(len(served), HALF, HD)
    blocks = []
    for block in range(H // HALF):
        span = slice(block * HALF, (block + 1) * HALF)
        own = [slot for slot, its in enumerate(served) if its == block]
        own_lse = lse_ref[span]
        best = own_lse
        for slot in own:
            best = jnp.maximum(best, sums[slot])
        total = jnp.exp2(own_lse - best)
        numerator = total * suffix_ref[span]
        for slot in own:
            factor = jnp.exp2(sums[slot] - best)
            total = total + factor
            numerator = numerator + factor * rows[slot]
        blocks.append(numerator / total)
    out_ref[0] = jnp.concatenate(blocks, axis=0).astype(jnp.bfloat16)


def call(kernel, name, outs, operands, specs=None, **cost):
    return pl.pallas_call(
        kernel,
        out_shape=outs,
        in_specs=specs or [VMEM] * len(operands),
        out_specs=jax.tree.map(lambda _: VMEM, outs),
        name=name,
        compiler_params=pltpu.CompilerParams(vmem_limit_bytes=LIMIT),
        cost_estimate=pl.CostEstimate(**cost) if cost else None,
    )(*operands)


def local(queries, prefix_kv, suffix_kv, new_kv, suffix_len):
    groups = lax.axis_size("grp")
    members = lax.axis_size("blk")
    per_head = members // KVH
    devices = groups * members
    span = prefix_kv.shape[2]
    cache_rows = suffix_kv.shape[1] * 2 * KVH
    chips = per_head // CORES
    served = [device % members // per_head * CORES + device % CORES for device in range(devices)]

    def one(rows):
        return jax.ShapeDtypeStruct((rows, HD), jnp.float32)

    def half(*shape):
        return jax.ShapeDtypeStruct((*shape, HD), jnp.bfloat16)

    def exchange(array):
        return lax.all_to_all(array, ("grp", "blk"), 0, 0, tiled=True)

    other = lax.ppermute(prefix_kv, "blk", [(i, i ^ 1) for i in range(members)]).reshape(2, span, HD)
    bound = [
        pltpu.with_memory_space_constraint(array, pltpu.HBM)
        for array in (
            queries.reshape(KVH, SHARE, HD),
            prefix_kv.reshape(2, span, HD),
            suffix_kv.reshape(cache_rows, HD),
        )
    ]
    outgoing, q, kv, cache = pl.pallas_call(
        fan_kernel,
        out_shape=[half(groups, KVH, chips, SHARE), half(KVH, SHARE), half(2, span), half(cache_rows)],
        in_specs=[pl.BlockSpec(memory_space=pltpu.HBM)] * 3,
        out_specs=[pl.BlockSpec(memory_space=pl.ANY), VMEM, VMEM, VMEM],
        scratch_shapes=[pltpu.SemaphoreType.DMA((groups * KVH * chips + 1 + 2 * span // PIECE + cache_rows // PIECE,))],
        name="fan",
        compiler_params=pltpu.CompilerParams(vmem_limit_bytes=LIMIT),
    )(*bound)
    arrived = exchange(outgoing.reshape(devices, HALF, HD)).reshape(devices * HALF, HD)
    suffix = call(
        suffix_kernel,
        "suffix",
        [one(H)] * 2,
        (suffix_len, new_kv.reshape(2 * KVH, HD), q, cache),
        [pl.BlockSpec(memory_space=pltpu.SMEM), VMEM, VMEM, VMEM],
        flops=70_000_000,
        bytes_accessed=600_000,
        transcendentals=140_000,
    )
    arrived, suffix = lax.optimization_barrier((arrived, suffix))
    partial = call(
        prefix_kernel,
        "prefix",
        half(devices * MESSAGE),
        (arrived, kv, other),
        flops=12 * devices * HALF * span * HD,
        bytes_accessed=1_600_000,
        transcendentals=2 * devices * HALF * span,
    )
    returned = exchange(partial.reshape(devices, MESSAGE // 2, 2, HD)).reshape(-1, HD)
    return call(
        functools.partial(merge_kernel, served),
        "merge",
        jax.ShapeDtypeStruct((1, H, HD), jnp.bfloat16),
        (returned, *suffix),
    )


def solution(mesh):
    in_specs = (
        P(("grp", "blk"), None, None),
        P(None, "grp", "blk", None),
        P(("grp", "blk"), None, None, None, None),
        P(("grp", "blk"), None, None, None),
        P(("grp", "blk")),
    )
    out_specs = P(("grp", "blk"), None, None)
    return jax.shard_map(local, mesh=mesh, in_specs=in_specs, out_specs=out_specs, check_vma=False)
```

```python
import functools
import math

import jax
import jax.numpy as jnp
from jax import lax
from jax.experimental import pallas as pl
from jax.experimental.pallas import tpu as pltpu
from jax.sharding import PartitionSpec as P

H = 64
KVH = 4
HD = 128
SHARE = H // KVH
SCALE2 = HD ** (-0.5) * math.log2(math.e)
VMEM = pl.BlockSpec(memory_space=pltpu.VMEM)
ROWS = 256
CHUNK = 512
CORES = 2
HALF = SHARE // CORES
MESSAGE = HALF + 2
LANES = HD // HALF
LIMIT = 24 * 1024 * 1024
NT = (((1,), (1,)), ((), ()))


def dot_nt(a, b):
    return lax.dot_general(a, b, NT, preferred_element_type=jnp.float32)


def dot(a, b):
    return jnp.dot(a, b, preferred_element_type=jnp.float32)


def log2(x):
    return jnp.log(x) * math.log2(math.e)


def pack_stats(x):
    hi = x.astype(jnp.bfloat16).astype(jnp.float32)
    rest = x - hi
    mid = rest.astype(jnp.bfloat16).astype(jnp.float32)
    low = rest - mid
    row = lax.broadcasted_iota(jnp.int32, x.shape, 1)
    lane = lax.broadcasted_iota(jnp.int32, x.shape, 2) - row * LANES
    return jnp.sum(jnp.where(lane == 0, hi, jnp.where(lane == 1, mid, jnp.where(lane == 2, low, 0.0))), axis=1)


def unpack_stats(rows):
    shape = (HALF, HD)
    mine = lax.broadcasted_iota(jnp.int32, shape, 1) // LANES == lax.broadcasted_iota(jnp.int32, shape, 0)
    pieces = [jnp.where(mine, jnp.broadcast_to(row, shape), 0.0) for row in rows]
    return dot(jnp.concatenate(pieces, axis=0).astype(jnp.bfloat16), jnp.ones((HD, HD), jnp.bfloat16))


def prefix_kernel(q_ref, kv_ref, other_ref, out_ref):
    chunks = [(ref, at) for ref in (other_ref, kv_ref) for at in range(0, ref.shape[1], CHUNK)]

    def block(trip):
        rows = q_ref[pl.ds(trip * ROWS, ROWS)]

        def score(ref, first):
            return dot_nt(rows, ref[0, first : first + CHUNK])

        parts = []
        ahead = score(*chunks[0])
        for index, (ref, first) in enumerate(chunks):
            scores = ahead
            if index + 1 < len(chunks):
                ahead = score(*chunks[index + 1])
            best = jnp.max(scores, axis=1, keepdims=True)
            weight = jnp.exp2((scores - best) * SCALE2).astype(jnp.bfloat16)
            values = ref[1, first : first + CHUNK]
            parts.append((best, dot(weight, jnp.concatenate([values, jnp.ones_like(values)], axis=1))))
        best = functools.reduce(jnp.maximum, [part[0] for part in parts])
        both = sum(jnp.exp2((its - best) * SCALE2) * sums for its, sums in parts)
        total = both[:, HD:]
        result = both[:, :HD] / total
        slots = ROWS // HALF
        stats = pack_stats((best * SCALE2 + log2(total)).reshape(slots, HALF, HD))
        empty = jnp.zeros((1, HD), jnp.float32)
        pieces = []
        for slot in range(slots):
            pieces += [result[slot * HALF : (slot + 1) * HALF], stats[slot : slot + 1], empty]
        out_ref[pl.ds(trip * slots * MESSAGE, slots * MESSAGE)] = jnp.concatenate(pieces, axis=0).astype(jnp.bfloat16)

    trips = q_ref.shape[0] // ROWS
    if trips == 1:
        block(0)
    else:

        def body(trip, unused):
            block(trip)
            return unused

        lax.fori_loop(0, trips, body, 0)


def owned(shape, limit):
    at = lax.broadcasted_iota(jnp.int32, shape, 1)
    head = lax.broadcasted_iota(jnp.int32, shape, 0) // SHARE
    return (at % (2 * KVH) == head) & (at < limit * (2 * KVH))


def suffix_kernel(len_ref, new_ref, q_ref, cache_ref, out_ref, lse_ref):
    q = q_ref[...]
    cache = cache_ref[...]
    new = new_ref[...]
    raw = dot_nt(q, cache)
    scores = jnp.where(owned(raw.shape, len_ref[0]), raw, -jnp.inf)
    new_raw = dot_nt(q, new)
    new_scores = jnp.where(owned(new_raw.shape, 1), new_raw, -jnp.inf)
    best = jnp.maximum(jnp.max(scores, axis=1, keepdims=True), jnp.max(new_scores, axis=1, keepdims=True))
    weight = jnp.exp2((scores - best) * SCALE2).astype(jnp.bfloat16).astype(jnp.float32)
    new_weight = jnp.exp2((new_scores - best) * SCALE2).astype(jnp.bfloat16).astype(jnp.float32)
    total = jnp.sum(weight, axis=1, keepdims=True) + jnp.sum(new_weight, axis=1, keepdims=True)
    moved = pltpu.roll(weight, KVH, 1).astype(jnp.bfloat16)
    new_moved = jnp.concatenate([new_weight[:, KVH:], new_weight[:, :KVH]], axis=1).astype(jnp.bfloat16)
    out_ref[...] = (dot(moved, cache) + dot(new_moved, new)) / total
    lse_ref[...] = jnp.broadcast_to(best * SCALE2 + log2(total), lse_ref.shape)


def fan_kernel(q_hbm, kv_hbm, cache_hbm, out_ref, q_ref, kv_ref, cache_ref, sems, fan_sems):
    pairs = [(q_hbm, q_ref), (cache_hbm, cache_ref), (kv_hbm, kv_ref)]
    loads = [pltpu.make_async_copy(source, target, sems.at[i]) for i, (source, target) in enumerate(pairs)]
    for load in loads:
        load.start()
    loads[0].wait()
    copies = [pltpu.make_async_copy(q_ref, out_ref.at[i], fan_sems.at[i]) for i in range(out_ref.shape[0])]
    for copy in copies:
        copy.start()
    for copy in copies + loads[1:]:
        copy.wait()


def merge_kernel(served, part_ref, suffix_ref, lse_ref, out_ref):
    part = part_ref[...].astype(jnp.float32)
    starts = range(0, len(served) * MESSAGE, MESSAGE)
    rows = [part[at : at + HALF] for at in starts]
    sums = unpack_stats([part[at + HALF : at + HALF + 1] for at in starts]).reshape(len(served), HALF, HD)
    blocks = []
    for block in range(H // HALF):
        span = slice(block * HALF, (block + 1) * HALF)
        own = [slot for slot, its in enumerate(served) if its == block]
        own_lse = lse_ref[span]
        best = own_lse
        for slot in own:
            best = jnp.maximum(best, sums[slot])
        total = jnp.exp2(own_lse - best)
        numerator = total * suffix_ref[span]
        for slot in own:
            factor = jnp.exp2(sums[slot] - best)
            total = total + factor
            numerator = numerator + factor * rows[slot]
        blocks.append(numerator / total)
    out_ref[0] = jnp.concatenate(blocks, axis=0).astype(jnp.bfloat16)


def call(kernel, name, outs, operands, specs=None, **cost):
    return pl.pallas_call(
        kernel,
        out_shape=outs,
        in_specs=specs or [VMEM] * len(operands),
        out_specs=jax.tree.map(lambda _: VMEM, outs),
        name=name,
        compiler_params=pltpu.CompilerParams(vmem_limit_bytes=LIMIT),
        cost_estimate=pl.CostEstimate(**cost) if cost else None,
    )(*operands)


def local(queries, prefix_kv, suffix_kv, new_kv, suffix_len):
    groups = lax.axis_size("grp")
    members = lax.axis_size("blk")
    per_head = members // KVH
    devices = groups * members
    span = prefix_kv.shape[2]
    cache_rows = suffix_kv.shape[1] * 2 * KVH
    chips = per_head // CORES
    order = [
        g * members + (head * chips + chip) * CORES + core
        for g in range(groups)
        for chip in range(chips)
        for head in range(KVH)
        for core in range(CORES)
    ]
    served = [device % members // per_head * CORES + device % CORES for device in order]

    def one(rows):
        return jax.ShapeDtypeStruct((rows, HD), jnp.float32)

    def half(*shape):
        return jax.ShapeDtypeStruct((*shape, HD), jnp.bfloat16)

    def exchange(array):
        return lax.all_to_all(array, ("grp", "blk"), 0, 0, axis_index_groups=[order], tiled=True)

    other = lax.ppermute(prefix_kv, "blk", [(i, i ^ 1) for i in range(members)]).reshape(2, span, HD)
    bound = [
        pltpu.with_memory_space_constraint(array, pltpu.HBM)
        for array in (
            queries.reshape(H, HD),
            prefix_kv.reshape(2, span, HD),
            suffix_kv.reshape(cache_rows, HD),
        )
    ]
    outgoing, q, kv, cache = pl.pallas_call(
        fan_kernel,
        out_shape=[half(groups * chips, H), half(H), half(2, span), half(cache_rows)],
        in_specs=[pl.BlockSpec(memory_space=pltpu.HBM)] * 3,
        out_specs=[pl.BlockSpec(memory_space=pl.ANY), VMEM, VMEM, VMEM],
        scratch_shapes=[pltpu.SemaphoreType.DMA((3,)), pltpu.SemaphoreType.DMA((groups * chips,))],
        name="fan",
        compiler_params=pltpu.CompilerParams(vmem_limit_bytes=LIMIT),
    )(*bound)
    arrived = exchange(outgoing.reshape(devices, HALF, HD)).reshape(devices * HALF, HD)
    suffix = call(
        suffix_kernel,
        "suffix",
        [one(H)] * 2,
        (suffix_len, new_kv.reshape(2 * KVH, HD), q, cache),
        [pl.BlockSpec(memory_space=pltpu.SMEM), VMEM, VMEM, VMEM],
        flops=70_000_000,
        bytes_accessed=600_000,
        transcendentals=140_000,
    )
    arrived, suffix = lax.optimization_barrier((arrived, suffix))
    partial = call(
        prefix_kernel,
        "prefix",
        half(devices * MESSAGE),
        (arrived, kv, other),
        flops=12 * devices * HALF * span * HD,
        bytes_accessed=1_600_000,
        transcendentals=2 * devices * HALF * span,
    )
    returned = exchange(partial.reshape(devices, MESSAGE // 2, 2, HD)).reshape(-1, HD)
    return call(
        functools.partial(merge_kernel, served),
        "merge",
        jax.ShapeDtypeStruct((1, H, HD), jnp.bfloat16),
        (returned, *suffix),
    )


def solution(mesh):
    in_specs = (
        P(("grp", "blk"), None, None),
        P(None, "grp", "blk", None),
        P(("grp", "blk"), None, None, None, None),
        P(("grp", "blk"), None, None, None),
        P(("grp", "blk")),
    )
    out_specs = P(("grp", "blk"), None, None)
    return jax.shard_map(local, mesh=mesh, in_specs=in_specs, out_specs=out_specs, check_vma=False)
```

```python
import functools
import math

import jax
import jax.numpy as jnp
from jax import lax
from jax.experimental import pallas as pl
from jax.experimental.pallas import tpu as pltpu
from jax.sharding import PartitionSpec as P

H = 64
KVH = 4
HD = 128
SHARE = H // KVH
SCALE2 = HD ** (-0.5) * math.log2(math.e)
VMEM = pl.BlockSpec(memory_space=pltpu.VMEM)
ROWS = 256
CHUNK = 512
CORES = 2
HALF = SHARE // CORES
MESSAGE = HALF + 2
LANES = HD // HALF
LIMIT = 24 * 1024 * 1024
NT = (((1,), (1,)), ((), ()))


def dot_nt(a, b):
    return lax.dot_general(a, b, NT, preferred_element_type=jnp.float32)


def dot(a, b):
    return jnp.dot(a, b, preferred_element_type=jnp.float32)


def log2(x):
    return jnp.log(x) * math.log2(math.e)


def pack_stats(x):
    hi = x.astype(jnp.bfloat16).astype(jnp.float32)
    rest = x - hi
    mid = rest.astype(jnp.bfloat16).astype(jnp.float32)
    low = rest - mid
    row = lax.broadcasted_iota(jnp.int32, x.shape, 1)
    lane = lax.broadcasted_iota(jnp.int32, x.shape, 2) - row * LANES
    return jnp.sum(jnp.where(lane == 0, hi, jnp.where(lane == 1, mid, jnp.where(lane == 2, low, 0.0))), axis=1)


def unpack_stats(rows):
    shape = (HALF, HD)
    mine = lax.broadcasted_iota(jnp.int32, shape, 1) // LANES == lax.broadcasted_iota(jnp.int32, shape, 0)
    pieces = [jnp.where(mine, jnp.broadcast_to(row, shape), 0.0) for row in rows]
    return dot(jnp.concatenate(pieces, axis=0).astype(jnp.bfloat16), jnp.ones((HD, HD), jnp.bfloat16))


def prefix_kernel(q_ref, kv_ref, other_ref, out_ref):
    chunks = [(ref, at) for ref in (other_ref, kv_ref) for at in range(0, ref.shape[1], CHUNK)]

    def block(trip):
        rows = q_ref[pl.ds(trip * ROWS, ROWS)]

        def score(ref, first):
            return dot_nt(rows, ref[0, first : first + CHUNK])

        parts = []
        ahead = score(*chunks[0])
        for index, (ref, first) in enumerate(chunks):
            scores = ahead
            if index + 1 < len(chunks):
                ahead = score(*chunks[index + 1])
            best = jnp.max(scores, axis=1, keepdims=True)
            weight = jnp.exp2((scores - best) * SCALE2).astype(jnp.bfloat16)
            values = ref[1, first : first + CHUNK]
            parts.append((best, dot(weight, jnp.concatenate([values, jnp.ones_like(values)], axis=1))))
        best = functools.reduce(jnp.maximum, [part[0] for part in parts])
        both = sum(jnp.exp2((its - best) * SCALE2) * sums for its, sums in parts)
        total = both[:, HD:]
        result = both[:, :HD] / total
        slots = ROWS // HALF
        stats = pack_stats((best * SCALE2 + log2(total)).reshape(slots, HALF, HD))
        empty = jnp.zeros((1, HD), jnp.float32)
        pieces = []
        for slot in range(slots):
            pieces += [result[slot * HALF : (slot + 1) * HALF], stats[slot : slot + 1], empty]
        out_ref[pl.ds(trip * slots * MESSAGE, slots * MESSAGE)] = jnp.concatenate(pieces, axis=0).astype(jnp.bfloat16)

    trips = q_ref.shape[0] // ROWS
    if trips == 1:
        block(0)
    else:

        def body(trip, unused):
            block(trip)
            return unused

        lax.fori_loop(0, trips, body, 0)


def owned(shape, limit):
    at = lax.broadcasted_iota(jnp.int32, shape, 1)
    head = lax.broadcasted_iota(jnp.int32, shape, 0) // SHARE
    return (at % (2 * KVH) == head) & (at < limit * (2 * KVH))


def suffix_kernel(len_ref, new_ref, q_ref, cache_ref, out_ref, lse_ref):
    q = q_ref[...].reshape(H, HD)
    cache = cache_ref[...]
    new = new_ref[...]
    raw = dot_nt(q, cache)
    scores = jnp.where(owned(raw.shape, len_ref[0]), raw, -jnp.inf)
    new_raw = dot_nt(q, new)
    new_scores = jnp.where(owned(new_raw.shape, 1), new_raw, -jnp.inf)
    best = jnp.maximum(jnp.max(scores, axis=1, keepdims=True), jnp.max(new_scores, axis=1, keepdims=True))
    weight = jnp.exp2((scores - best) * SCALE2).astype(jnp.bfloat16).astype(jnp.float32)
    new_weight = jnp.exp2((new_scores - best) * SCALE2).astype(jnp.bfloat16).astype(jnp.float32)
    total = jnp.sum(weight, axis=1, keepdims=True) + jnp.sum(new_weight, axis=1, keepdims=True)
    moved = pltpu.roll(weight, KVH, 1).astype(jnp.bfloat16)
    new_moved = jnp.concatenate([new_weight[:, KVH:], new_weight[:, :KVH]], axis=1).astype(jnp.bfloat16)
    out_ref[...] = (dot(moved, cache) + dot(new_moved, new)) / total
    lse_ref[...] = jnp.broadcast_to(best * SCALE2 + log2(total), lse_ref.shape)


def fan_kernel(q_hbm, kv_hbm, cache_hbm, out_ref, q_ref, kv_ref, cache_ref, sems, fan_sems):
    pairs = [(q_hbm, q_ref), (cache_hbm, cache_ref), (kv_hbm, kv_ref)]
    loads = [pltpu.make_async_copy(source, target, sems.at[i]) for i, (source, target) in enumerate(pairs)]
    for load in loads:
        load.start()
    loads[0].wait()
    copies = [
        pltpu.make_async_copy(q_ref, out_ref.at[chip, :, group], fan_sems.at[chip, group])
        for chip in range(out_ref.shape[0])
        for group in range(out_ref.shape[2])
    ]
    for copy in copies:
        copy.start()
    for copy in copies + loads[1:]:
        copy.wait()


def merge_kernel(served, part_ref, suffix_ref, lse_ref, out_ref):
    part = part_ref[...].astype(jnp.float32)
    starts = range(0, len(served) * MESSAGE, MESSAGE)
    rows = [part[at : at + HALF] for at in starts]
    sums = unpack_stats([part[at + HALF : at + HALF + 1] for at in starts]).reshape(len(served), HALF, HD)
    blocks = []
    for block in range(H // HALF):
        span = slice(block * HALF, (block + 1) * HALF)
        own = [slot for slot, its in enumerate(served) if its == block]
        own_lse = lse_ref[span]
        best = own_lse
        for slot in own:
            best = jnp.maximum(best, sums[slot])
        total = jnp.exp2(own_lse - best)
        numerator = total * suffix_ref[span]
        for slot in own:
            factor = jnp.exp2(sums[slot] - best)
            total = total + factor
            numerator = numerator + factor * rows[slot]
        blocks.append(numerator / total)
    out_ref[0] = jnp.concatenate(blocks, axis=0).astype(jnp.bfloat16)


def call(kernel, name, outs, operands, specs=None, **cost):
    return pl.pallas_call(
        kernel,
        out_shape=outs,
        in_specs=specs or [VMEM] * len(operands),
        out_specs=jax.tree.map(lambda _: VMEM, outs),
        name=name,
        compiler_params=pltpu.CompilerParams(vmem_limit_bytes=LIMIT),
        cost_estimate=pl.CostEstimate(**cost) if cost else None,
    )(*operands)


def local(queries, prefix_kv, suffix_kv, new_kv, suffix_len):
    groups = lax.axis_size("grp")
    members = lax.axis_size("blk")
    per_head = members // KVH
    devices = groups * members
    span = prefix_kv.shape[2]
    cache_rows = suffix_kv.shape[1] * 2 * KVH
    chips = per_head // CORES
    order = [
        g * members + (head * chips + chip) * CORES + core
        for chip in range(chips)
        for head in range(KVH)
        for g in range(groups)
        for core in range(CORES)
    ]
    served = [device % members // per_head * CORES + device % CORES for device in order]

    def one(rows):
        return jax.ShapeDtypeStruct((rows, HD), jnp.float32)

    def half(*shape):
        return jax.ShapeDtypeStruct((*shape, HD), jnp.bfloat16)

    def exchange(array):
        return lax.all_to_all(array, ("grp", "blk"), 0, 0, axis_index_groups=[order], tiled=True)

    other = lax.ppermute(prefix_kv, "blk", [(i, i ^ 1) for i in range(members)]).reshape(2, span, HD)
    bound = [
        pltpu.with_memory_space_constraint(array, pltpu.HBM)
        for array in (
            queries.reshape(KVH, SHARE, HD),
            prefix_kv.reshape(2, span, HD),
            suffix_kv.reshape(cache_rows, HD),
        )
    ]
    outgoing, q, kv, cache = pl.pallas_call(
        fan_kernel,
        out_shape=[half(chips, KVH, groups, SHARE), half(KVH, SHARE), half(2, span), half(cache_rows)],
        in_specs=[pl.BlockSpec(memory_space=pltpu.HBM)] * 3,
        out_specs=[pl.BlockSpec(memory_space=pl.ANY), VMEM, VMEM, VMEM],
        scratch_shapes=[pltpu.SemaphoreType.DMA((3,)), pltpu.SemaphoreType.DMA((chips, groups))],
        name="fan",
        compiler_params=pltpu.CompilerParams(vmem_limit_bytes=LIMIT),
    )(*bound)
    arrived = exchange(outgoing.reshape(devices, HALF, HD)).reshape(devices * HALF, HD)
    suffix = call(
        suffix_kernel,
        "suffix",
        [one(H)] * 2,
        (suffix_len, new_kv.reshape(2 * KVH, HD), q, cache),
        [pl.BlockSpec(memory_space=pltpu.SMEM), VMEM, VMEM, VMEM],
        flops=70_000_000,
        bytes_accessed=600_000,
        transcendentals=140_000,
    )
    arrived, suffix = lax.optimization_barrier((arrived, suffix))
    partial = call(
        prefix_kernel,
        "prefix",
        half(devices * MESSAGE),
        (arrived, kv, other),
        flops=12 * devices * HALF * span * HD,
        bytes_accessed=1_600_000,
        transcendentals=2 * devices * HALF * span,
    )
    returned = exchange(partial.reshape(devices, MESSAGE // 2, 2, HD)).reshape(-1, HD)
    return call(
        functools.partial(merge_kernel, served),
        "merge",
        jax.ShapeDtypeStruct((1, H, HD), jnp.bfloat16),
        (returned, *suffix),
    )


def solution(mesh):
    in_specs = (
        P(("grp", "blk"), None, None),
        P(None, "grp", "blk", None),
        P(("grp", "blk"), None, None, None, None),
        P(("grp", "blk"), None, None, None),
        P(("grp", "blk")),
    )
    out_specs = P(("grp", "blk"), None, None)
    return jax.shard_map(local, mesh=mesh, in_specs=in_specs, out_specs=out_specs, check_vma=False)
```

```python
import functools
import math

import jax
import jax.numpy as jnp
from jax import lax
from jax.experimental import pallas as pl
from jax.experimental.pallas import tpu as pltpu
from jax.sharding import PartitionSpec as P

H = 64
KVH = 4
HD = 128
SHARE = H // KVH
SCALE2 = HD ** (-0.5) * math.log2(math.e)
VMEM = pl.BlockSpec(memory_space=pltpu.VMEM)
ROWS = 256
CHUNK = 512
CORES = 2
HALF = SHARE // CORES
MESSAGE = HALF + 2
LANES = HD // HALF
LIMIT = 24 * 1024 * 1024
NT = (((1,), (1,)), ((), ()))


def dot_nt(a, b):
    return lax.dot_general(a, b, NT, preferred_element_type=jnp.float32)


def dot(a, b):
    return jnp.dot(a, b, preferred_element_type=jnp.float32)


def log2(x):
    return jnp.log(x) * math.log2(math.e)


def pack_stats(x):
    hi = x.astype(jnp.bfloat16).astype(jnp.float32)
    rest = x - hi
    mid = rest.astype(jnp.bfloat16).astype(jnp.float32)
    low = rest - mid
    row = lax.broadcasted_iota(jnp.int32, x.shape, 1)
    lane = lax.broadcasted_iota(jnp.int32, x.shape, 2) - row * LANES
    return jnp.sum(jnp.where(lane == 0, hi, jnp.where(lane == 1, mid, jnp.where(lane == 2, low, 0.0))), axis=1)


def unpack_stats(rows):
    shape = (HALF, HD)
    mine = lax.broadcasted_iota(jnp.int32, shape, 1) // LANES == lax.broadcasted_iota(jnp.int32, shape, 0)
    pieces = [jnp.where(mine, jnp.broadcast_to(row, shape), 0.0) for row in rows]
    return dot(jnp.concatenate(pieces, axis=0).astype(jnp.bfloat16), jnp.ones((HD, HD), jnp.bfloat16))


def prefix_kernel(q_ref, kv_ref, other_ref, out_ref, message_ref):
    chunks = [(ref, at) for ref in (other_ref, kv_ref) for at in range(0, ref.shape[1], CHUNK)]

    def block(trip):
        rows = q_ref[pl.ds(trip * ROWS, ROWS)]

        def score(ref, first):
            return dot_nt(rows, ref[0, first : first + CHUNK])

        parts = []
        ahead = score(*chunks[0])
        for index, (ref, first) in enumerate(chunks):
            scores = ahead
            if index + 1 < len(chunks):
                ahead = score(*chunks[index + 1])
            best = jnp.max(scores, axis=1, keepdims=True)
            weight = jnp.exp2((scores - best) * SCALE2).astype(jnp.bfloat16)
            values = ref[1, first : first + CHUNK]
            parts.append((best, dot(weight, jnp.concatenate([values, jnp.ones_like(values)], axis=1))))
        best = functools.reduce(jnp.maximum, [part[0] for part in parts])
        both = sum(jnp.exp2((its - best) * SCALE2) * sums for its, sums in parts)
        total = both[:, HD:]
        result = both[:, :HD] / total
        slots = ROWS // HALF
        stats = pack_stats((best * SCALE2 + log2(total)).reshape(slots, HALF, HD))
        empty = jnp.zeros((1, HD), jnp.float32)
        for slot in range(slots):
            at = slot * MESSAGE
            message_ref[at : at + HALF] = result[slot * HALF : (slot + 1) * HALF]
            message_ref[at + HALF : at + MESSAGE] = jnp.concatenate([stats[slot : slot + 1], empty], axis=0)
        out_ref[pl.ds(trip * slots * MESSAGE, slots * MESSAGE)] = message_ref[...].astype(jnp.bfloat16)

    trips = q_ref.shape[0] // ROWS
    if trips == 1:
        block(0)
    else:

        def body(trip, unused):
            block(trip)
            return unused

        lax.fori_loop(0, trips, body, 0)


def owned(shape, limit):
    at = lax.broadcasted_iota(jnp.int32, shape, 1)
    head = lax.broadcasted_iota(jnp.int32, shape, 0) // SHARE
    return (at % (2 * KVH) == head) & (at < limit * (2 * KVH))


def suffix_kernel(len_ref, new_ref, q_ref, cache_ref, out_ref, lse_ref):
    q = q_ref[...].reshape(H, HD)
    cache = cache_ref[...]
    new = new_ref[...]
    raw = dot_nt(q, cache)
    scores = jnp.where(owned(raw.shape, len_ref[0]), raw, -jnp.inf)
    new_raw = dot_nt(q, new)
    new_scores = jnp.where(owned(new_raw.shape, 1), new_raw, -jnp.inf)
    best = jnp.maximum(jnp.max(scores, axis=1, keepdims=True), jnp.max(new_scores, axis=1, keepdims=True))
    weight = jnp.exp2((scores - best) * SCALE2).astype(jnp.bfloat16).astype(jnp.float32)
    new_weight = jnp.exp2((new_scores - best) * SCALE2).astype(jnp.bfloat16).astype(jnp.float32)
    total = jnp.sum(weight, axis=1, keepdims=True) + jnp.sum(new_weight, axis=1, keepdims=True)
    moved = pltpu.roll(weight, KVH, 1).astype(jnp.bfloat16)
    new_moved = jnp.concatenate([new_weight[:, KVH:], new_weight[:, :KVH]], axis=1).astype(jnp.bfloat16)
    out_ref[...] = (dot(moved, cache) + dot(new_moved, new)) / total
    lse_ref[...] = jnp.broadcast_to(best * SCALE2 + log2(total), lse_ref.shape)


def fan_kernel(q_hbm, kv_hbm, cache_hbm, out_ref, q_ref, kv_ref, cache_ref, sems, fan_sems):
    pairs = [(q_hbm, q_ref), (cache_hbm, cache_ref), (kv_hbm, kv_ref)]
    loads = [pltpu.make_async_copy(source, target, sems.at[i]) for i, (source, target) in enumerate(pairs)]
    for load in loads:
        load.start()
    loads[0].wait()
    copies = [
        pltpu.make_async_copy(q_ref, out_ref.at[group, :, chip], fan_sems.at[group, chip])
        for group in range(out_ref.shape[0])
        for chip in range(out_ref.shape[2])
    ]
    for copy in copies:
        copy.start()
    for copy in copies + loads[1:]:
        copy.wait()


def merge_kernel(served, part_ref, suffix_ref, lse_ref, out_ref, message_ref):
    message_ref[...] = part_ref[...].astype(jnp.float32)
    starts = range(0, len(served) * MESSAGE, MESSAGE)
    rows = [message_ref[at : at + HALF] for at in starts]
    sums = unpack_stats([message_ref[at + HALF : at + HALF + 1] for at in starts]).reshape(len(served), HALF, HD)
    blocks = []
    for block in range(H // HALF):
        span = slice(block * HALF, (block + 1) * HALF)
        own = [slot for slot, its in enumerate(served) if its == block]
        own_lse = lse_ref[span]
        best = own_lse
        for slot in own:
            best = jnp.maximum(best, sums[slot])
        total = jnp.exp2(own_lse - best)
        numerator = total * suffix_ref[span]
        for slot in own:
            factor = jnp.exp2(sums[slot] - best)
            total = total + factor
            numerator = numerator + factor * rows[slot]
        blocks.append(numerator / total)
    out_ref[0] = jnp.concatenate(blocks, axis=0).astype(jnp.bfloat16)


def call(kernel, name, outs, operands, specs=None, scratch=(), **cost):
    return pl.pallas_call(
        kernel,
        out_shape=outs,
        in_specs=specs or [VMEM] * len(operands),
        out_specs=jax.tree.map(lambda _: VMEM, outs),
        scratch_shapes=scratch,
        name=name,
        compiler_params=pltpu.CompilerParams(vmem_limit_bytes=LIMIT),
        cost_estimate=pl.CostEstimate(**cost) if cost else None,
    )(*operands)


def local(queries, prefix_kv, suffix_kv, new_kv, suffix_len):
    groups = lax.axis_size("grp")
    members = lax.axis_size("blk")
    per_head = members // KVH
    devices = groups * members
    span = prefix_kv.shape[2]
    cache_rows = suffix_kv.shape[1] * 2 * KVH
    chips = per_head // CORES
    served = [device % members // per_head * CORES + device % CORES for device in range(devices)]

    def one(rows):
        return jax.ShapeDtypeStruct((rows, HD), jnp.float32)

    def half(*shape):
        return jax.ShapeDtypeStruct((*shape, HD), jnp.bfloat16)

    def exchange(array):
        return lax.all_to_all(array, ("grp", "blk"), 0, 0, tiled=True)

    other = lax.ppermute(prefix_kv, "blk", [(i, i ^ 1) for i in range(members)]).reshape(2, span, HD)
    bound = [
        pltpu.with_memory_space_constraint(array, pltpu.HBM)
        for array in (
            queries.reshape(KVH, SHARE, HD),
            prefix_kv.reshape(2, span, HD),
            suffix_kv.reshape(cache_rows, HD),
        )
    ]
    outgoing, q, kv, cache = pl.pallas_call(
        fan_kernel,
        out_shape=[half(groups, KVH, chips, SHARE), half(KVH, SHARE), half(2, span), half(cache_rows)],
        in_specs=[pl.BlockSpec(memory_space=pltpu.HBM)] * 3,
        out_specs=[pl.BlockSpec(memory_space=pl.ANY), VMEM, VMEM, VMEM],
        scratch_shapes=[pltpu.SemaphoreType.DMA((3,)), pltpu.SemaphoreType.DMA((groups, chips))],
        name="fan",
        compiler_params=pltpu.CompilerParams(vmem_limit_bytes=LIMIT),
    )(*bound)
    arrived = exchange(outgoing.reshape(devices, HALF, HD)).reshape(devices * HALF, HD)
    suffix = call(
        suffix_kernel,
        "suffix",
        [one(H)] * 2,
        (suffix_len, new_kv.reshape(2 * KVH, HD), q, cache),
        [pl.BlockSpec(memory_space=pltpu.SMEM), VMEM, VMEM, VMEM],
        flops=70_000_000,
        bytes_accessed=600_000,
        transcendentals=140_000,
    )
    arrived, suffix = lax.optimization_barrier((arrived, suffix))
    partial = call(
        prefix_kernel,
        "prefix",
        half(devices * MESSAGE),
        (arrived, kv, other),
        scratch=[pltpu.VMEM((ROWS // HALF * MESSAGE, HD), jnp.float32)],
        flops=12 * devices * HALF * span * HD,
        bytes_accessed=1_600_000,
        transcendentals=2 * devices * HALF * span,
    )
    returned = exchange(partial.reshape(devices, MESSAGE // 2, 2, HD)).reshape(-1, HD)
    return call(
        functools.partial(merge_kernel, served),
        "merge",
        jax.ShapeDtypeStruct((1, H, HD), jnp.bfloat16),
        (returned, *suffix),
        scratch=[pltpu.VMEM((devices * MESSAGE, HD), jnp.float32)],
    )


def solution(mesh):
    in_specs = (
        P(("grp", "blk"), None, None),
        P(None, "grp", "blk", None),
        P(("grp", "blk"), None, None, None, None),
        P(("grp", "blk"), None, None, None),
        P(("grp", "blk")),
    )
    out_specs = P(("grp", "blk"), None, None)
    return jax.shard_map(local, mesh=mesh, in_specs=in_specs, out_specs=out_specs, check_vma=False)
```

```python
import functools
import math

import jax
import jax.numpy as jnp
from jax import lax
from jax.experimental import pallas as pl
from jax.experimental.pallas import tpu as pltpu
from jax.sharding import PartitionSpec as P

H = 64
KVH = 4
HD = 128
SHARE = H // KVH
SCALE2 = HD ** (-0.5) * math.log2(math.e)
VMEM = pl.BlockSpec(memory_space=pltpu.VMEM)
ROWS = 256
CHUNK = 512
CORES = 2
HALF = SHARE // CORES
MESSAGE = HALF + 2
LANES = HD // HALF
ONES = 16
LIMIT = 24 * 1024 * 1024
NT = (((1,), (1,)), ((), ()))


def dot_nt(a, b):
    return lax.dot_general(a, b, NT, preferred_element_type=jnp.float32)


def dot(a, b):
    return jnp.dot(a, b, preferred_element_type=jnp.float32)


def log2(x):
    return jnp.log(x) * math.log2(math.e)


def pack_stats(x):
    hi = x.astype(jnp.bfloat16).astype(jnp.float32)
    rest = x - hi
    mid = rest.astype(jnp.bfloat16).astype(jnp.float32)
    low = rest - mid
    row = lax.broadcasted_iota(jnp.int32, x.shape, 1)
    lane = lax.broadcasted_iota(jnp.int32, x.shape, 2) - row * LANES
    return jnp.sum(jnp.where(lane == 0, hi, jnp.where(lane == 1, mid, jnp.where(lane == 2, low, 0.0))), axis=1)


def unpack_stats(rows):
    shape = (HALF, HD)
    mine = lax.broadcasted_iota(jnp.int32, shape, 1) // LANES == lax.broadcasted_iota(jnp.int32, shape, 0)
    pieces = [jnp.where(mine, jnp.broadcast_to(row, shape), 0.0) for row in rows]
    return dot(jnp.concatenate(pieces, axis=0).astype(jnp.bfloat16), jnp.ones((HD, HD), jnp.bfloat16))


def prefix_kernel(q_ref, kv_ref, other_ref, values_ref, other_values_ref, out_ref):
    pairs = [(other_ref, other_values_ref), (kv_ref, values_ref)]
    chunks = [(ref, values, at) for ref, values in pairs for at in range(0, ref.shape[1], CHUNK)]

    def block(trip):
        rows = q_ref[pl.ds(trip * ROWS, ROWS)]

        def score(ref, values, first):
            return dot_nt(ref[0, first : first + CHUNK], rows)

        parts = []
        ahead = score(*chunks[0])
        for index, (ref, values, first) in enumerate(chunks):
            scores = ahead
            if index + 1 < len(chunks):
                ahead = score(*chunks[index + 1])
            best = jnp.max(scores, axis=0, keepdims=True)
            weight = jnp.exp2((scores - best) * SCALE2).astype(jnp.bfloat16)
            parts.append((best, dot(values[:, first : first + CHUNK], weight)))
        best = functools.reduce(jnp.maximum, [part[0] for part in parts])
        both = sum(jnp.exp2((its - best) * SCALE2) * sums for its, sums in parts)
        total = both[HD : HD + 1]
        result = (both[:HD] / total).T
        lse = jnp.broadcast_to(best * SCALE2 + log2(total), (HD, ROWS)).T
        slots = ROWS // HALF
        stats = pack_stats(lse.reshape(slots, HALF, HD))
        empty = jnp.zeros((1, HD), jnp.float32)
        pieces = []
        for slot in range(slots):
            pieces += [result[slot * HALF : (slot + 1) * HALF], stats[slot : slot + 1], empty]
        out_ref[pl.ds(trip * slots * MESSAGE, slots * MESSAGE)] = jnp.concatenate(pieces, axis=0).astype(jnp.bfloat16)

    trips = q_ref.shape[0] // ROWS
    if trips == 1:
        block(0)
    else:

        def body(trip, unused):
            block(trip)
            return unused

        lax.fori_loop(0, trips, body, 0)


def owned(shape, limit):
    at = lax.broadcasted_iota(jnp.int32, shape, 1)
    head = lax.broadcasted_iota(jnp.int32, shape, 0) // SHARE
    return (at % (2 * KVH) == head) & (at < limit * (2 * KVH))


def suffix_kernel(len_ref, new_ref, q_ref, cache_ref, kv_ref, other_ref, out_ref, lse_ref, values_ref, other_values_ref):
    for ref, transposed in ((kv_ref, values_ref), (other_ref, other_values_ref)):
        transposed[:HD] = ref[1].T
        transposed[HD:] = jnp.ones((ONES, ref.shape[1]), jnp.bfloat16)
    q = q_ref[...].reshape(H, HD)
    cache = cache_ref[...]
    new = new_ref[...]
    raw = dot_nt(q, cache)
    scores = jnp.where(owned(raw.shape, len_ref[0]), raw, -jnp.inf)
    new_raw = dot_nt(q, new)
    new_scores = jnp.where(owned(new_raw.shape, 1), new_raw, -jnp.inf)
    best = jnp.maximum(jnp.max(scores, axis=1, keepdims=True), jnp.max(new_scores, axis=1, keepdims=True))
    weight = jnp.exp2((scores - best) * SCALE2).astype(jnp.bfloat16).astype(jnp.float32)
    new_weight = jnp.exp2((new_scores - best) * SCALE2).astype(jnp.bfloat16).astype(jnp.float32)
    total = jnp.sum(weight, axis=1, keepdims=True) + jnp.sum(new_weight, axis=1, keepdims=True)
    moved = pltpu.roll(weight, KVH, 1).astype(jnp.bfloat16)
    new_moved = jnp.concatenate([new_weight[:, KVH:], new_weight[:, :KVH]], axis=1).astype(jnp.bfloat16)
    out_ref[...] = (dot(moved, cache) + dot(new_moved, new)) / total
    lse_ref[...] = jnp.broadcast_to(best * SCALE2 + log2(total), lse_ref.shape)


def fan_kernel(q_hbm, kv_hbm, cache_hbm, out_ref, q_ref, kv_ref, cache_ref, sems, fan_sems):
    pairs = [(q_hbm, q_ref), (cache_hbm, cache_ref), (kv_hbm, kv_ref)]
    loads = [pltpu.make_async_copy(source, target, sems.at[i]) for i, (source, target) in enumerate(pairs)]
    for load in loads:
        load.start()
    loads[0].wait()
    copies = [
        pltpu.make_async_copy(q_ref, out_ref.at[group, :, chip], fan_sems.at[group, chip])
        for group in range(out_ref.shape[0])
        for chip in range(out_ref.shape[2])
    ]
    for copy in copies:
        copy.start()
    for copy in copies + loads[1:]:
        copy.wait()


def merge_kernel(served, part_ref, suffix_ref, lse_ref, out_ref):
    part = part_ref[...].astype(jnp.float32)
    starts = range(0, len(served) * MESSAGE, MESSAGE)
    rows = [part[at : at + HALF] for at in starts]
    sums = unpack_stats([part[at + HALF : at + HALF + 1] for at in starts]).reshape(len(served), HALF, HD)
    blocks = []
    for block in range(H // HALF):
        span = slice(block * HALF, (block + 1) * HALF)
        own = [slot for slot, its in enumerate(served) if its == block]
        own_lse = lse_ref[span]
        best = own_lse
        for slot in own:
            best = jnp.maximum(best, sums[slot])
        total = jnp.exp2(own_lse - best)
        numerator = total * suffix_ref[span]
        for slot in own:
            factor = jnp.exp2(sums[slot] - best)
            total = total + factor
            numerator = numerator + factor * rows[slot]
        blocks.append(numerator / total)
    out_ref[0] = jnp.concatenate(blocks, axis=0).astype(jnp.bfloat16)


def call(kernel, name, outs, operands, specs=None, **cost):
    return pl.pallas_call(
        kernel,
        out_shape=outs,
        in_specs=specs or [VMEM] * len(operands),
        out_specs=jax.tree.map(lambda _: VMEM, outs),
        name=name,
        compiler_params=pltpu.CompilerParams(vmem_limit_bytes=LIMIT),
        cost_estimate=pl.CostEstimate(**cost) if cost else None,
    )(*operands)


def local(queries, prefix_kv, suffix_kv, new_kv, suffix_len):
    groups = lax.axis_size("grp")
    members = lax.axis_size("blk")
    per_head = members // KVH
    devices = groups * members
    span = prefix_kv.shape[2]
    cache_rows = suffix_kv.shape[1] * 2 * KVH
    chips = per_head // CORES
    served = [device % members // per_head * CORES + device % CORES for device in range(devices)]

    def one(rows):
        return jax.ShapeDtypeStruct((rows, HD), jnp.float32)

    def half(*shape):
        return jax.ShapeDtypeStruct((*shape, HD), jnp.bfloat16)

    def exchange(array):
        return lax.all_to_all(array, ("grp", "blk"), 0, 0, tiled=True)

    other = lax.ppermute(prefix_kv, "blk", [(i, i ^ 1) for i in range(members)]).reshape(2, span, HD)
    bound = [
        pltpu.with_memory_space_constraint(array, pltpu.HBM)
        for array in (
            queries.reshape(KVH, SHARE, HD),
            prefix_kv.reshape(2, span, HD),
            suffix_kv.reshape(cache_rows, HD),
        )
    ]
    outgoing, q, kv, cache = pl.pallas_call(
        fan_kernel,
        out_shape=[half(groups, KVH, chips, SHARE), half(KVH, SHARE), half(2, span), half(cache_rows)],
        in_specs=[pl.BlockSpec(memory_space=pltpu.HBM)] * 3,
        out_specs=[pl.BlockSpec(memory_space=pl.ANY), VMEM, VMEM, VMEM],
        scratch_shapes=[pltpu.SemaphoreType.DMA((3,)), pltpu.SemaphoreType.DMA((groups, chips))],
        name="fan",
        compiler_params=pltpu.CompilerParams(vmem_limit_bytes=LIMIT),
    )(*bound)
    arrived = exchange(outgoing.reshape(devices, HALF, HD)).reshape(devices * HALF, HD)
    transposed = jax.ShapeDtypeStruct((HD + ONES, span), jnp.bfloat16)
    suffix = call(
        suffix_kernel,
        "suffix",
        [one(H), one(H), transposed, transposed],
        (suffix_len, new_kv.reshape(2 * KVH, HD), q, cache, kv, other),
        [pl.BlockSpec(memory_space=pltpu.SMEM)] + [VMEM] * 5,
        flops=70_000_000,
        bytes_accessed=600_000,
        transcendentals=140_000,
    )
    arrived, suffix = lax.optimization_barrier((arrived, suffix))
    partial = call(
        prefix_kernel,
        "prefix",
        half(devices * MESSAGE),
        (arrived, kv, other, *suffix[2:]),
        flops=12 * devices * HALF * span * HD,
        bytes_accessed=1_600_000,
        transcendentals=2 * devices * HALF * span,
    )
    returned = exchange(partial.reshape(devices, MESSAGE // 2, 2, HD)).reshape(-1, HD)
    return call(
        functools.partial(merge_kernel, served),
        "merge",
        jax.ShapeDtypeStruct((1, H, HD), jnp.bfloat16),
        (returned, *suffix[:2]),
    )


def solution(mesh):
    in_specs = (
        P(("grp", "blk"), None, None),
        P(None, "grp", "blk", None),
        P(("grp", "blk"), None, None, None, None),
        P(("grp", "blk"), None, None, None),
        P(("grp", "blk")),
    )
    out_specs = P(("grp", "blk"), None, None)
    return jax.shard_map(local, mesh=mesh, in_specs=in_specs, out_specs=out_specs, check_vma=False)
```

```python
import functools
import math

import jax
import jax.numpy as jnp
from jax import lax
from jax.experimental import pallas as pl
from jax.experimental.pallas import tpu as pltpu
from jax.sharding import PartitionSpec as P

H = 64
KVH = 4
HD = 128
SHARE = H // KVH
SCALE2 = HD ** (-0.5) * math.log2(math.e)
VMEM = pl.BlockSpec(memory_space=pltpu.VMEM)
ROWS = 256
EDGE = 256
CORES = 2
HALF = SHARE // CORES
MESSAGE = HALF + 2
LANES = HD // HALF
LIMIT = 24 * 1024 * 1024
NT = (((1,), (1,)), ((), ()))


def dot_nt(a, b):
    return lax.dot_general(a, b, NT, preferred_element_type=jnp.float32)


def dot(a, b):
    return jnp.dot(a, b, preferred_element_type=jnp.float32)


def log2(x):
    return jnp.log(x) * math.log2(math.e)


def pack_stats(x):
    hi = x.astype(jnp.bfloat16).astype(jnp.float32)
    rest = x - hi
    mid = rest.astype(jnp.bfloat16).astype(jnp.float32)
    low = rest - mid
    row = lax.broadcasted_iota(jnp.int32, x.shape, 1)
    lane = lax.broadcasted_iota(jnp.int32, x.shape, 2) - row * LANES
    return jnp.sum(jnp.where(lane == 0, hi, jnp.where(lane == 1, mid, jnp.where(lane == 2, low, 0.0))), axis=1)


def unpack_stats(rows):
    shape = (HALF, HD)
    mine = lax.broadcasted_iota(jnp.int32, shape, 1) // LANES == lax.broadcasted_iota(jnp.int32, shape, 0)
    pieces = [jnp.where(mine, jnp.broadcast_to(row, shape), 0.0) for row in rows]
    return dot(jnp.concatenate(pieces, axis=0).astype(jnp.bfloat16), jnp.ones((HD, HD), jnp.bfloat16))


def prefix_kernel(q_ref, kv_ref, other_ref, out_ref):
    span = kv_ref.shape[1]
    chunks = [
        (other_ref, slice(0, EDGE)),
        (other_ref, slice(EDGE, span)),
        (kv_ref, slice(0, span - EDGE)),
        (kv_ref, slice(span - EDGE, span)),
    ]

    def block(trip):
        rows = q_ref[pl.ds(trip * ROWS, ROWS)]

        def score(ref, positions):
            return dot_nt(rows, ref[0, positions])

        parts = []
        ahead = score(*chunks[0])
        for index, (ref, positions) in enumerate(chunks):
            scores = ahead
            if index + 1 < len(chunks):
                ahead = score(*chunks[index + 1])
            best = jnp.max(scores, axis=1, keepdims=True)
            weight = jnp.exp2((scores - best) * SCALE2).astype(jnp.bfloat16)
            values = ref[1, positions]
            parts.append((best, dot(weight, jnp.concatenate([values, jnp.ones_like(values)], axis=1))))
        best = functools.reduce(jnp.maximum, [part[0] for part in parts])
        both = sum(jnp.exp2((its - best) * SCALE2) * sums for its, sums in parts)
        total = both[:, HD:]
        result = both[:, :HD] / total
        slots = ROWS // HALF
        stats = pack_stats((best * SCALE2 + log2(total)).reshape(slots, HALF, HD))
        empty = jnp.zeros((1, HD), jnp.float32)
        pieces = []
        for slot in range(slots):
            pieces += [result[slot * HALF : (slot + 1) * HALF], stats[slot : slot + 1], empty]
        out_ref[pl.ds(trip * slots * MESSAGE, slots * MESSAGE)] = jnp.concatenate(pieces, axis=0).astype(jnp.bfloat16)

    trips = q_ref.shape[0] // ROWS
    if trips == 1:
        block(0)
    else:

        def body(trip, unused):
            block(trip)
            return unused

        lax.fori_loop(0, trips, body, 0)


def owned(shape, limit):
    at = lax.broadcasted_iota(jnp.int32, shape, 1)
    head = lax.broadcasted_iota(jnp.int32, shape, 0) // SHARE
    return (at % (2 * KVH) == head) & (at < limit * (2 * KVH))


def suffix_kernel(len_ref, new_ref, q_ref, cache_ref, out_ref, lse_ref):
    q = q_ref[...].reshape(H, HD)
    cache = cache_ref[...]
    new = new_ref[...]
    raw = dot_nt(q, cache)
    scores = jnp.where(owned(raw.shape, len_ref[0]), raw, -jnp.inf)
    new_raw = dot_nt(q, new)
    new_scores = jnp.where(owned(new_raw.shape, 1), new_raw, -jnp.inf)
    best = jnp.maximum(jnp.max(scores, axis=1, keepdims=True), jnp.max(new_scores, axis=1, keepdims=True))
    weight = jnp.exp2((scores - best) * SCALE2).astype(jnp.bfloat16).astype(jnp.float32)
    new_weight = jnp.exp2((new_scores - best) * SCALE2).astype(jnp.bfloat16).astype(jnp.float32)
    total = jnp.sum(weight, axis=1, keepdims=True) + jnp.sum(new_weight, axis=1, keepdims=True)
    moved = pltpu.roll(weight, KVH, 1).astype(jnp.bfloat16)
    new_moved = jnp.concatenate([new_weight[:, KVH:], new_weight[:, :KVH]], axis=1).astype(jnp.bfloat16)
    out_ref[...] = (dot(moved, cache) + dot(new_moved, new)) / total
    lse_ref[...] = jnp.broadcast_to(best * SCALE2 + log2(total), lse_ref.shape)


def fan_kernel(q_hbm, kv_hbm, cache_hbm, out_ref, q_ref, kv_ref, cache_ref, sems, fan_sems):
    pairs = [(q_hbm, q_ref), (cache_hbm, cache_ref), (kv_hbm, kv_ref)]
    loads = [pltpu.make_async_copy(source, target, sems.at[i]) for i, (source, target) in enumerate(pairs)]
    for load in loads:
        load.start()
    loads[0].wait()
    copies = [
        pltpu.make_async_copy(q_ref, out_ref.at[group, :, chip], fan_sems.at[group, chip])
        for group in range(out_ref.shape[0])
        for chip in range(out_ref.shape[2])
    ]
    for copy in copies:
        copy.start()
    for copy in copies + loads[1:]:
        copy.wait()


def merge_kernel(served, part_ref, suffix_ref, lse_ref, out_ref):
    part = part_ref[...].astype(jnp.float32)
    starts = range(0, len(served) * MESSAGE, MESSAGE)
    rows = [part[at : at + HALF] for at in starts]
    sums = unpack_stats([part[at + HALF : at + HALF + 1] for at in starts]).reshape(len(served), HALF, HD)
    blocks = []
    for block in range(H // HALF):
        span = slice(block * HALF, (block + 1) * HALF)
        own = [slot for slot, its in enumerate(served) if its == block]
        own_lse = lse_ref[span]
        best = own_lse
        for slot in own:
            best = jnp.maximum(best, sums[slot])
        total = jnp.exp2(own_lse - best)
        numerator = total * suffix_ref[span]
        for slot in own:
            factor = jnp.exp2(sums[slot] - best)
            total = total + factor
            numerator = numerator + factor * rows[slot]
        blocks.append(numerator / total)
    out_ref[0] = jnp.concatenate(blocks, axis=0).astype(jnp.bfloat16)


def call(kernel, name, outs, operands, specs=None, **cost):
    return pl.pallas_call(
        kernel,
        out_shape=outs,
        in_specs=specs or [VMEM] * len(operands),
        out_specs=jax.tree.map(lambda _: VMEM, outs),
        name=name,
        compiler_params=pltpu.CompilerParams(vmem_limit_bytes=LIMIT),
        cost_estimate=pl.CostEstimate(**cost) if cost else None,
    )(*operands)


def local(queries, prefix_kv, suffix_kv, new_kv, suffix_len):
    groups = lax.axis_size("grp")
    members = lax.axis_size("blk")
    per_head = members // KVH
    devices = groups * members
    span = prefix_kv.shape[2]
    cache_rows = suffix_kv.shape[1] * 2 * KVH
    chips = per_head // CORES
    served = [device % members // per_head * CORES + device % CORES for device in range(devices)]

    def one(rows):
        return jax.ShapeDtypeStruct((rows, HD), jnp.float32)

    def half(*shape):
        return jax.ShapeDtypeStruct((*shape, HD), jnp.bfloat16)

    def exchange(array):
        return lax.all_to_all(array, ("grp", "blk"), 0, 0, tiled=True)

    other = lax.ppermute(prefix_kv, "blk", [(i, i ^ 1) for i in range(members)]).reshape(2, span, HD)
    bound = [
        pltpu.with_memory_space_constraint(array, pltpu.HBM)
        for array in (
            queries.reshape(KVH, SHARE, HD),
            prefix_kv.reshape(2, span, HD),
            suffix_kv.reshape(cache_rows, HD),
        )
    ]
    outgoing, q, kv, cache = pl.pallas_call(
        fan_kernel,
        out_shape=[half(groups, KVH, chips, SHARE), half(KVH, SHARE), half(2, span), half(cache_rows)],
        in_specs=[pl.BlockSpec(memory_space=pltpu.HBM)] * 3,
        out_specs=[pl.BlockSpec(memory_space=pl.ANY), VMEM, VMEM, VMEM],
        scratch_shapes=[pltpu.SemaphoreType.DMA((3,)), pltpu.SemaphoreType.DMA((groups, chips))],
        name="fan",
        compiler_params=pltpu.CompilerParams(vmem_limit_bytes=LIMIT),
    )(*bound)
    arrived = exchange(outgoing.reshape(devices, HALF, HD)).reshape(devices * HALF, HD)
    suffix = call(
        suffix_kernel,
        "suffix",
        [one(H)] * 2,
        (suffix_len, new_kv.reshape(2 * KVH, HD), q, cache),
        [pl.BlockSpec(memory_space=pltpu.SMEM), VMEM, VMEM, VMEM],
        flops=70_000_000,
        bytes_accessed=600_000,
        transcendentals=140_000,
    )
    arrived, suffix = lax.optimization_barrier((arrived, suffix))
    partial = call(
        prefix_kernel,
        "prefix",
        half(devices * MESSAGE),
        (arrived, kv, other),
        flops=12 * devices * HALF * span * HD,
        bytes_accessed=1_600_000,
        transcendentals=2 * devices * HALF * span,
    )
    returned = exchange(partial.reshape(devices, MESSAGE // 2, 2, HD)).reshape(-1, HD)
    return call(
        functools.partial(merge_kernel, served),
        "merge",
        jax.ShapeDtypeStruct((1, H, HD), jnp.bfloat16),
        (returned, *suffix),
    )


def solution(mesh):
    in_specs = (
        P(("grp", "blk"), None, None),
        P(None, "grp", "blk", None),
        P(("grp", "blk"), None, None, None, None),
        P(("grp", "blk"), None, None, None),
        P(("grp", "blk")),
    )
    out_specs = P(("grp", "blk"), None, None)
    return jax.shard_map(local, mesh=mesh, in_specs=in_specs, out_specs=out_specs, check_vma=False)
```

```python
import functools
import math

import jax
import jax.numpy as jnp
from jax import lax
from jax.experimental import pallas as pl
from jax.experimental.pallas import tpu as pltpu
from jax.sharding import PartitionSpec as P

H = 64
KVH = 4
HD = 128
SHARE = H // KVH
SCALE2 = HD ** (-0.5) * math.log2(math.e)
VMEM = pl.BlockSpec(memory_space=pltpu.VMEM)
ROWS = 256
CHUNK = 512
CORES = 2
HALF = SHARE // CORES
MESSAGE = HALF + 2
LANES = HD // HALF
LIMIT = 24 * 1024 * 1024
NT = (((1,), (1,)), ((), ()))


def dot_nt(a, b):
    return lax.dot_general(a, b, NT, preferred_element_type=jnp.float32)


def dot(a, b):
    return jnp.dot(a, b, preferred_element_type=jnp.float32)


def log2(x):
    return jnp.log(x) * math.log2(math.e)


def pack_stats(x):
    hi = x.astype(jnp.bfloat16).astype(jnp.float32)
    rest = x - hi
    mid = rest.astype(jnp.bfloat16).astype(jnp.float32)
    low = rest - mid
    row = lax.broadcasted_iota(jnp.int32, x.shape, 1)
    lane = lax.broadcasted_iota(jnp.int32, x.shape, 2) - row * LANES
    return jnp.sum(jnp.where(lane == 0, hi, jnp.where(lane == 1, mid, jnp.where(lane == 2, low, 0.0))), axis=1)


def unpack_stats(rows):
    shape = (HALF, HD)
    mine = lax.broadcasted_iota(jnp.int32, shape, 1) // LANES == lax.broadcasted_iota(jnp.int32, shape, 0)
    pieces = [jnp.where(mine, jnp.broadcast_to(row, shape), 0.0) for row in rows]
    return dot(jnp.concatenate(pieces, axis=0).astype(jnp.bfloat16), jnp.ones((HD, HD), jnp.bfloat16))


def prefix_kernel(q_ref, kv_ref, other_ref, out_ref):
    chunks = [(ref, at) for ref in (other_ref, kv_ref) for at in range(0, ref.shape[1], CHUNK)]

    def block(trip):
        rows = q_ref[pl.ds(trip * ROWS, ROWS)]

        def score(ref, first):
            return dot_nt(rows, ref[0, first : first + CHUNK])

        parts = []
        ahead = score(*chunks[0])
        for index, (ref, first) in enumerate(chunks):
            scores = ahead
            if index + 1 < len(chunks):
                ahead = score(*chunks[index + 1])
            best = jnp.max(scores, axis=1, keepdims=True)
            weight = jnp.exp2((scores - best) * SCALE2).astype(jnp.bfloat16)
            values = ref[1, first : first + CHUNK]
            parts.append((best, dot(weight, jnp.concatenate([values, jnp.ones_like(values)], axis=1))))
        best = functools.reduce(jnp.maximum, [part[0] for part in parts])
        both = sum(jnp.exp2((its - best) * SCALE2) * sums for its, sums in parts)
        total = both[:, HD:]
        result = both[:, :HD] / total
        slots = ROWS // HALF
        stats = pack_stats((best * SCALE2 + log2(total)).reshape(slots, HALF, HD))
        empty = jnp.zeros((1, HD), jnp.float32)
        pieces = []
        for slot in range(slots):
            pieces += [result[slot * HALF : (slot + 1) * HALF], stats[slot : slot + 1], empty]
        out_ref[pl.ds(trip * slots * MESSAGE, slots * MESSAGE)] = jnp.concatenate(pieces, axis=0).astype(jnp.bfloat16)

    trips = q_ref.shape[0] // ROWS
    if trips == 1:
        block(0)
    else:

        def body(trip, unused):
            block(trip)
            return unused

        lax.fori_loop(0, trips, body, 0)


def owned(shape, limit):
    at = lax.broadcasted_iota(jnp.int32, shape, 1)
    head = lax.broadcasted_iota(jnp.int32, shape, 0) // SHARE
    return (at % (2 * KVH) == head) & (at < limit * (2 * KVH))


def suffix_kernel(len_ref, new_ref, q_ref, cache_ref, out_ref, lse_ref):
    q = q_ref[...].reshape(H, HD)
    cache = cache_ref[...]
    new = new_ref[...]
    raw = dot_nt(q, cache)
    scores = jnp.where(owned(raw.shape, len_ref[0]), raw, -jnp.inf)
    new_raw = dot_nt(q, new)
    new_scores = jnp.where(owned(new_raw.shape, 1), new_raw, -jnp.inf)
    best = jnp.maximum(jnp.max(scores, axis=1, keepdims=True), jnp.max(new_scores, axis=1, keepdims=True))
    weight = jnp.exp2((scores - best) * SCALE2).astype(jnp.bfloat16).astype(jnp.float32)
    new_weight = jnp.exp2((new_scores - best) * SCALE2).astype(jnp.bfloat16).astype(jnp.float32)
    total = jnp.sum(weight, axis=1, keepdims=True) + jnp.sum(new_weight, axis=1, keepdims=True)
    moved = pltpu.roll(weight, KVH, 1).astype(jnp.bfloat16)
    new_moved = jnp.concatenate([new_weight[:, KVH:], new_weight[:, :KVH]], axis=1).astype(jnp.bfloat16)
    out_ref[...] = (dot(moved, cache) + dot(new_moved, new)) / total
    lse_ref[...] = jnp.broadcast_to(best * SCALE2 + log2(total), lse_ref.shape)


def fan_kernel(q_hbm, kv_hbm, cache_hbm, out_ref, q_ref, kv_ref, cache_ref, sems, fan_sems):
    pairs = [(q_hbm, q_ref), (cache_hbm, cache_ref), (kv_hbm, kv_ref)]
    loads = [pltpu.make_async_copy(source, target, sems.at[i]) for i, (source, target) in enumerate(pairs)]
    for load in loads:
        load.start()
    loads[0].wait()
    copies = [
        pltpu.make_async_copy(q_ref, out_ref.at[group, :, chip], fan_sems.at[group, chip])
        for group in range(out_ref.shape[0])
        for chip in range(out_ref.shape[2])
    ]
    for copy in copies:
        copy.start()
    for copy in copies + loads[1:]:
        copy.wait()


def merge_kernel(served, part_ref, suffix_ref, lse_ref, out_ref):
    part = part_ref[...].astype(jnp.float32)
    starts = range(0, len(served) * MESSAGE, MESSAGE)
    rows = [part[at : at + HALF] for at in starts]
    sums = unpack_stats([part[at + HALF : at + HALF + 1] for at in starts]).reshape(len(served), HALF, HD)
    blocks = []
    for block in range(H // HALF):
        span = slice(block * HALF, (block + 1) * HALF)
        own = [slot for slot, its in enumerate(served) if its == block]
        own_lse = lse_ref[span]
        best = own_lse
        for slot in own:
            best = jnp.maximum(best, sums[slot])
        total = jnp.exp2(own_lse - best)
        numerator = total * suffix_ref[span]
        for slot in own:
            factor = jnp.exp2(sums[slot] - best)
            total = total + factor
            numerator = numerator + factor * rows[slot]
        blocks.append(numerator / total)
    out_ref[0] = jnp.concatenate(blocks, axis=0).astype(jnp.bfloat16)


def call(kernel, name, outs, operands, specs=None, **cost):
    return pl.pallas_call(
        kernel,
        out_shape=outs,
        in_specs=specs or [VMEM] * len(operands),
        out_specs=jax.tree.map(lambda _: VMEM, outs),
        name=name,
        compiler_params=pltpu.CompilerParams(vmem_limit_bytes=LIMIT),
        cost_estimate=pl.CostEstimate(**cost) if cost else None,
    )(*operands)


def local(queries, prefix_kv, suffix_kv, new_kv, suffix_len):
    groups = lax.axis_size("grp")
    members = lax.axis_size("blk")
    per_head = members // KVH
    devices = groups * members
    span = prefix_kv.shape[2]
    cache_rows = suffix_kv.shape[1] * 2 * KVH
    chips = per_head // CORES
    served = [device % members // per_head * CORES + device % CORES for device in range(devices)]

    def one(rows):
        return jax.ShapeDtypeStruct((rows, HD), jnp.float32)

    def half(*shape):
        return jax.ShapeDtypeStruct((*shape, HD), jnp.bfloat16)

    def exchange(array):
        return lax.all_to_all(array, ("grp", "blk"), 0, 0, tiled=True)

    bound = [
        pltpu.with_memory_space_constraint(array, pltpu.HBM)
        for array in (
            queries.reshape(KVH, SHARE, HD),
            prefix_kv.reshape(2, span, HD),
            suffix_kv.reshape(cache_rows, HD),
        )
    ]
    outgoing, q, kv, cache = pl.pallas_call(
        fan_kernel,
        out_shape=[half(groups, KVH, chips, SHARE), half(KVH, SHARE), half(2, span), half(cache_rows)],
        in_specs=[pl.BlockSpec(memory_space=pltpu.HBM)] * 3,
        out_specs=[pl.BlockSpec(memory_space=pl.ANY), VMEM, VMEM, VMEM],
        scratch_shapes=[pltpu.SemaphoreType.DMA((3,)), pltpu.SemaphoreType.DMA((groups, chips))],
        name="fan",
        compiler_params=pltpu.CompilerParams(vmem_limit_bytes=LIMIT),
    )(*bound)
    arrived = exchange(outgoing.reshape(devices, HALF, HD)).reshape(devices * HALF, HD)
    other = lax.ppermute(kv, "blk", [(i, i ^ 1) for i in range(members)])
    suffix = call(
        suffix_kernel,
        "suffix",
        [one(H)] * 2,
        (suffix_len, new_kv.reshape(2 * KVH, HD), q, cache),
        [pl.BlockSpec(memory_space=pltpu.SMEM), VMEM, VMEM, VMEM],
        flops=20_000_000_000,
        bytes_accessed=600_000,
        transcendentals=140_000,
    )
    arrived, suffix = lax.optimization_barrier((arrived, suffix))
    partial = call(
        prefix_kernel,
        "prefix",
        half(devices * MESSAGE),
        (arrived, kv, other),
        flops=12 * devices * HALF * span * HD,
        bytes_accessed=1_600_000,
        transcendentals=2 * devices * HALF * span,
    )
    returned = exchange(partial.reshape(devices, MESSAGE // 2, 2, HD)).reshape(-1, HD)
    return call(
        functools.partial(merge_kernel, served),
        "merge",
        jax.ShapeDtypeStruct((1, H, HD), jnp.bfloat16),
        (returned, *suffix),
    )


def solution(mesh):
    in_specs = (
        P(("grp", "blk"), None, None),
        P(None, "grp", "blk", None),
        P(("grp", "blk"), None, None, None, None),
        P(("grp", "blk"), None, None, None),
        P(("grp", "blk")),
    )
    out_specs = P(("grp", "blk"), None, None)
    return jax.shard_map(local, mesh=mesh, in_specs=in_specs, out_specs=out_specs, check_vma=False)
```

```python
import functools
import math

import jax
import jax.numpy as jnp
from jax import lax
from jax.experimental import pallas as pl
from jax.experimental.pallas import tpu as pltpu
from jax.sharding import PartitionSpec as P

H = 64
KVH = 4
HD = 128
SHARE = H // KVH
SCALE2 = HD ** (-0.5) * math.log2(math.e)
VMEM = pl.BlockSpec(memory_space=pltpu.VMEM)
ROWS = 256
EDGE = 256
CORES = 2
HALF = SHARE // CORES
MESSAGE = HALF + 2
LANES = HD // HALF
LIMIT = 24 * 1024 * 1024
NT = (((1,), (1,)), ((), ()))


def dot_nt(a, b):
    return lax.dot_general(a, b, NT, preferred_element_type=jnp.float32)


def dot(a, b):
    return jnp.dot(a, b, preferred_element_type=jnp.float32)


def log2(x):
    return jnp.log(x) * math.log2(math.e)


def pack_stats(x):
    hi = x.astype(jnp.bfloat16).astype(jnp.float32)
    rest = x - hi
    mid = rest.astype(jnp.bfloat16).astype(jnp.float32)
    low = rest - mid
    row = lax.broadcasted_iota(jnp.int32, x.shape, 1)
    lane = lax.broadcasted_iota(jnp.int32, x.shape, 2) - row * LANES
    return jnp.sum(jnp.where(lane == 0, hi, jnp.where(lane == 1, mid, jnp.where(lane == 2, low, 0.0))), axis=1)


def unpack_stats(rows):
    shape = (HALF, HD)
    mine = lax.broadcasted_iota(jnp.int32, shape, 1) // LANES == lax.broadcasted_iota(jnp.int32, shape, 0)
    pieces = [jnp.where(mine, jnp.broadcast_to(row, shape), 0.0) for row in rows]
    return dot(jnp.concatenate(pieces, axis=0).astype(jnp.bfloat16), jnp.ones((HD, HD), jnp.bfloat16))


def prefix_kernel(q_ref, kv_ref, other_ref, out_ref):
    span = kv_ref.shape[1]
    chunks = [
        (other_ref, slice(0, EDGE)),
        (other_ref, slice(EDGE, span)),
        (kv_ref, slice(0, span - EDGE)),
        (kv_ref, slice(span - EDGE, span)),
    ]

    def block(trip):
        rows = q_ref[pl.ds(trip * ROWS, ROWS)]

        def score(ref, positions):
            return dot_nt(rows, ref[0, positions])

        parts = []
        ahead = score(*chunks[0])
        for index, (ref, positions) in enumerate(chunks):
            scores = ahead
            if index + 1 < len(chunks):
                ahead = score(*chunks[index + 1])
            best = jnp.max(scores, axis=1, keepdims=True)
            weight = jnp.exp2((scores - best) * SCALE2).astype(jnp.bfloat16)
            values = ref[1, positions]
            parts.append((best, dot(weight, jnp.concatenate([values, jnp.ones_like(values)], axis=1))))
        best = functools.reduce(jnp.maximum, [part[0] for part in parts])
        both = sum(jnp.exp2((its - best) * SCALE2) * sums for its, sums in parts)
        total = both[:, HD:]
        result = both[:, :HD] / total
        slots = ROWS // HALF
        stats = pack_stats((best * SCALE2 + log2(total)).reshape(slots, HALF, HD))
        empty = jnp.zeros((1, HD), jnp.float32)
        pieces = []
        for slot in range(slots):
            pieces += [result[slot * HALF : (slot + 1) * HALF], stats[slot : slot + 1], empty]
        out_ref[pl.ds(trip * slots * MESSAGE, slots * MESSAGE)] = jnp.concatenate(pieces, axis=0).astype(jnp.bfloat16)

    trips = q_ref.shape[0] // ROWS
    if trips == 1:
        block(0)
    else:

        def body(trip, unused):
            block(trip)
            return unused

        lax.fori_loop(0, trips, body, 0)


def owned(shape, limit):
    at = lax.broadcasted_iota(jnp.int32, shape, 1)
    head = lax.broadcasted_iota(jnp.int32, shape, 0) // SHARE
    return (at % (2 * KVH) == head) & (at < limit * (2 * KVH))


def suffix_kernel(len_ref, new_ref, q_ref, cache_ref, out_ref, lse_ref):
    q = q_ref[...].reshape(H, HD)
    cache = cache_ref[...]
    new = new_ref[...]
    raw = dot_nt(q, cache)
    scores = jnp.where(owned(raw.shape, len_ref[0]), raw, -jnp.inf)
    new_raw = dot_nt(q, new)
    new_scores = jnp.where(owned(new_raw.shape, 1), new_raw, -jnp.inf)
    best = jnp.maximum(jnp.max(scores, axis=1, keepdims=True), jnp.max(new_scores, axis=1, keepdims=True))
    weight = jnp.exp2((scores - best) * SCALE2).astype(jnp.bfloat16).astype(jnp.float32)
    new_weight = jnp.exp2((new_scores - best) * SCALE2).astype(jnp.bfloat16).astype(jnp.float32)
    total = jnp.sum(weight, axis=1, keepdims=True) + jnp.sum(new_weight, axis=1, keepdims=True)
    moved = pltpu.roll(weight, KVH, 1).astype(jnp.bfloat16)
    new_moved = jnp.concatenate([new_weight[:, KVH:], new_weight[:, :KVH]], axis=1).astype(jnp.bfloat16)
    out_ref[...] = (dot(moved, cache) + dot(new_moved, new)) / total
    lse_ref[...] = jnp.broadcast_to(best * SCALE2 + log2(total), lse_ref.shape)


def fan_kernel(q_hbm, kv_hbm, cache_hbm, out_ref, q_ref, kv_ref, cache_ref, sems, fan_sems):
    pairs = [(q_hbm, q_ref), (cache_hbm, cache_ref), (kv_hbm, kv_ref)]
    loads = [pltpu.make_async_copy(source, target, sems.at[i]) for i, (source, target) in enumerate(pairs)]
    for load in loads:
        load.start()
    loads[0].wait()
    copies = [
        pltpu.make_async_copy(q_ref, out_ref.at[group, :, chip], fan_sems.at[group, chip])
        for group in range(out_ref.shape[0])
        for chip in range(out_ref.shape[2])
    ]
    for copy in copies:
        copy.start()
    for copy in copies + loads[1:]:
        copy.wait()


def merge_kernel(served, part_ref, suffix_ref, lse_ref, out_ref):
    part = part_ref[...].astype(jnp.float32)
    starts = range(0, len(served) * MESSAGE, MESSAGE)
    rows = [part[at : at + HALF] for at in starts]
    sums = unpack_stats([part[at + HALF : at + HALF + 1] for at in starts]).reshape(len(served), HALF, HD)
    blocks = []
    for block in range(H // HALF):
        span = slice(block * HALF, (block + 1) * HALF)
        own = [slot for slot, its in enumerate(served) if its == block]
        own_lse = lse_ref[span]
        best = own_lse
        for slot in own:
            best = jnp.maximum(best, sums[slot])
        total = jnp.exp2(own_lse - best)
        numerator = total * suffix_ref[span]
        for slot in own:
            factor = jnp.exp2(sums[slot] - best)
            total = total + factor
            numerator = numerator + factor * rows[slot]
        blocks.append(numerator / total)
    out_ref[0] = jnp.concatenate(blocks, axis=0).astype(jnp.bfloat16)


def call(kernel, name, outs, operands, specs=None, **cost):
    return pl.pallas_call(
        kernel,
        out_shape=outs,
        in_specs=specs or [VMEM] * len(operands),
        out_specs=jax.tree.map(lambda _: VMEM, outs),
        name=name,
        compiler_params=pltpu.CompilerParams(vmem_limit_bytes=LIMIT),
        cost_estimate=pl.CostEstimate(**cost) if cost else None,
    )(*operands)


def local(queries, prefix_kv, suffix_kv, new_kv, suffix_len):
    groups = lax.axis_size("grp")
    members = lax.axis_size("blk")
    per_head = members // KVH
    devices = groups * members
    span = prefix_kv.shape[2]
    cache_rows = suffix_kv.shape[1] * 2 * KVH
    chips = per_head // CORES
    served = [device % members // per_head * CORES + device % CORES for device in range(devices)]

    def one(rows):
        return jax.ShapeDtypeStruct((rows, HD), jnp.float32)

    def half(*shape):
        return jax.ShapeDtypeStruct((*shape, HD), jnp.bfloat16)

    def exchange(array):
        return lax.all_to_all(array, ("grp", "blk"), 0, 0, tiled=True)

    bound = [
        pltpu.with_memory_space_constraint(array, pltpu.HBM)
        for array in (
            queries.reshape(KVH, SHARE, HD),
            prefix_kv.reshape(2, span, HD),
            suffix_kv.reshape(cache_rows, HD),
        )
    ]
    outgoing, q, kv, cache = pl.pallas_call(
        fan_kernel,
        out_shape=[half(groups, KVH, chips, SHARE), half(KVH, SHARE), half(2, span), half(cache_rows)],
        in_specs=[pl.BlockSpec(memory_space=pltpu.HBM)] * 3,
        out_specs=[pl.BlockSpec(memory_space=pl.ANY), VMEM, VMEM, VMEM],
        scratch_shapes=[pltpu.SemaphoreType.DMA((3,)), pltpu.SemaphoreType.DMA((groups, chips))],
        name="fan",
        compiler_params=pltpu.CompilerParams(vmem_limit_bytes=LIMIT),
    )(*bound)
    arrived = exchange(outgoing.reshape(devices, HALF, HD)).reshape(devices * HALF, HD)
    other = lax.ppermute(kv, "blk", [(i, i ^ 1) for i in range(members)])
    suffix = call(
        suffix_kernel,
        "suffix",
        [one(H)] * 2,
        (suffix_len, new_kv.reshape(2 * KVH, HD), q, cache),
        [pl.BlockSpec(memory_space=pltpu.SMEM), VMEM, VMEM, VMEM],
        flops=20_000_000_000,
        bytes_accessed=600_000,
        transcendentals=140_000,
    )
    arrived, suffix = lax.optimization_barrier((arrived, suffix))
    partial = call(
        prefix_kernel,
        "prefix",
        half(devices * MESSAGE),
        (arrived, kv, other),
        flops=12 * devices * HALF * span * HD,
        bytes_accessed=1_600_000,
        transcendentals=2 * devices * HALF * span,
    )
    returned = exchange(partial.reshape(devices, MESSAGE // 2, 2, HD)).reshape(-1, HD)
    return call(
        functools.partial(merge_kernel, served),
        "merge",
        jax.ShapeDtypeStruct((1, H, HD), jnp.bfloat16),
        (returned, *suffix),
    )


def solution(mesh):
    in_specs = (
        P(("grp", "blk"), None, None),
        P(None, "grp", "blk", None),
        P(("grp", "blk"), None, None, None, None),
        P(("grp", "blk"), None, None, None),
        P(("grp", "blk")),
    )
    out_specs = P(("grp", "blk"), None, None)
    return jax.shard_map(local, mesh=mesh, in_specs=in_specs, out_specs=out_specs, check_vma=False)
```

```python
import functools
import math

import jax
import jax.numpy as jnp
from jax import lax
from jax.experimental import pallas as pl
from jax.experimental.pallas import tpu as pltpu
from jax.sharding import PartitionSpec as P

H = 64
KVH = 4
HD = 128
SHARE = H // KVH
SCALE2 = HD ** (-0.5) * math.log2(math.e)
VMEM = pl.BlockSpec(memory_space=pltpu.VMEM)
ROWS = 256
EDGE = 256
CORES = 2
HALF = SHARE // CORES
MESSAGE = HALF + 2
LANES = HD // HALF
LIMIT = 24 * 1024 * 1024
NT = (((1,), (1,)), ((), ()))


def dot_nt(a, b):
    return lax.dot_general(a, b, NT, preferred_element_type=jnp.float32)


def dot(a, b):
    return jnp.dot(a, b, preferred_element_type=jnp.float32)


def log2(x):
    return jnp.log(x) * math.log2(math.e)


def pack_stats(x):
    hi = x.astype(jnp.bfloat16).astype(jnp.float32)
    rest = x - hi
    mid = rest.astype(jnp.bfloat16).astype(jnp.float32)
    low = rest - mid
    row = lax.broadcasted_iota(jnp.int32, x.shape, 1)
    lane = lax.broadcasted_iota(jnp.int32, x.shape, 2) - row * LANES
    return jnp.sum(jnp.where(lane == 0, hi, jnp.where(lane == 1, mid, jnp.where(lane == 2, low, 0.0))), axis=1)


def unpack_stats(rows):
    shape = (HALF, HD)
    mine = lax.broadcasted_iota(jnp.int32, shape, 1) // LANES == lax.broadcasted_iota(jnp.int32, shape, 0)
    pieces = [jnp.where(mine, jnp.broadcast_to(row, shape), 0.0) for row in rows]
    return dot(jnp.concatenate(pieces, axis=0).astype(jnp.bfloat16), jnp.ones((HD, HD), jnp.bfloat16))


def prefix_kernel(q_ref, kv_ref, other_ref, out_ref):
    span = kv_ref.shape[1]
    chunks = [
        (other_ref, slice(0, EDGE)),
        (other_ref, slice(EDGE, span)),
        (kv_ref, slice(0, span - EDGE)),
        (kv_ref, slice(span - EDGE, span)),
    ]

    def block(trip):
        rows = q_ref[pl.ds(trip * ROWS, ROWS)]

        def score(ref, positions):
            return dot_nt(rows, ref[0, positions])

        parts = []
        ahead = score(*chunks[0])
        for index, (ref, positions) in enumerate(chunks):
            scores = ahead
            if index + 1 < len(chunks):
                ahead = score(*chunks[index + 1])
            best = jnp.max(scores, axis=1, keepdims=True)
            weight = jnp.exp2((scores - best) * SCALE2).astype(jnp.bfloat16)
            values = ref[1, positions]
            parts.append((best, dot(weight, jnp.concatenate([values, jnp.ones_like(values)], axis=1))))
        best = functools.reduce(jnp.maximum, [part[0] for part in parts])
        both = sum(jnp.exp2((its - best) * SCALE2) * sums for its, sums in parts)
        total = both[:, HD:]
        result = both[:, :HD] / total
        slots = ROWS // HALF
        stats = pack_stats((best * SCALE2 + log2(total)).reshape(slots, HALF, HD))
        empty = jnp.zeros((1, HD), jnp.float32)
        pieces = []
        for slot in range(slots):
            pieces += [result[slot * HALF : (slot + 1) * HALF], stats[slot : slot + 1], empty]
        out_ref[pl.ds(trip * slots * MESSAGE, slots * MESSAGE)] = jnp.concatenate(pieces, axis=0).astype(jnp.bfloat16)

    trips = q_ref.shape[0] // ROWS
    if trips == 1:
        block(0)
    else:

        def body(trip, unused):
            block(trip)
            return unused

        lax.fori_loop(0, trips, body, 0)


def owned(shape, limit):
    at = lax.broadcasted_iota(jnp.int32, shape, 1)
    head = lax.broadcasted_iota(jnp.int32, shape, 0) // SHARE
    return (at % (2 * KVH) == head) & (at < limit * (2 * KVH))


def suffix_kernel(len_ref, new_ref, q_ref, cache_ref, out_ref, lse_ref):
    q = q_ref[...].reshape(H, HD)
    cache = cache_ref[...]
    new = new_ref[...]
    raw = dot_nt(q, cache)
    scores = jnp.where(owned(raw.shape, len_ref[0]), raw, -jnp.inf)
    new_raw = dot_nt(q, new)
    new_scores = jnp.where(owned(new_raw.shape, 1), new_raw, -jnp.inf)
    best = jnp.maximum(jnp.max(scores, axis=1, keepdims=True), jnp.max(new_scores, axis=1, keepdims=True))
    weight = jnp.exp2((scores - best) * SCALE2).astype(jnp.bfloat16).astype(jnp.float32)
    new_weight = jnp.exp2((new_scores - best) * SCALE2).astype(jnp.bfloat16).astype(jnp.float32)
    total = jnp.sum(weight, axis=1, keepdims=True) + jnp.sum(new_weight, axis=1, keepdims=True)
    moved = pltpu.roll(weight, KVH, 1).astype(jnp.bfloat16)
    new_moved = jnp.concatenate([new_weight[:, KVH:], new_weight[:, :KVH]], axis=1).astype(jnp.bfloat16)
    out_ref[...] = (dot(moved, cache) + dot(new_moved, new)) / total
    lse_ref[...] = jnp.broadcast_to(best * SCALE2 + log2(total), lse_ref.shape)


def fan_kernel(q_hbm, kv_hbm, cache_hbm, out_ref, q_ref, kv_ref, cache_ref, sems, fan_sems):
    pairs = [(q_hbm, q_ref), (cache_hbm, cache_ref), (kv_hbm, kv_ref)]
    loads = [pltpu.make_async_copy(source, target, sems.at[i]) for i, (source, target) in enumerate(pairs)]
    loads[0].start()
    for load in loads[1:]:
        load.start(priority=1)
    loads[0].wait()
    copies = [
        pltpu.make_async_copy(q_ref, out_ref.at[group, :, chip], fan_sems.at[group, chip])
        for group in range(out_ref.shape[0])
        for chip in range(out_ref.shape[2])
    ]
    for copy in copies:
        copy.start()
    for copy in copies + loads[1:]:
        copy.wait()


def merge_kernel(served, part_ref, suffix_ref, lse_ref, out_ref):
    part = part_ref[...].astype(jnp.float32)
    starts = range(0, len(served) * MESSAGE, MESSAGE)
    rows = [part[at : at + HALF] for at in starts]
    sums = unpack_stats([part[at + HALF : at + HALF + 1] for at in starts]).reshape(len(served), HALF, HD)
    blocks = []
    for block in range(H // HALF):
        span = slice(block * HALF, (block + 1) * HALF)
        own = [slot for slot, its in enumerate(served) if its == block]
        own_lse = lse_ref[span]
        best = own_lse
        for slot in own:
            best = jnp.maximum(best, sums[slot])
        total = jnp.exp2(own_lse - best)
        numerator = total * suffix_ref[span]
        for slot in own:
            factor = jnp.exp2(sums[slot] - best)
            total = total + factor
            numerator = numerator + factor * rows[slot]
        blocks.append(numerator / total)
    out_ref[0] = jnp.concatenate(blocks, axis=0).astype(jnp.bfloat16)


def call(kernel, name, outs, operands, specs=None, **cost):
    return pl.pallas_call(
        kernel,
        out_shape=outs,
        in_specs=specs or [VMEM] * len(operands),
        out_specs=jax.tree.map(lambda _: VMEM, outs),
        name=name,
        compiler_params=pltpu.CompilerParams(vmem_limit_bytes=LIMIT),
        cost_estimate=pl.CostEstimate(**cost) if cost else None,
    )(*operands)


def local(queries, prefix_kv, suffix_kv, new_kv, suffix_len):
    groups = lax.axis_size("grp")
    members = lax.axis_size("blk")
    per_head = members // KVH
    devices = groups * members
    span = prefix_kv.shape[2]
    cache_rows = suffix_kv.shape[1] * 2 * KVH
    chips = per_head // CORES
    served = [device % members // per_head * CORES + device % CORES for device in range(devices)]

    def one(rows):
        return jax.ShapeDtypeStruct((rows, HD), jnp.float32)

    def half(*shape):
        return jax.ShapeDtypeStruct((*shape, HD), jnp.bfloat16)

    def exchange(array):
        return lax.all_to_all(array, ("grp", "blk"), 0, 0, tiled=True)

    bound = [
        pltpu.with_memory_space_constraint(array, pltpu.HBM)
        for array in (
            queries.reshape(KVH, SHARE, HD),
            prefix_kv.reshape(2, span, HD),
            suffix_kv.reshape(cache_rows, HD),
        )
    ]
    outgoing, q, kv, cache = pl.pallas_call(
        fan_kernel,
        out_shape=[half(groups, KVH, chips, SHARE), half(KVH, SHARE), half(2, span), half(cache_rows)],
        in_specs=[pl.BlockSpec(memory_space=pltpu.HBM)] * 3,
        out_specs=[pl.BlockSpec(memory_space=pl.ANY), VMEM, VMEM, VMEM],
        scratch_shapes=[pltpu.SemaphoreType.DMA((3,)), pltpu.SemaphoreType.DMA((groups, chips))],
        name="fan",
        compiler_params=pltpu.CompilerParams(vmem_limit_bytes=LIMIT),
    )(*bound)
    arrived = exchange(outgoing.reshape(devices, HALF, HD)).reshape(devices * HALF, HD)
    other = lax.ppermute(kv, "blk", [(i, i ^ 1) for i in range(members)])
    suffix = call(
        suffix_kernel,
        "suffix",
        [one(H)] * 2,
        (suffix_len, new_kv.reshape(2 * KVH, HD), q, cache),
        [pl.BlockSpec(memory_space=pltpu.SMEM), VMEM, VMEM, VMEM],
        flops=20_000_000_000,
        bytes_accessed=600_000,
        transcendentals=140_000,
    )
    arrived, suffix = lax.optimization_barrier((arrived, suffix))
    partial = call(
        prefix_kernel,
        "prefix",
        half(devices * MESSAGE),
        (arrived, kv, other),
        flops=12 * devices * HALF * span * HD,
        bytes_accessed=1_600_000,
        transcendentals=2 * devices * HALF * span,
    )
    returned = exchange(partial.reshape(devices, MESSAGE // 2, 2, HD)).reshape(-1, HD)
    return call(
        functools.partial(merge_kernel, served),
        "merge",
        jax.ShapeDtypeStruct((1, H, HD), jnp.bfloat16),
        (returned, *suffix),
    )


def solution(mesh):
    in_specs = (
        P(("grp", "blk"), None, None),
        P(None, "grp", "blk", None),
        P(("grp", "blk"), None, None, None, None),
        P(("grp", "blk"), None, None, None),
        P(("grp", "blk")),
    )
    out_specs = P(("grp", "blk"), None, None)
    return jax.shard_map(local, mesh=mesh, in_specs=in_specs, out_specs=out_specs, check_vma=False)
```

```python
import functools
import math

import jax
import jax.numpy as jnp
from jax import lax
from jax.experimental import pallas as pl
from jax.experimental.pallas import tpu as pltpu
from jax.sharding import PartitionSpec as P

H = 64
KVH = 4
HD = 128
SHARE = H // KVH
SCALE2 = HD ** (-0.5) * math.log2(math.e)
VMEM = pl.BlockSpec(memory_space=pltpu.VMEM)
ROWS = 256
EDGE = 256
CORES = 2
HALF = SHARE // CORES
MESSAGE = HALF + 2
LANES = HD // HALF
LIMIT = 24 * 1024 * 1024
NT = (((1,), (1,)), ((), ()))


def dot_nt(a, b):
    return lax.dot_general(a, b, NT, preferred_element_type=jnp.float32)


def dot(a, b):
    return jnp.dot(a, b, preferred_element_type=jnp.float32)


def log2(x):
    return jnp.log(x) * math.log2(math.e)


def pack_stats(x):
    hi = x.astype(jnp.bfloat16).astype(jnp.float32)
    rest = x - hi
    mid = rest.astype(jnp.bfloat16).astype(jnp.float32)
    low = rest - mid
    row = lax.broadcasted_iota(jnp.int32, x.shape, 1)
    lane = lax.broadcasted_iota(jnp.int32, x.shape, 2) - row * LANES
    return jnp.sum(jnp.where(lane == 0, hi, jnp.where(lane == 1, mid, jnp.where(lane == 2, low, 0.0))), axis=1)


def unpack_stats(rows):
    shape = (HALF, HD)
    mine = lax.broadcasted_iota(jnp.int32, shape, 1) // LANES == lax.broadcasted_iota(jnp.int32, shape, 0)
    pieces = [jnp.where(mine, jnp.broadcast_to(row, shape), 0.0) for row in rows]
    return dot(jnp.concatenate(pieces, axis=0).astype(jnp.bfloat16), jnp.ones((HD, HD), jnp.bfloat16))


def prefix_kernel(q_ref, kv_ref, other_ref, out_ref):
    span = kv_ref.shape[1]
    chunks = [
        (other_ref, slice(0, EDGE)),
        (other_ref, slice(EDGE, span)),
        (kv_ref, slice(0, span - EDGE)),
        (kv_ref, slice(span - EDGE, span)),
    ]

    def block(trip):
        rows = q_ref[pl.ds(trip * ROWS, ROWS)]

        def score(ref, positions):
            return dot_nt(rows, ref[0, positions])

        parts = []
        ahead = score(*chunks[0])
        for index, (ref, positions) in enumerate(chunks):
            scores = ahead
            if index + 1 < len(chunks):
                ahead = score(*chunks[index + 1])
            best = jnp.max(scores, axis=1, keepdims=True)
            weight = jnp.exp2((scores - best) * SCALE2).astype(jnp.bfloat16)
            values = ref[1, positions]
            parts.append((best, dot(weight, jnp.concatenate([values, jnp.ones_like(values)], axis=1))))
        best = functools.reduce(jnp.maximum, [part[0] for part in parts])
        both = sum(jnp.exp2((its - best) * SCALE2) * sums for its, sums in parts)
        total = both[:, HD:]
        result = both[:, :HD] / total
        slots = ROWS // HALF
        stats = pack_stats((best * SCALE2 + log2(total)).reshape(slots, HALF, HD))
        empty = jnp.zeros((1, HD), jnp.float32)
        pieces = []
        for slot in range(slots):
            pieces += [result[slot * HALF : (slot + 1) * HALF], stats[slot : slot + 1], empty]
        out_ref[pl.ds(trip * slots * MESSAGE, slots * MESSAGE)] = jnp.concatenate(pieces, axis=0).astype(jnp.bfloat16)

    trips = q_ref.shape[0] // ROWS
    if trips == 1:
        block(0)
    else:

        def body(trip, unused):
            block(trip)
            return unused

        lax.fori_loop(0, trips, body, 0)


def owned(shape, limit):
    at = lax.broadcasted_iota(jnp.int32, shape, 1)
    head = lax.broadcasted_iota(jnp.int32, shape, 0) // SHARE
    return (at % (2 * KVH) == head) & (at < limit * (2 * KVH))


def suffix_kernel(len_ref, new_ref, q_ref, cache_ref, out_ref, lse_ref):
    q = q_ref[...].reshape(H, HD)
    cache = cache_ref[...]
    new = new_ref[...]
    raw = dot_nt(q, cache)
    scores = jnp.where(owned(raw.shape, len_ref[0]), raw, -jnp.inf)
    new_raw = dot_nt(q, new)
    new_scores = jnp.where(owned(new_raw.shape, 1), new_raw, -jnp.inf)
    best = jnp.maximum(jnp.max(scores, axis=1, keepdims=True), jnp.max(new_scores, axis=1, keepdims=True))
    weight = jnp.exp2((scores - best) * SCALE2).astype(jnp.bfloat16).astype(jnp.float32)
    new_weight = jnp.exp2((new_scores - best) * SCALE2).astype(jnp.bfloat16).astype(jnp.float32)
    total = jnp.sum(weight, axis=1, keepdims=True) + jnp.sum(new_weight, axis=1, keepdims=True)
    moved = pltpu.roll(weight, KVH, 1).astype(jnp.bfloat16)
    new_moved = jnp.concatenate([new_weight[:, KVH:], new_weight[:, :KVH]], axis=1).astype(jnp.bfloat16)
    out_ref[...] = (dot(moved, cache) + dot(new_moved, new)) / total
    lse_ref[...] = jnp.broadcast_to(best * SCALE2 + log2(total), lse_ref.shape)


def fan_kernel(q_hbm, kv_hbm, cache_hbm, out_ref, q_ref, kv_ref, cache_ref, sems, fan_sems):
    groups, heads, chips = out_ref.shape[:3]
    pairs = [(q_hbm.at[head], q_ref.at[head]) for head in range(heads)] + [(cache_hbm, cache_ref), (kv_hbm, kv_ref)]
    loads = [pltpu.make_async_copy(source, target, sems.at[i]) for i, (source, target) in enumerate(pairs)]
    for load in loads:
        load.start()
    copies = []
    for head in range(heads):
        loads[head].wait()
        for group in range(groups):
            for chip in range(chips):
                sem = fan_sems.at[group, head, chip]
                copies.append(pltpu.make_async_copy(q_ref.at[head], out_ref.at[group, head, chip], sem))
                copies[-1].start()
    for copy in copies + loads[heads:]:
        copy.wait()


def merge_kernel(served, part_ref, suffix_ref, lse_ref, out_ref):
    part = part_ref[...].astype(jnp.float32)
    starts = range(0, len(served) * MESSAGE, MESSAGE)
    rows = [part[at : at + HALF] for at in starts]
    sums = unpack_stats([part[at + HALF : at + HALF + 1] for at in starts]).reshape(len(served), HALF, HD)
    blocks = []
    for block in range(H // HALF):
        span = slice(block * HALF, (block + 1) * HALF)
        own = [slot for slot, its in enumerate(served) if its == block]
        own_lse = lse_ref[span]
        best = own_lse
        for slot in own:
            best = jnp.maximum(best, sums[slot])
        total = jnp.exp2(own_lse - best)
        numerator = total * suffix_ref[span]
        for slot in own:
            factor = jnp.exp2(sums[slot] - best)
            total = total + factor
            numerator = numerator + factor * rows[slot]
        blocks.append(numerator / total)
    out_ref[0] = jnp.concatenate(blocks, axis=0).astype(jnp.bfloat16)


def call(kernel, name, outs, operands, specs=None, **cost):
    return pl.pallas_call(
        kernel,
        out_shape=outs,
        in_specs=specs or [VMEM] * len(operands),
        out_specs=jax.tree.map(lambda _: VMEM, outs),
        name=name,
        compiler_params=pltpu.CompilerParams(vmem_limit_bytes=LIMIT),
        cost_estimate=pl.CostEstimate(**cost) if cost else None,
    )(*operands)


def local(queries, prefix_kv, suffix_kv, new_kv, suffix_len):
    groups = lax.axis_size("grp")
    members = lax.axis_size("blk")
    per_head = members // KVH
    devices = groups * members
    span = prefix_kv.shape[2]
    cache_rows = suffix_kv.shape[1] * 2 * KVH
    chips = per_head // CORES
    served = [device % members // per_head * CORES + device % CORES for device in range(devices)]

    def one(rows):
        return jax.ShapeDtypeStruct((rows, HD), jnp.float32)

    def half(*shape):
        return jax.ShapeDtypeStruct((*shape, HD), jnp.bfloat16)

    def exchange(array):
        return lax.all_to_all(array, ("grp", "blk"), 0, 0, tiled=True)

    bound = [
        pltpu.with_memory_space_constraint(array, pltpu.HBM)
        for array in (
            queries.reshape(KVH, SHARE, HD),
            prefix_kv.reshape(2, span, HD),
            suffix_kv.reshape(cache_rows, HD),
        )
    ]
    outgoing, q, kv, cache = pl.pallas_call(
        fan_kernel,
        out_shape=[half(groups, KVH, chips, SHARE), half(KVH, SHARE), half(2, span), half(cache_rows)],
        in_specs=[pl.BlockSpec(memory_space=pltpu.HBM)] * 3,
        out_specs=[pl.BlockSpec(memory_space=pl.ANY), VMEM, VMEM, VMEM],
        scratch_shapes=[pltpu.SemaphoreType.DMA((KVH + 2,)), pltpu.SemaphoreType.DMA((groups, KVH, chips))],
        name="fan",
        compiler_params=pltpu.CompilerParams(vmem_limit_bytes=LIMIT),
    )(*bound)
    arrived = exchange(outgoing.reshape(devices, HALF, HD)).reshape(devices * HALF, HD)
    other = lax.ppermute(kv, "blk", [(i, i ^ 1) for i in range(members)])
    suffix = call(
        suffix_kernel,
        "suffix",
        [one(H)] * 2,
        (suffix_len, new_kv.reshape(2 * KVH, HD), q, cache),
        [pl.BlockSpec(memory_space=pltpu.SMEM), VMEM, VMEM, VMEM],
        flops=20_000_000_000,
        bytes_accessed=600_000,
        transcendentals=140_000,
    )
    arrived, suffix = lax.optimization_barrier((arrived, suffix))
    partial = call(
        prefix_kernel,
        "prefix",
        half(devices * MESSAGE),
        (arrived, kv, other),
        flops=12 * devices * HALF * span * HD,
        bytes_accessed=1_600_000,
        transcendentals=2 * devices * HALF * span,
    )
    returned = exchange(partial.reshape(devices, MESSAGE // 2, 2, HD)).reshape(-1, HD)
    return call(
        functools.partial(merge_kernel, served),
        "merge",
        jax.ShapeDtypeStruct((1, H, HD), jnp.bfloat16),
        (returned, *suffix),
    )


def solution(mesh):
    in_specs = (
        P(("grp", "blk"), None, None),
        P(None, "grp", "blk", None),
        P(("grp", "blk"), None, None, None, None),
        P(("grp", "blk"), None, None, None),
        P(("grp", "blk")),
    )
    out_specs = P(("grp", "blk"), None, None)
    return jax.shard_map(local, mesh=mesh, in_specs=in_specs, out_specs=out_specs, check_vma=False)
```

```python
import functools
import math

import jax
import jax.numpy as jnp
from jax import lax
from jax.experimental import pallas as pl
from jax.experimental.pallas import tpu as pltpu
from jax.sharding import PartitionSpec as P

H = 64
KVH = 4
HD = 128
SHARE = H // KVH
SCALE2 = HD ** (-0.5) * math.log2(math.e)
VMEM = pl.BlockSpec(memory_space=pltpu.VMEM)
ROWS = 256
EDGE = 256
CORES = 2
HALF = SHARE // CORES
MESSAGE = HALF + 2
LANES = HD // HALF
LIMIT = 24 * 1024 * 1024
NT = (((1,), (1,)), ((), ()))


def dot_nt(a, b):
    return lax.dot_general(a, b, NT, preferred_element_type=jnp.float32)


def dot(a, b):
    return jnp.dot(a, b, preferred_element_type=jnp.float32)


def log2(x):
    return jnp.log(x) * math.log2(math.e)


def pack_stats(x):
    hi = x.astype(jnp.bfloat16).astype(jnp.float32)
    rest = x - hi
    mid = rest.astype(jnp.bfloat16).astype(jnp.float32)
    low = rest - mid
    row = lax.broadcasted_iota(jnp.int32, x.shape, 1)
    lane = lax.broadcasted_iota(jnp.int32, x.shape, 2) - row * LANES
    return jnp.sum(jnp.where(lane == 0, hi, jnp.where(lane == 1, mid, jnp.where(lane == 2, low, 0.0))), axis=1)


def unpack_stats(rows):
    shape = (HALF, HD)
    mine = lax.broadcasted_iota(jnp.int32, shape, 1) // LANES == lax.broadcasted_iota(jnp.int32, shape, 0)
    pieces = [jnp.where(mine, jnp.broadcast_to(row, shape), 0.0) for row in rows]
    return dot(jnp.concatenate(pieces, axis=0).astype(jnp.bfloat16), jnp.ones((HD, HD), jnp.bfloat16))


def prefix_kernel(q_ref, kv_ref, other_ref, out_ref):
    span = kv_ref.shape[1]
    chunks = [
        (other_ref, slice(0, EDGE)),
        (other_ref, slice(EDGE, span)),
        (kv_ref, slice(0, span - EDGE)),
        (kv_ref, slice(span - EDGE, span)),
    ]

    def block(trip):
        rows = q_ref[pl.ds(trip * ROWS, ROWS)]

        def score(ref, positions):
            return dot_nt(rows, ref[0, positions])

        parts = []
        ahead = score(*chunks[0])
        for index, (ref, positions) in enumerate(chunks):
            scores = ahead
            if index + 1 < len(chunks):
                ahead = score(*chunks[index + 1])
            best = jnp.max(scores, axis=1, keepdims=True)
            weight = jnp.exp2((scores - best) * SCALE2).astype(jnp.bfloat16)
            values = ref[1, positions]
            parts.append((best, dot(weight, jnp.concatenate([values, jnp.ones_like(values)], axis=1))))
        best = functools.reduce(jnp.maximum, [part[0] for part in parts])
        both = sum(jnp.exp2((its - best) * SCALE2) * sums for its, sums in parts)
        total = both[:, HD:]
        result = both[:, :HD] / total
        slots = ROWS // HALF
        stats = pack_stats((best * SCALE2 + log2(total)).reshape(slots, HALF, HD))
        empty = jnp.zeros((1, HD), jnp.float32)
        pieces = []
        for slot in range(slots):
            pieces += [result[slot * HALF : (slot + 1) * HALF], stats[slot : slot + 1], empty]
        out_ref[pl.ds(trip * slots * MESSAGE, slots * MESSAGE)] = jnp.concatenate(pieces, axis=0).astype(jnp.bfloat16)

    trips = q_ref.shape[0] // ROWS
    if trips == 1:
        block(0)
    else:

        def body(trip, unused):
            block(trip)
            return unused

        lax.fori_loop(0, trips, body, 0)


def owned(shape, limit):
    at = lax.broadcasted_iota(jnp.int32, shape, 1)
    head = lax.broadcasted_iota(jnp.int32, shape, 0) // SHARE
    return (at % (2 * KVH) == head) & (at < limit * (2 * KVH))


def suffix_kernel(len_ref, new_ref, q_ref, cache_ref, out_ref, lse_ref):
    q = q_ref[...].reshape(H, HD)
    cache = cache_ref[...]
    new = new_ref[...]
    raw = dot_nt(q, cache)
    scores = jnp.where(owned(raw.shape, len_ref[0]), raw, -jnp.inf)
    new_raw = dot_nt(q, new)
    new_scores = jnp.where(owned(new_raw.shape, 1), new_raw, -jnp.inf)
    best = jnp.maximum(jnp.max(scores, axis=1, keepdims=True), jnp.max(new_scores, axis=1, keepdims=True))
    weight = jnp.exp2((scores - best) * SCALE2).astype(jnp.bfloat16).astype(jnp.float32)
    new_weight = jnp.exp2((new_scores - best) * SCALE2).astype(jnp.bfloat16).astype(jnp.float32)
    total = jnp.sum(weight, axis=1, keepdims=True) + jnp.sum(new_weight, axis=1, keepdims=True)
    moved = pltpu.roll(weight, KVH, 1).astype(jnp.bfloat16)
    new_moved = jnp.concatenate([new_weight[:, KVH:], new_weight[:, :KVH]], axis=1).astype(jnp.bfloat16)
    out_ref[...] = (dot(moved, cache) + dot(new_moved, new)) / total
    lse_ref[...] = jnp.broadcast_to(best * SCALE2 + log2(total), lse_ref.shape)


def fan_kernel(q_hbm, kv_hbm, cache_hbm, out_ref, q_ref, kv_ref, cache_ref, fan_ref, sems):
    pairs = [(q_hbm, q_ref), (cache_hbm, cache_ref), (kv_hbm, kv_ref)]
    loads = [pltpu.make_async_copy(source, target, sems.at[i]) for i, (source, target) in enumerate(pairs)]
    for load in loads:
        load.start()
    loads[0].wait()
    for group in range(out_ref.shape[0]):
        for chip in range(out_ref.shape[2]):
            fan_ref[group, :, chip] = q_ref[...]
    copy = pltpu.make_async_copy(fan_ref, out_ref, sems.at[len(loads)])
    copy.start()
    for load in loads[1:]:
        load.wait()
    copy.wait()


def merge_kernel(served, part_ref, suffix_ref, lse_ref, out_ref):
    part = part_ref[...].astype(jnp.float32)
    starts = range(0, len(served) * MESSAGE, MESSAGE)
    rows = [part[at : at + HALF] for at in starts]
    sums = unpack_stats([part[at + HALF : at + HALF + 1] for at in starts]).reshape(len(served), HALF, HD)
    blocks = []
    for block in range(H // HALF):
        span = slice(block * HALF, (block + 1) * HALF)
        own = [slot for slot, its in enumerate(served) if its == block]
        own_lse = lse_ref[span]
        best = own_lse
        for slot in own:
            best = jnp.maximum(best, sums[slot])
        total = jnp.exp2(own_lse - best)
        numerator = total * suffix_ref[span]
        for slot in own:
            factor = jnp.exp2(sums[slot] - best)
            total = total + factor
            numerator = numerator + factor * rows[slot]
        blocks.append(numerator / total)
    out_ref[0] = jnp.concatenate(blocks, axis=0).astype(jnp.bfloat16)


def call(kernel, name, outs, operands, specs=None, **cost):
    return pl.pallas_call(
        kernel,
        out_shape=outs,
        in_specs=specs or [VMEM] * len(operands),
        out_specs=jax.tree.map(lambda _: VMEM, outs),
        name=name,
        compiler_params=pltpu.CompilerParams(vmem_limit_bytes=LIMIT),
        cost_estimate=pl.CostEstimate(**cost) if cost else None,
    )(*operands)


def local(queries, prefix_kv, suffix_kv, new_kv, suffix_len):
    groups = lax.axis_size("grp")
    members = lax.axis_size("blk")
    per_head = members // KVH
    devices = groups * members
    span = prefix_kv.shape[2]
    cache_rows = suffix_kv.shape[1] * 2 * KVH
    chips = per_head // CORES
    served = [device % members // per_head * CORES + device % CORES for device in range(devices)]

    def one(rows):
        return jax.ShapeDtypeStruct((rows, HD), jnp.float32)

    def half(*shape):
        return jax.ShapeDtypeStruct((*shape, HD), jnp.bfloat16)

    def exchange(array):
        return lax.all_to_all(array, ("grp", "blk"), 0, 0, tiled=True)

    bound = [
        pltpu.with_memory_space_constraint(array, pltpu.HBM)
        for array in (
            queries.reshape(KVH, SHARE, HD),
            prefix_kv.reshape(2, span, HD),
            suffix_kv.reshape(cache_rows, HD),
        )
    ]
    outgoing, q, kv, cache = pl.pallas_call(
        fan_kernel,
        out_shape=[half(groups, KVH, chips, SHARE), half(KVH, SHARE), half(2, span), half(cache_rows)],
        in_specs=[pl.BlockSpec(memory_space=pltpu.HBM)] * 3,
        out_specs=[pl.BlockSpec(memory_space=pl.ANY), VMEM, VMEM, VMEM],
        scratch_shapes=[pltpu.VMEM((groups, KVH, chips, SHARE, HD), jnp.bfloat16), pltpu.SemaphoreType.DMA((4,))],
        name="fan",
        compiler_params=pltpu.CompilerParams(vmem_limit_bytes=LIMIT),
    )(*bound)
    arrived = exchange(outgoing.reshape(devices, HALF, HD)).reshape(devices * HALF, HD)
    other = lax.ppermute(kv, "blk", [(i, i ^ 1) for i in range(members)])
    suffix = call(
        suffix_kernel,
        "suffix",
        [one(H)] * 2,
        (suffix_len, new_kv.reshape(2 * KVH, HD), q, cache),
        [pl.BlockSpec(memory_space=pltpu.SMEM), VMEM, VMEM, VMEM],
        flops=20_000_000_000,
        bytes_accessed=600_000,
        transcendentals=140_000,
    )
    arrived, suffix = lax.optimization_barrier((arrived, suffix))
    partial = call(
        prefix_kernel,
        "prefix",
        half(devices * MESSAGE),
        (arrived, kv, other),
        flops=12 * devices * HALF * span * HD,
        bytes_accessed=1_600_000,
        transcendentals=2 * devices * HALF * span,
    )
    returned = exchange(partial.reshape(devices, MESSAGE // 2, 2, HD)).reshape(-1, HD)
    return call(
        functools.partial(merge_kernel, served),
        "merge",
        jax.ShapeDtypeStruct((1, H, HD), jnp.bfloat16),
        (returned, *suffix),
    )


def solution(mesh):
    in_specs = (
        P(("grp", "blk"), None, None),
        P(None, "grp", "blk", None),
        P(("grp", "blk"), None, None, None, None),
        P(("grp", "blk"), None, None, None),
        P(("grp", "blk")),
    )
    out_specs = P(("grp", "blk"), None, None)
    return jax.shard_map(local, mesh=mesh, in_specs=in_specs, out_specs=out_specs, check_vma=False)
```

```python
import functools
import math

import jax
import jax.numpy as jnp
from jax import lax
from jax.experimental import pallas as pl
from jax.experimental.pallas import tpu as pltpu
from jax.sharding import PartitionSpec as P

H = 64
KVH = 4
HD = 128
SHARE = H // KVH
SCALE2 = HD ** (-0.5) * math.log2(math.e)
VMEM = pl.BlockSpec(memory_space=pltpu.VMEM)
ROWS = 256
EDGE = 256
CORES = 2
HALF = SHARE // CORES
MESSAGE = HALF + 2
LANES = HD // HALF
PIECES = 3
LIMIT = 24 * 1024 * 1024
NT = (((1,), (1,)), ((), ()))


def dot_nt(a, b):
    return lax.dot_general(a, b, NT, preferred_element_type=jnp.float32)


def dot(a, b):
    return jnp.dot(a, b, preferred_element_type=jnp.float32)


def log2(x):
    return jnp.log(x) * math.log2(math.e)


def split3(x):
    hi = x.astype(jnp.bfloat16).astype(jnp.float32)
    rest = x - hi
    mid = rest.astype(jnp.bfloat16).astype(jnp.float32)
    return hi, mid, rest - mid


def pack_stats(best, total):
    row = lax.broadcasted_iota(jnp.int32, best.shape, 1)
    lane = lax.broadcasted_iota(jnp.int32, best.shape, 2) - row * LANES
    packed = jnp.zeros_like(best)
    for at, piece in enumerate((*split3(best), *split3(total))):
        packed = jnp.where(lane == at, piece, packed)
    return jnp.sum(packed, axis=1)


def unpack_stats(rows):
    shape = (HALF, HD)
    mine = lax.broadcasted_iota(jnp.int32, shape, 1) // LANES == lax.broadcasted_iota(jnp.int32, shape, 0)
    pieces = [jnp.where(mine, jnp.broadcast_to(row, shape), 0.0) for row in rows]
    shape = (HD, 2 * HD)
    which = lax.broadcasted_iota(jnp.int32, shape, 0) % LANES // PIECES
    select = jnp.where(which == lax.broadcasted_iota(jnp.int32, shape, 1) // HD, 1.0, 0.0)
    return dot(jnp.concatenate(pieces, axis=0).astype(jnp.bfloat16), select.astype(jnp.bfloat16))


def prefix_kernel(q_ref, kv_ref, other_ref, out_ref):
    span = kv_ref.shape[1]
    chunks = [
        (other_ref, slice(0, EDGE)),
        (other_ref, slice(EDGE, span)),
        (kv_ref, slice(0, span - EDGE)),
        (kv_ref, slice(span - EDGE, span)),
    ]

    def block(trip):
        rows = q_ref[pl.ds(trip * ROWS, ROWS)]

        def score(ref, positions):
            return dot_nt(rows, ref[0, positions])

        parts = []
        ahead = score(*chunks[0])
        for index, (ref, positions) in enumerate(chunks):
            scores = ahead
            if index + 1 < len(chunks):
                ahead = score(*chunks[index + 1])
            best = jnp.max(scores, axis=1, keepdims=True)
            weight = jnp.exp2((scores - best) * SCALE2).astype(jnp.bfloat16)
            values = ref[1, positions]
            parts.append((best, dot(weight, jnp.concatenate([values, jnp.ones_like(values)], axis=1))))
        best = functools.reduce(jnp.maximum, [part[0] for part in parts])
        both = sum(jnp.exp2((its - best) * SCALE2) * sums for its, sums in parts)
        numerator = both[:, :HD]
        slots = ROWS // HALF
        shape = (slots, HALF, HD)
        best = jnp.broadcast_to(best * SCALE2, numerator.shape)
        stats = pack_stats(best.reshape(shape), both[:, HD:].reshape(shape))
        empty = jnp.zeros((1, HD), jnp.float32)
        pieces = []
        for slot in range(slots):
            pieces += [numerator[slot * HALF : (slot + 1) * HALF], stats[slot : slot + 1], empty]
        out_ref[pl.ds(trip * slots * MESSAGE, slots * MESSAGE)] = jnp.concatenate(pieces, axis=0).astype(jnp.bfloat16)

    trips = q_ref.shape[0] // ROWS
    if trips == 1:
        block(0)
    else:

        def body(trip, unused):
            block(trip)
            return unused

        lax.fori_loop(0, trips, body, 0)


def owned(shape, limit):
    at = lax.broadcasted_iota(jnp.int32, shape, 1)
    head = lax.broadcasted_iota(jnp.int32, shape, 0) // SHARE
    return (at % (2 * KVH) == head) & (at < limit * (2 * KVH))


def suffix_kernel(len_ref, new_ref, q_ref, cache_ref, out_ref, lse_ref):
    q = q_ref[...].reshape(H, HD)
    cache = cache_ref[...]
    new = new_ref[...]
    raw = dot_nt(q, cache)
    scores = jnp.where(owned(raw.shape, len_ref[0]), raw, -jnp.inf)
    new_raw = dot_nt(q, new)
    new_scores = jnp.where(owned(new_raw.shape, 1), new_raw, -jnp.inf)
    best = jnp.maximum(jnp.max(scores, axis=1, keepdims=True), jnp.max(new_scores, axis=1, keepdims=True))
    weight = jnp.exp2((scores - best) * SCALE2).astype(jnp.bfloat16).astype(jnp.float32)
    new_weight = jnp.exp2((new_scores - best) * SCALE2).astype(jnp.bfloat16).astype(jnp.float32)
    total = jnp.sum(weight, axis=1, keepdims=True) + jnp.sum(new_weight, axis=1, keepdims=True)
    moved = pltpu.roll(weight, KVH, 1).astype(jnp.bfloat16)
    new_moved = jnp.concatenate([new_weight[:, KVH:], new_weight[:, :KVH]], axis=1).astype(jnp.bfloat16)
    out_ref[...] = (dot(moved, cache) + dot(new_moved, new)) / total
    lse_ref[...] = jnp.broadcast_to(best * SCALE2 + log2(total), lse_ref.shape)


def fan_kernel(q_hbm, kv_hbm, cache_hbm, out_ref, q_ref, kv_ref, cache_ref, fan_ref, sems):
    pairs = [(q_hbm, q_ref), (cache_hbm, cache_ref), (kv_hbm, kv_ref)]
    loads = [pltpu.make_async_copy(source, target, sems.at[i]) for i, (source, target) in enumerate(pairs)]
    for load in loads:
        load.start()
    loads[0].wait()
    for group in range(out_ref.shape[0]):
        for chip in range(out_ref.shape[2]):
            fan_ref[group, :, chip] = q_ref[...]
    copy = pltpu.make_async_copy(fan_ref, out_ref, sems.at[len(loads)])
    copy.start()
    for load in loads[1:]:
        load.wait()
    copy.wait()


def merge_kernel(served, part_ref, suffix_ref, lse_ref, out_ref):
    part = part_ref[...].astype(jnp.float32)
    starts = range(0, len(served) * MESSAGE, MESSAGE)
    rows = [part[at : at + HALF] for at in starts]
    sums = unpack_stats([part[at + HALF : at + HALF + 1] for at in starts]).reshape(len(served), HALF, 2 * HD)
    blocks = []
    for block in range(H // HALF):
        span = slice(block * HALF, (block + 1) * HALF)
        own = [slot for slot, its in enumerate(served) if its == block]
        own_lse = lse_ref[span]
        best = own_lse
        for slot in own:
            best = jnp.maximum(best, sums[slot, :, :HD])
        total = jnp.exp2(own_lse - best)
        numerator = total * suffix_ref[span]
        for slot in own:
            factor = jnp.exp2(sums[slot, :, :HD] - best)
            total = total + factor * sums[slot, :, HD:]
            numerator = numerator + factor * rows[slot]
        blocks.append(numerator / total)
    out_ref[0] = jnp.concatenate(blocks, axis=0).astype(jnp.bfloat16)


def call(kernel, name, outs, operands, specs=None, **cost):
    return pl.pallas_call(
        kernel,
        out_shape=outs,
        in_specs=specs or [VMEM] * len(operands),
        out_specs=jax.tree.map(lambda _: VMEM, outs),
        name=name,
        compiler_params=pltpu.CompilerParams(vmem_limit_bytes=LIMIT),
        cost_estimate=pl.CostEstimate(**cost) if cost else None,
    )(*operands)


def local(queries, prefix_kv, suffix_kv, new_kv, suffix_len):
    groups = lax.axis_size("grp")
    members = lax.axis_size("blk")
    per_head = members // KVH
    devices = groups * members
    span = prefix_kv.shape[2]
    cache_rows = suffix_kv.shape[1] * 2 * KVH
    chips = per_head // CORES
    served = [device % members // per_head * CORES + device % CORES for device in range(devices)]

    def one(rows):
        return jax.ShapeDtypeStruct((rows, HD), jnp.float32)

    def half(*shape):
        return jax.ShapeDtypeStruct((*shape, HD), jnp.bfloat16)

    def exchange(array):
        return lax.all_to_all(array, ("grp", "blk"), 0, 0, tiled=True)

    bound = [
        pltpu.with_memory_space_constraint(array, pltpu.HBM)
        for array in (
            queries.reshape(KVH, SHARE, HD),
            prefix_kv.reshape(2, span, HD),
            suffix_kv.reshape(cache_rows, HD),
        )
    ]
    outgoing, q, kv, cache = pl.pallas_call(
        fan_kernel,
        out_shape=[half(groups, KVH, chips, SHARE), half(KVH, SHARE), half(2, span), half(cache_rows)],
        in_specs=[pl.BlockSpec(memory_space=pltpu.HBM)] * 3,
        out_specs=[pl.BlockSpec(memory_space=pl.ANY), VMEM, VMEM, VMEM],
        scratch_shapes=[pltpu.VMEM((groups, KVH, chips, SHARE, HD), jnp.bfloat16), pltpu.SemaphoreType.DMA((4,))],
        name="fan",
        compiler_params=pltpu.CompilerParams(vmem_limit_bytes=LIMIT),
    )(*bound)
    arrived = exchange(outgoing.reshape(devices, HALF, HD)).reshape(devices * HALF, HD)
    other = lax.ppermute(kv, "blk", [(i, i ^ 1) for i in range(members)])
    suffix = call(
        suffix_kernel,
        "suffix",
        [one(H)] * 2,
        (suffix_len, new_kv.reshape(2 * KVH, HD), q, cache),
        [pl.BlockSpec(memory_space=pltpu.SMEM), VMEM, VMEM, VMEM],
        flops=20_000_000_000,
        bytes_accessed=600_000,
        transcendentals=140_000,
    )
    arrived, suffix = lax.optimization_barrier((arrived, suffix))
    partial = call(
        prefix_kernel,
        "prefix",
        half(devices * MESSAGE),
        (arrived, kv, other),
        flops=12 * devices * HALF * span * HD,
        bytes_accessed=1_600_000,
        transcendentals=2 * devices * HALF * span,
    )
    returned = exchange(partial.reshape(devices, MESSAGE // 2, 2, HD)).reshape(-1, HD)
    return call(
        functools.partial(merge_kernel, served),
        "merge",
        jax.ShapeDtypeStruct((1, H, HD), jnp.bfloat16),
        (returned, *suffix),
    )


def solution(mesh):
    in_specs = (
        P(("grp", "blk"), None, None),
        P(None, "grp", "blk", None),
        P(("grp", "blk"), None, None, None, None),
        P(("grp", "blk"), None, None, None),
        P(("grp", "blk")),
    )
    out_specs = P(("grp", "blk"), None, None)
    return jax.shard_map(local, mesh=mesh, in_specs=in_specs, out_specs=out_specs, check_vma=False)
```
